32 devices in a mesh: row: 4 (over y, x), col: 8 (over z, core).
Axes of the slice: x: 2, y: 2, z: 4, core: 2. Of those that a mesh axis runs over, the one named last changes fastest.
Arguments:
- initial_kelvin_state: float32 [8, 512, 1024], P(None, 'row', 'col'), may hold values from -6 to 6
- substance_region: int32 [8, 512, 1024], P(None, 'row', 'col'), may hold values from 0 to 2, as said below
- source_energy: float32 [8, 512, 1024], P(None, 'row', 'col'), may hold values from 0.2 to 5
- substance_transfer_magnitude: float32 [3], replicated, may hold values from 0.02 to 6, as said below
- substance_softening_rate: float32 [3], replicated, may hold values from 0.05 to 0.25
Outputs:
- new_temperature: float32 [8, 512, 1024], P(None, 'row', 'col')
The draws below stay inside these ranges and needn't reach their ends.
Inputs may be any that keep to these rules, and one draw needn't show every extreme that they name: `substance_region`: 0 die, 1 thermal interface material, 2 spreader. `substance_transfer_magnitude`: positive conductivity scales of die, interface material and spreader, in that order.
All inputs are finite; a program needn't handle non-finite values.
Results may differ from the reference program's by a relative error of at most 0.0027.
Values sent between devices are 32-bit elements; how exact they have to be, the bound alone decides.
A program may use at most 192 MiB of HBM per device.

```python
import math
import jax
import jax.numpy as jnp
from jax import lax

NODES_THROUGH = 8
NODES_ACROSS = 1024
NODES_DOWNWARD = 512


def draw_substance_region(key, part):
    rolled = jax.random.randint(key, (NODES_THROUGH, NODES_DOWNWARD, NODES_ACROSS), 0, 10)
    layer = lax.broadcasted_iota(jnp.int32, (NODES_THROUGH, NODES_DOWNWARD, NODES_ACROSS), 0)
    spreader_cells = jnp.where(rolled < 2, 0, 2)
    interface_cells = jnp.where(rolled < 1, 0, 1)
    die_cells = jnp.where(rolled < 2, 2, 0)
    middle = NODES_THROUGH // 2
    return jnp.where(layer < middle, spreader_cells, jnp.where(layer == middle, interface_cells, die_cells)).astype(jnp.int32)


def draw_substance_transfer_magnitude(key, part):
    lowest = jnp.array([0.8, 0.02, 2.0], jnp.float32)
    highest = jnp.array([2.5, 0.08, 6.0], jnp.float32)
    fraction = jax.random.uniform(key, (3,), jnp.float32)
    return lowest * jnp.exp(fraction * jnp.log(highest / lowest))


def levels(own_key, shape, cuts, smallest, largest):
    gain = 1.0
    for dim, shards_of in cuts:
        steps = jax.random.uniform(jax.random.fold_in(jax.random.fold_in(own_key, 6), dim), (shards_of,), jnp.float32, smallest / len(cuts), largest / len(cuts))
        gain = gain * jnp.repeat(jnp.exp(steps), shape[dim] // shards_of).reshape((-1,) + (1,) * (len(shape) - 1 - dim))
    return gain


def gaussian(own_key, dims, scale, bound, shards=(), kind=jnp.bfloat16):
    entries = jax.random.normal(own_key, dims, jnp.float32) * scale
    if len(shards) > 0:
        entries = levels(own_key, dims, shards, -0.22, 0.18) * entries
    return jnp.clip(entries, min=-bound, max=bound).astype(kind)


def setup_inputs(seed: int = 0) -> dict:
    keys = jax.random.split(jax.random.key(seed), 6)
    initial_kelvin_state = gaussian(keys[0], (NODES_THROUGH, NODES_DOWNWARD, NODES_ACROSS), 1.0, 6.0, ((1, 4), (2, 8)), jnp.float32)
    substance_region = draw_substance_region(jax.random.fold_in(keys[5], 71), 0)
    source_energy = jnp.clip(jnp.exp(math.log(5.0) - 3.218876 * jax.random.uniform(keys[2], (NODES_THROUGH, NODES_DOWNWARD, NODES_ACROSS), jnp.float32) ** levels(keys[2], (NODES_THROUGH, NODES_DOWNWARD, NODES_ACROSS), ((1, 4), (2, 8)), -0.2, 0.2)), 0.2, 5.0)
    substance_transfer_magnitude = draw_substance_transfer_magnitude(jax.random.fold_in(keys[5], 71), 0)
    substance_softening_rate = jnp.clip(jax.random.uniform(keys[4], (3,), jnp.float32, 0.05, 0.25), 0.05, 0.25)
    return dict(initial_kelvin_state=initial_kelvin_state, substance_region=substance_region, source_energy=source_energy, substance_transfer_magnitude=substance_transfer_magnitude, substance_softening_rate=substance_softening_rate)


inplane_ratio = 1000.0
depth_ratio = 0.08


def transfer_coefficient_array(initial_kelvin_state, substance_region, substance_transfer_magnitude, substance_softening_rate):
    nodal_transfer_coefficient = jnp.where(substance_region == 0, substance_transfer_magnitude[0], jnp.where(substance_region == 1, substance_transfer_magnitude[1], substance_transfer_magnitude[2]))
    nodal_thermal_softening = jnp.where(substance_region == 0, substance_softening_rate[0], jnp.where(substance_region == 1, substance_softening_rate[1], substance_softening_rate[2]))
    return nodal_transfer_coefficient * jnp.exp(-nodal_thermal_softening * initial_kelvin_state)


def face_conductance(center, beside):
    return 2.0 * center * beside / (center + beside)


def forward_diffusion_parts(field_padded, cond_padded):
    field_center = field_padded[:, 1:-1, 1:-1]
    cond_center = cond_padded[:, 1:-1, 1:-1]

    def flux(field_beside, cond_beside):
        return face_conductance(cond_center, cond_beside) * (field_beside - field_center)

    implicit_pass_first_axis = inplane_ratio * (flux(field_padded[:, 1:-1, 2:], cond_padded[:, 1:-1, 2:]) + flux(field_padded[:, 1:-1, :-2], cond_padded[:, 1:-1, :-2]))
    implicit_pass_second_axis = inplane_ratio * (flux(field_padded[:, 2:, 1:-1], cond_padded[:, 2:, 1:-1]) + flux(field_padded[:, :-2, 1:-1], cond_padded[:, :-2, 1:-1]))
    field_layers = jnp.pad(field_center, ((1, 1), (0, 0), (0, 0)))
    cond_layers = jnp.pad(cond_center, ((1, 1), (0, 0), (0, 0)))
    implicit_pass_third_axis = depth_ratio * (flux(field_layers[2:], cond_layers[2:]) + flux(field_layers[:-2], cond_layers[:-2]))
    bottom = (lax.broadcasted_iota(jnp.int32, field_center.shape, 0) == 0).astype(field_center.dtype)
    implicit_pass_third_axis = implicit_pass_third_axis - depth_ratio * bottom * cond_center * field_center
    return implicit_pass_first_axis, implicit_pass_second_axis, implicit_pass_third_axis


def line_system(cond_lines, line_axis, ratio):
    length = cond_lines.shape[line_axis]
    plate_thicknesses = [(0, 0)] * cond_lines.ndim
    plate_thicknesses[line_axis] = (1, 1)
    cond_padded = jnp.pad(cond_lines, plate_thicknesses)
    before = lax.slice_in_dim(cond_padded, 0, length, axis=line_axis)
    after = lax.slice_in_dim(cond_padded, 2, length + 2, axis=line_axis)
    lower_band = -0.5 * ratio * face_conductance(cond_lines, before)
    upper_band = -0.5 * ratio * face_conductance(cond_lines, after)
    main_band = 1.0 - lower_band - upper_band
    return lower_band, main_band, upper_band


def append_slab(values, filler, line_axis):
    slab_shape = list(values.shape)
    slab_shape[line_axis] = 1
    return jnp.concatenate([values, jnp.full(slab_shape, filler, values.dtype)], line_axis)


def prepend_slab(values, filler, line_axis):
    slab_shape = list(values.shape)
    slab_shape[line_axis] = 1
    return jnp.concatenate([jnp.full(slab_shape, filler, values.dtype), values], line_axis)


def reduce_solve(lower_band, main_band, upper_band, right_side, line_axis):
    length = right_side.shape[line_axis]
    if length == 1:
        return right_side / main_band
    if length % 2 == 1:
        lower_band = append_slab(lower_band, 0.0, line_axis)
        main_band = append_slab(main_band, 1.0, line_axis)
        upper_band = append_slab(upper_band, 0.0, line_axis)
        right_side = append_slab(right_side, 0.0, line_axis)
    padded_length = right_side.shape[line_axis]
    half_length = padded_length // 2

    def evens(values):
        return lax.slice_in_dim(values, 0, padded_length, 2, line_axis)

    def odds(values):
        return lax.slice_in_dim(values, 1, padded_length, 2, line_axis)

    def following(values, filler):
        return append_slab(lax.slice_in_dim(evens(values), 1, half_length, axis=line_axis), filler, line_axis)

    left_factor = -odds(lower_band) / evens(main_band)
    right_factor = -odds(upper_band) / following(main_band, 1.0)
    new_lower = left_factor * evens(lower_band)
    new_upper = right_factor * following(upper_band, 0.0)
    new_main = odds(main_band) + left_factor * evens(upper_band) + right_factor * following(lower_band, 0.0)
    new_right = odds(right_side) + left_factor * evens(right_side) + right_factor * following(right_side, 0.0)
    odd_values = reduce_solve(new_lower, new_main, new_upper, new_right, line_axis)
    earlier = prepend_slab(lax.slice_in_dim(odd_values, 0, half_length - 1, axis=line_axis), 0.0, line_axis)
    even_values = (evens(right_side) - evens(lower_band) * earlier - evens(upper_band) * odd_values) / evens(main_band)
    joined_shape = list(right_side.shape)
    joined = jnp.stack([even_values, odd_values], line_axis + 1).reshape(joined_shape)
    return lax.slice_in_dim(joined, 0, length, axis=line_axis)


def reference(initial_kelvin_state, substance_region, source_energy, substance_transfer_magnitude, substance_softening_rate):
    transfer_coefficient_volume = transfer_coefficient_array(initial_kelvin_state, substance_region, substance_transfer_magnitude, substance_softening_rate)
    plate_thicknesses = ((0, 0), (1, 1), (1, 1))
    implicit_pass_first_axis, implicit_pass_second_axis, implicit_pass_third_axis = forward_diffusion_parts(jnp.pad(initial_kelvin_state, plate_thicknesses), jnp.pad(transfer_coefficient_volume, plate_thicknesses))
    first_boundary_face = initial_kelvin_state + 0.5 * implicit_pass_first_axis + implicit_pass_second_axis + implicit_pass_third_axis + source_energy

    def solve_rows(pieces):
        cond_layer, side_layer = pieces
        lower_band, main_band, upper_band = line_system(cond_layer, 1, inplane_ratio)
        return reduce_solve(lower_band, main_band, upper_band, side_layer, 1)

    def solve_columns(pieces):
        cond_layer, side_layer = pieces
        lower_band, main_band, upper_band = line_system(cond_layer, 0, inplane_ratio)
        return reduce_solve(lower_band, main_band, upper_band, side_layer, 0)

    half_step = lax.map(solve_rows, (transfer_coefficient_volume, first_boundary_face))
    second_side = half_step - 0.5 * implicit_pass_second_axis
    return lax.map(solve_columns, (transfer_coefficient_volume, second_side))
```

```python
import functools

import jax
import jax.numpy as jnp
from jax import lax
from jax.experimental import pallas as pl
from jax.experimental.pallas import tpu as pltpu
from jax.sharding import PartitionSpec as P

MESH = pl.DeviceIdType.MESH
inplane_half = 500.0
depth_ratio = 0.08

NZ = 8
L = 128
BLOCK = 16


def inverse(value):
    guess = pl.reciprocal(value, approx=True)
    return guess * (2.0 - value * guess)


def pairs(values):
    split = values.reshape((values.shape[0] // 2, 2) + values.shape[1:])
    return split[:, 0], split[:, 1]


def shifted_up(values, last):
    if values.shape[0] == 1:
        return last
    return jnp.concatenate([values[1:], last], axis=0)


def shifted_down(values, first):
    if values.shape[0] == 1:
        return first
    return jnp.concatenate([first, values[:-1]], axis=0)


def nodes(ref, first, count):
    return ref[pl.ds(first * NZ, count * NZ), :].reshape(count, NZ, L)


def put_nodes(ref, first, values):
    count = values.shape[0]
    ref[pl.ds(first * NZ, count * NZ), :] = values.reshape(count * NZ, L)


def levels():
    count = L
    while count > 1:
        half = count // 2
        yield count, half, L - 2 * count, L - 2 * half
        count = half


def eliminate_coefficients(link_ref, gl_ref, gr_ref, r_ref, w_ref, s_ref):
    pushed_out = jnp.zeros((1, NZ, L), jnp.float32)
    for count, half, node_at, pair_at in levels():
        block = min(half, BLOCK)
        carry = jnp.zeros((1, NZ, L), jnp.float32)
        for first in reversed(range(0, half, block)):
            if count == L:
                wl, wr = pairs(nodes(link_ref, 2 * first, 2 * block))
                inv = inverse(1.0 + wl + wr)
                gl, gr = wl * inv, wr * inv
                push = gl
                surplus = 1.0 + gr + shifted_up(push, carry)
            else:
                wl, wr = pairs(nodes(w_ref, node_at + 2 * first, 2 * block))
                se, so = pairs(nodes(s_ref, node_at + 2 * first, 2 * block))
                inv = inverse(se + wl + wr)
                gl, gr = wl * inv, wr * inv
                push = gl * se
                surplus = so + gr * se + shifted_up(push, carry)
            carry = push[:1]
            put_nodes(gl_ref, pair_at + first, gl)
            put_nodes(gr_ref, pair_at + first, gr)
            put_nodes(r_ref, pair_at + first, inv)
            put_nodes(w_ref, L - 2 * half + first, gl * wr)
            put_nodes(s_ref, L - 2 * half + first, surplus)
        pushed_out = pushed_out + carry
    return w_ref[pl.ds((L - 2) * NZ, NZ), :], s_ref[pl.ds((L - 2) * NZ, NZ), :], pushed_out[0]


def eliminate_right_side(side_ref, gl_ref, gr_ref, r_ref, d_ref, q_ref):
    pushed_out = jnp.zeros((1, NZ, L), jnp.float32)
    for count, half, node_at, pair_at in levels():
        block = min(half, BLOCK)
        carry = jnp.zeros((1, NZ, L), jnp.float32)
        for first in reversed(range(0, half, block)):
            if count == L:
                de, do = pairs(nodes(side_ref, 2 * first, 2 * block))
            else:
                de, do = pairs(nodes(d_ref, node_at + 2 * first, 2 * block))
            push = nodes(gl_ref, pair_at + first, block) * de
            side = do + nodes(gr_ref, pair_at + first, block) * de + shifted_up(push, carry)
            carry = push[:1]
            put_nodes(q_ref, pair_at + first, nodes(r_ref, pair_at + first, block) * de)
            put_nodes(d_ref, L - 2 * half + first, side)
        pushed_out = pushed_out + carry
    return d_ref[pl.ds((L - 2) * NZ, NZ), :], pushed_out[0]


def substitute(before, last, gl_ref, gr_ref, q_ref, v_ref, store):
    v_ref[pl.ds((L - 2) * NZ, NZ), :] = last
    for count, half, node_at, pair_at in reversed(list(levels())):
        block = min(half, BLOCK)
        carry = before[None]
        for first in range(0, half, block):
            vo = nodes(v_ref, L - 2 * half + first, block)
            ve = (
                nodes(gl_ref, pair_at + first, block) * shifted_down(vo, carry)
                + nodes(gr_ref, pair_at + first, block) * vo
                + nodes(q_ref, pair_at + first, block)
            )
            carry = vo[block - 1 :]
            joined = jnp.stack([ve, vo], axis=1).reshape(2 * block, NZ, L)
            if count == L:
                store(2 * first, joined)
            else:
                put_nodes(v_ref, node_at + 2 * first, joined)


def factor_chain(n, coefficients, chain_g, chain_r):
    flow = None
    for p in range(n):
        surplus = coefficients[p, NZ : 2 * NZ, :]
        if p < n - 1:
            surplus = surplus + coefficients[p + 1, 2 * NZ :, :]
        if flow is not None:
            surplus = surplus + flow
        if p < n - 1:
            weight = coefficients[p + 1, :NZ, :]
            inv = inverse(surplus + weight)
            share = weight * inv
            chain_g[p] = share
            flow = share * surplus
        else:
            inv = inverse(surplus)
        chain_r[p] = inv


def solve_chain(n, sides, chain_g, chain_r, chain_v):
    flow = None
    scaled = []
    for p in range(n):
        side = sides[p, :NZ, :]
        if p < n - 1:
            side = side + sides[p + 1, NZ:, :]
        if flow is not None:
            side = side + flow
        if p < n - 1:
            flow = chain_g[p] * side
        scaled.append(side * chain_r[p])
    value = scaled[n - 1]
    chain_v[0] = jnp.zeros((NZ, L), jnp.float32)
    chain_v[n] = value
    for p in reversed(range(n - 1)):
        value = scaled[p] + chain_g[p] * value
        chain_v[p + 1] = value


class Gather:
    def __init__(self, axis, n, buffer, send, recv):
        self.axis, self.n, self.buffer, self.send, self.recv = axis, n, buffer, send, recv
        self.me = lax.axis_index(axis)

    def copy(self, step, slot):
        return pltpu.make_async_remote_copy(
            src_ref=self.buffer.at[slot],
            dst_ref=self.buffer.at[slot],
            send_sem=self.send.at[step - 1],
            recv_sem=self.recv.at[step - 1],
            device_id={self.axis: lax.rem(self.me + step, self.n)},
            device_id_type=MESH,
        )

    def start(self):
        for step in range(1, self.n):
            self.copy(step, self.me).start()

    def wait(self):
        for step in range(1, self.n):
            self.copy(step, lax.rem(self.me + self.n - step, self.n)).wait_recv()

    def finish(self):
        for step in range(1, self.n):
            self.copy(step, self.me).wait_send()


class Halo:
    def __init__(self, axis, n, edges, halo, send, recv):
        self.axis, self.n, self.edges, self.halo, self.send, self.recv = axis, n, edges, halo, send, recv
        self.me = lax.axis_index(axis)

    def copy(self, side):
        to = self.me - 1 if side == 0 else self.me + 1
        return pltpu.make_async_remote_copy(
            src_ref=self.edges.at[side],
            dst_ref=self.halo.at[1 - side],
            send_sem=self.send.at[side],
            recv_sem=self.recv.at[1 - side],
            device_id={self.axis: to},
            device_id_type=MESH,
        )

    def start(self):
        @pl.when(self.me > 0)
        def _():
            self.copy(0).start()

        @pl.when(self.me < self.n - 1)
        def _():
            self.copy(1).start()

    def wait(self):
        @pl.when(self.me > 0)
        def _():
            self.copy(1).wait_recv()

        @pl.when(self.me == 0)
        def _():
            self.halo[0] = jnp.zeros((2 * NZ, L), jnp.float32)

        @pl.when(self.me < self.n - 1)
        def _():
            self.copy(0).wait_recv()

        @pl.when(self.me == self.n - 1)
        def _():
            self.halo[1] = jnp.zeros((2 * NZ, L), jnp.float32)

    def finish(self):
        @pl.when(self.me > 0)
        def _():
            self.copy(0).wait_send()

        @pl.when(self.me < self.n - 1)
        def _():
            self.copy(1).wait_send()


def links(cond, field, cond_before, field_before):
    beside = shifted_down(cond, cond_before)
    weight = (2.0 * inplane_half) * cond * beside * inverse(cond + beside)
    return weight, weight * (field - shifted_down(field, field_before))


def kernel(
    n_row,
    n_col,
    mag,
    rate,
    field_hbm,
    region_hbm,
    source_hbm,
    out_hbm,
    field,
    region,
    source,
    cond,
    base,
    half_y,
    link_y,
    field_x,
    cond_x,
    side_x,
    link_x,
    solved,
    out,
    gl_x,
    gr_x,
    r_x,
    gl_y,
    gr_y,
    r_y,
    work_a,
    work_b,
    edges_y,
    halo_y,
    edges_x,
    halo_x,
    coef_x,
    rhs_x,
    coef_y,
    rhs_y,
    chain_gx,
    chain_rx,
    chain_vx,
    chain_gy,
    chain_ry,
    chain_vy,
    in_sem,
    out_sem,
    hy_send,
    hy_recv,
    hx_send,
    hx_recv,
    cx_send,
    cx_recv,
    rx_send,
    rx_recv,
    cy_send,
    cy_recv,
    ry_send,
    ry_recv,
):
    loads = [
        pltpu.make_async_copy(field_hbm, field, in_sem.at[0]),
        pltpu.make_async_copy(region_hbm, region, in_sem.at[1]),
        pltpu.make_async_copy(source_hbm, source, in_sem.at[2]),
    ]
    for load in loads:
        load.start()
    my_row, my_col = lax.axis_index("row"), lax.axis_index("col")
    barrier = pltpu.get_barrier_semaphore()
    for step in range(1, n_row):
        pl.semaphore_signal(
            barrier, inc=1, device_id={"row": lax.rem(my_row + step, n_row)}, device_id_type=MESH
        )
    for step in range(1, n_col):
        pl.semaphore_signal(
            barrier, inc=1, device_id={"col": lax.rem(my_col + step, n_col)}, device_id_type=MESH
        )

    share_y = Halo("row", n_row, edges_y, halo_y, hy_send, hy_recv)
    share_x = Halo("col", n_col, edges_x, halo_x, hx_send, hx_recv)
    gather_cx = Gather("col", n_col, coef_x, cx_send, cx_recv)
    gather_rx = Gather("col", n_col, rhs_x, rx_send, rx_recv)
    gather_cy = Gather("row", n_row, coef_y, cy_send, cy_recv)
    gather_ry = Gather("row", n_row, rhs_y, ry_send, ry_recv)

    m0, m1, m2 = mag[0], mag[1], mag[2]
    k0, k1, k2 = rate[0], rate[1], rate[2]

    def conductivity(kelvin, kind):
        first, second = kind == 0, kind == 1
        scale = jnp.where(first, m0, jnp.where(second, m1, m2))
        soft = jnp.where(first, k0, jnp.where(second, k1, k2))
        return scale * jnp.exp(-soft * kelvin)

    loads[0].wait()
    loads[1].wait()
    for side, y in ((0, 0), (1, L - 1)):
        kelvin = field[pl.ds(y, NZ, stride=L), :]
        edges_y[side, :NZ, :] = kelvin
        edges_y[side, NZ:, :] = conductivity(kelvin, region[pl.ds(y, NZ, stride=L), :])
    pl.semaphore_wait(barrier, n_row + n_col - 2)
    share_y.start()

    for z in range(NZ):
        rows = pl.ds(z * L, L)
        kelvin = field[rows, :]
        value = conductivity(kelvin, region[rows, :])
        cond[rows, :] = value
        field_x[pl.ds(z, L, stride=NZ), :] = kelvin.T
        cond_x[pl.ds(z, L, stride=NZ), :] = value.T
    for side, x in ((0, 0), (1, L - 1)):
        edges_x[side, :NZ, :] = field_x[pl.ds(x * NZ, NZ), :]
        edges_x[side, NZ:, :] = cond_x[pl.ds(x * NZ, NZ), :]
    share_x.start()

    share_y.wait()
    t_before, c_before = halo_y[0, :NZ, :][None], halo_y[0, NZ:, :][None]
    flux_before = None
    for first in range(0, L + 1, BLOCK):
        if first < L:
            t = jnp.stack([field[pl.ds(first + i, NZ, stride=L), :] for i in range(BLOCK)])
            c = jnp.stack([cond[pl.ds(first + i, NZ, stride=L), :] for i in range(BLOCK)])
        else:
            t, c = halo_y[1, :NZ, :][None], halo_y[1, NZ:, :][None]
        weight, flux = links(c, t, c_before, t_before)
        if first < L:
            put_nodes(link_y, first, weight)
            put_nodes(half_y, first, shifted_up(flux, flux[-1:]) - flux)
        if flux_before is not None:
            half_y[pl.ds((first - 1) * NZ, NZ), :] = flux[0] - flux_before
        t_before, c_before, flux_before = t[-1:], c[-1:], flux[-1]
    w, s, push = eliminate_coefficients(link_y, gl_y, gr_y, r_y, work_a, work_b)
    coef_y[my_row, :NZ, :] = w
    coef_y[my_row, NZ : 2 * NZ, :] = s
    coef_y[my_row, 2 * NZ :, :] = push
    gather_cy.start()

    loads[2].wait()
    lower = None
    for z in range(NZ):
        rows = pl.ds(z * L, L)
        t, c = field[rows, :], cond[rows, :]
        if z == 0:
            lower = depth_ratio * c * t
        if z < NZ - 1:
            above = pl.ds((z + 1) * L, L)
            ta, ca = field[above, :], cond[above, :]
            upper = (2.0 * depth_ratio) * c * ca * inverse(c + ca) * (ta - t)
            along_z = upper - lower
            lower = upper
        else:
            along_z = -lower
        total = t + 2.0 * half_y[pl.ds(z, L, stride=NZ), :] + along_z + source[rows, :]
        side_x[pl.ds(z, L, stride=NZ), :] = total.T

    share_x.wait()
    t_before, c_before = halo_x[0, :NZ, :][None], halo_x[0, NZ:, :][None]
    flux_before = None
    for first in range(0, L + 1, BLOCK):
        if first < L:
            t, c = nodes(field_x, first, BLOCK), nodes(cond_x, first, BLOCK)
        else:
            t, c = halo_x[1, :NZ, :][None], halo_x[1, NZ:, :][None]
        weight, flux = links(c, t, c_before, t_before)
        if first < L:
            put_nodes(link_x, first, weight)
            extra = shifted_up(flux, jnp.zeros((1, NZ, L), jnp.float32)) - flux
            put_nodes(side_x, first, nodes(side_x, first, BLOCK) + extra)
        if first > 0:
            at = pl.ds((first - 1) * NZ, NZ)
            side_x[at, :] = side_x[at, :] + flux[0]
        t_before, c_before = t[-1:], c[-1:]
    w, s, push = eliminate_coefficients(link_x, gl_x, gr_x, r_x, work_a, work_b)
    coef_x[my_col, :NZ, :] = w
    coef_x[my_col, NZ : 2 * NZ, :] = s
    coef_x[my_col, 2 * NZ :, :] = push
    gather_cx.start()
    d, push = eliminate_right_side(side_x, gl_x, gr_x, r_x, work_a, work_b)
    rhs_x[my_col, :NZ, :] = d
    rhs_x[my_col, NZ:, :] = push
    gather_rx.start()

    gather_cy.wait()
    factor_chain(n_row, coef_y, chain_gy, chain_ry)
    gather_cx.wait()
    factor_chain(n_col, coef_x, chain_gx, chain_rx)
    gather_rx.wait()
    solve_chain(n_col, rhs_x, chain_gx, chain_rx, chain_vx)

    def store_x(first, values):
        put_nodes(solved, first, values)

    substitute(chain_vx[my_col], chain_vx[my_col + 1], gl_x, gr_x, work_b, work_a, store_x)

    for z in range(NZ):
        at = pl.ds(z, L, stride=NZ)
        side_x[at, :] = solved[at, :].T - half_y[at, :]
    d, push = eliminate_right_side(side_x, gl_y, gr_y, r_y, work_a, work_b)
    rhs_y[my_row, :NZ, :] = d
    rhs_y[my_row, NZ:, :] = push
    gather_ry.start()
    gather_ry.wait()
    solve_chain(n_row, rhs_y, chain_gy, chain_ry, chain_vy)

    def store_y(first, values):
        for i in range(values.shape[0]):
            out[pl.ds(first + i, NZ, stride=L), :] = values[i]

    substitute(chain_vy[my_row], chain_vy[my_row + 1], gl_y, gr_y, work_b, work_a, store_y)
    result = pltpu.make_async_copy(out, out_hbm, out_sem)
    result.start()
    for transfer in (share_y, share_x, gather_cx, gather_rx, gather_cy, gather_ry):
        transfer.finish()
    result.wait()


def solution(mesh):
    n_row, n_col = mesh.shape["row"], mesh.shape["col"]

    def local(field, region, source, mag, rate):
        def flat(values):
            return values.reshape(NZ * L, L)

        whole = pltpu.VMEM((NZ * L, L), jnp.float32)
        integer = pltpu.VMEM((NZ * L, L), jnp.int32)

        def stack(count, height):
            return pltpu.VMEM((count, height * NZ, L), jnp.float32)

        def dma(count):
            return pltpu.SemaphoreType.DMA((count,))

        result = pl.pallas_call(
            functools.partial(kernel, n_row, n_col),
            out_shape=jax.ShapeDtypeStruct((NZ * L, L), jnp.float32),
            in_specs=[pl.BlockSpec(memory_space=pltpu.SMEM)] * 2 + [pl.BlockSpec(memory_space=pl.ANY)] * 3,
            out_specs=pl.BlockSpec(memory_space=pl.ANY),
            scratch_shapes=[whole, integer]
            + [whole] * 19
            + [stack(2, 2)] * 4
            + [stack(n_col, 3), stack(n_col, 2), stack(n_row, 3), stack(n_row, 2)]
            + [stack(n_col, 1), stack(n_col, 1), stack(n_col + 1, 1)]
            + [stack(n_row, 1), stack(n_row, 1), stack(n_row + 1, 1)]
            + [dma(3), pltpu.SemaphoreType.DMA]
            + [dma(2)] * 4
            + [dma(n_col - 1)] * 4
            + [dma(n_row - 1)] * 4,
            compiler_params=pltpu.CompilerParams(
                collective_id=0, has_side_effects=True, vmem_limit_bytes=40 * 1024 * 1024
            ),
            cost_estimate=pl.CostEstimate(
                flops=20_000_000, bytes_accessed=2_200_000, transcendentals=400_000
            ),
        )(mag, rate, flat(field), flat(region), flat(source))
        return result.reshape(NZ, L, L)

    spec = P(None, "row", "col")
    return jax.shard_map(
        local, mesh=mesh, in_specs=(spec, spec, spec, P(), P()), out_specs=spec, check_vma=False
    )
```

```python
import functools

import jax
import jax.numpy as jnp
from jax import lax
from jax.experimental import pallas as pl
from jax.experimental.pallas import tpu as pltpu
from jax.sharding import PartitionSpec as P

MESH = pl.DeviceIdType.MESH
inplane_half = 500.0
depth_ratio = 0.08

NZ = 8
L = 128
BLOCK = 16


def inverse(value):
    guess = pl.reciprocal(value, approx=True)
    return guess * (2.0 - value * guess)


def pairs(values):
    split = values.reshape((values.shape[0] // 2, 2) + values.shape[1:])
    return split[:, 0], split[:, 1]


def shifted_up(values, last):
    if values.shape[0] == 1:
        return last
    return jnp.concatenate([values[1:], last], axis=0)


def shifted_down(values, first):
    if values.shape[0] == 1:
        return first
    return jnp.concatenate([first, values[:-1]], axis=0)


def nodes(ref, first, count):
    return ref[pl.ds(first * NZ, count * NZ), :].reshape(count, NZ, L)


def put_nodes(ref, first, values):
    count = values.shape[0]
    ref[pl.ds(first * NZ, count * NZ), :] = values.reshape(count * NZ, L)


def levels():
    count = L
    while count > 1:
        half = count // 2
        yield count, half, L - 2 * count, L - 2 * half
        count = half


def eliminate_coefficients(link_ref, gl_ref, gr_ref, r_ref, w_ref, s_ref):
    pushed_out = jnp.zeros((1, NZ, L), jnp.float32)
    for count, half, node_at, pair_at in levels():
        block = min(half, BLOCK)
        carry = jnp.zeros((1, NZ, L), jnp.float32)
        for first in reversed(range(0, half, block)):
            if count == L:
                wl, wr = pairs(nodes(link_ref, 2 * first, 2 * block))
                inv = inverse(1.0 + wl + wr)
                gl, gr = wl * inv, wr * inv
                push = gl
                surplus = 1.0 + gr + shifted_up(push, carry)
            else:
                wl, wr = pairs(nodes(w_ref, node_at + 2 * first, 2 * block))
                se, so = pairs(nodes(s_ref, node_at + 2 * first, 2 * block))
                inv = inverse(se + wl + wr)
                gl, gr = wl * inv, wr * inv
                push = gl * se
                surplus = so + gr * se + shifted_up(push, carry)
            carry = push[:1]
            put_nodes(gl_ref, pair_at + first, gl)
            put_nodes(gr_ref, pair_at + first, gr)
            put_nodes(r_ref, pair_at + first, inv)
            put_nodes(w_ref, L - 2 * half + first, gl * wr)
            put_nodes(s_ref, L - 2 * half + first, surplus)
        pushed_out = pushed_out + carry
    return w_ref[pl.ds((L - 2) * NZ, NZ), :], s_ref[pl.ds((L - 2) * NZ, NZ), :], pushed_out[0]


def eliminate_right_side(side_ref, gl_ref, gr_ref, r_ref, d_ref, q_ref):
    pushed_out = jnp.zeros((1, NZ, L), jnp.float32)
    for count, half, node_at, pair_at in levels():
        block = min(half, BLOCK)
        carry = jnp.zeros((1, NZ, L), jnp.float32)
        for first in reversed(range(0, half, block)):
            if count == L:
                de, do = pairs(nodes(side_ref, 2 * first, 2 * block))
            else:
                de, do = pairs(nodes(d_ref, node_at + 2 * first, 2 * block))
            push = nodes(gl_ref, pair_at + first, block) * de
            side = do + nodes(gr_ref, pair_at + first, block) * de + shifted_up(push, carry)
            carry = push[:1]
            put_nodes(q_ref, pair_at + first, nodes(r_ref, pair_at + first, block) * de)
            put_nodes(d_ref, L - 2 * half + first, side)
        pushed_out = pushed_out + carry
    return d_ref[pl.ds((L - 2) * NZ, NZ), :], pushed_out[0]


def substitute(before, last, gl_ref, gr_ref, q_ref, v_ref, store):
    v_ref[pl.ds((L - 2) * NZ, NZ), :] = last
    for count, half, node_at, pair_at in reversed(list(levels())):
        block = min(half, BLOCK)
        carry = before[None]
        for first in range(0, half, block):
            vo = nodes(v_ref, L - 2 * half + first, block)
            ve = (
                nodes(gl_ref, pair_at + first, block) * shifted_down(vo, carry)
                + nodes(gr_ref, pair_at + first, block) * vo
                + nodes(q_ref, pair_at + first, block)
            )
            carry = vo[block - 1 :]
            joined = jnp.stack([ve, vo], axis=1).reshape(2 * block, NZ, L)
            if count == L:
                store(2 * first, joined)
            else:
                put_nodes(v_ref, node_at + 2 * first, joined)


def factor_chain(n, coefficients, chain_g, chain_r):
    flow = None
    for p in range(n):
        surplus = coefficients[p, NZ : 2 * NZ, :]
        if p < n - 1:
            surplus = surplus + coefficients[p + 1, 2 * NZ :, :]
        if flow is not None:
            surplus = surplus + flow
        if p < n - 1:
            weight = coefficients[p + 1, :NZ, :]
            inv = inverse(surplus + weight)
            share = weight * inv
            chain_g[p] = share
            flow = share * surplus
        else:
            inv = inverse(surplus)
        chain_r[p] = inv


def solve_chain(n, sides, chain_g, chain_r, chain_v):
    flow = None
    scaled = []
    for p in range(n):
        side = sides[p, :NZ, :]
        if p < n - 1:
            side = side + sides[p + 1, NZ:, :]
        if flow is not None:
            side = side + flow
        if p < n - 1:
            flow = chain_g[p] * side
        scaled.append(side * chain_r[p])
    value = scaled[n - 1]
    chain_v[0] = jnp.zeros((NZ, L), jnp.float32)
    chain_v[n] = value
    for p in reversed(range(n - 1)):
        value = scaled[p] + chain_g[p] * value
        chain_v[p + 1] = value


class Gather:
    def __init__(self, axis, n, buffer, send, recv):
        self.axis, self.n, self.buffer, self.send, self.recv = axis, n, buffer, send, recv
        self.me = lax.axis_index(axis)

    def copy(self, step, slot):
        return pltpu.make_async_remote_copy(
            src_ref=self.buffer.at[slot],
            dst_ref=self.buffer.at[slot],
            send_sem=self.send.at[step - 1],
            recv_sem=self.recv.at[step - 1],
            device_id={self.axis: lax.rem(self.me + step, self.n)},
            device_id_type=MESH,
        )

    def start(self):
        for step in range(1, self.n):
            self.copy(step, self.me).start()

    def wait(self):
        for step in range(1, self.n):
            self.copy(step, lax.rem(self.me + self.n - step, self.n)).wait_recv()

    def finish(self):
        for step in range(1, self.n):
            self.copy(step, self.me).wait_send()


class Halo:
    def __init__(self, axis, n, edges, halo, send, recv):
        self.axis, self.n, self.edges, self.halo, self.send, self.recv = axis, n, edges, halo, send, recv
        self.me = lax.axis_index(axis)

    def copy(self, side):
        to = self.me - 1 if side == 0 else self.me + 1
        return pltpu.make_async_remote_copy(
            src_ref=self.edges.at[side],
            dst_ref=self.halo.at[1 - side],
            send_sem=self.send.at[side],
            recv_sem=self.recv.at[1 - side],
            device_id={self.axis: to},
            device_id_type=MESH,
        )

    def start(self):
        @pl.when(self.me > 0)
        def _():
            self.copy(0).start()

        @pl.when(self.me < self.n - 1)
        def _():
            self.copy(1).start()

    def wait(self):
        @pl.when(self.me > 0)
        def _():
            self.copy(1).wait_recv()

        @pl.when(self.me == 0)
        def _():
            self.halo[0] = jnp.zeros((2 * NZ, L), jnp.float32)

        @pl.when(self.me < self.n - 1)
        def _():
            self.copy(0).wait_recv()

        @pl.when(self.me == self.n - 1)
        def _():
            self.halo[1] = jnp.zeros((2 * NZ, L), jnp.float32)

    def finish(self):
        @pl.when(self.me > 0)
        def _():
            self.copy(0).wait_send()

        @pl.when(self.me < self.n - 1)
        def _():
            self.copy(1).wait_send()


def links(cond, field, cond_before, field_before):
    beside = shifted_down(cond, cond_before)
    weight = (2.0 * inplane_half) * cond * beside * inverse(cond + beside)
    return weight, weight * (field - shifted_down(field, field_before))


def kernel(
    n_row,
    n_col,
    mag_hbm,
    rate_hbm,
    field_hbm,
    region_hbm,
    source_hbm,
    out,
    mag,
    rate,
    field,
    region,
    source,
    cond,
    half_y,
    link_y,
    field_x,
    cond_x,
    side_x,
    link_x,
    solved,
    gl_x,
    gr_x,
    r_x,
    gl_y,
    gr_y,
    r_y,
    work_a,
    work_b,
    work_c,
    work_d,
    edges_y,
    halo_y,
    edges_x,
    halo_x,
    coef_x,
    rhs_x,
    coef_y,
    rhs_y,
    chain_gx,
    chain_rx,
    chain_vx,
    chain_gy,
    chain_ry,
    chain_vy,
    par_sem,
    in_sem,
    hy_send,
    hy_recv,
    hx_send,
    hx_recv,
    cx_send,
    cx_recv,
    rx_send,
    rx_recv,
    cy_send,
    cy_recv,
    ry_send,
    ry_recv,
):
    parameters = [
        pltpu.make_async_copy(mag_hbm, mag, par_sem.at[0]),
        pltpu.make_async_copy(rate_hbm, rate, par_sem.at[1]),
    ]
    for load in parameters:
        load.start()

    def layer(source_ref, target_ref, kind, z):
        rows = pl.ds(z * L, L)
        return pltpu.make_async_copy(source_ref.at[rows], target_ref.at[rows], in_sem.at[kind, z])

    loads = [
        (layer(field_hbm, field, 0, z), layer(region_hbm, region, 1, z)) for z in range(NZ)
    ]
    source_loads = [layer(source_hbm, source, 2, z) for z in range(NZ)]
    for field_load, region_load in loads:
        field_load.start()
        region_load.start()
    for load in source_loads:
        load.start()
    my_row, my_col = lax.axis_index("row"), lax.axis_index("col")
    barrier = pltpu.get_barrier_semaphore()
    for step in range(1, n_row):
        pl.semaphore_signal(
            barrier, inc=1, device_id={"row": lax.rem(my_row + step, n_row)}, device_id_type=MESH
        )
    for step in range(1, n_col):
        pl.semaphore_signal(
            barrier, inc=1, device_id={"col": lax.rem(my_col + step, n_col)}, device_id_type=MESH
        )

    share_y = Halo("row", n_row, edges_y, halo_y, hy_send, hy_recv)
    share_x = Halo("col", n_col, edges_x, halo_x, hx_send, hx_recv)
    gather_cx = Gather("col", n_col, coef_x, cx_send, cx_recv)
    gather_rx = Gather("col", n_col, rhs_x, rx_send, rx_recv)
    gather_cy = Gather("row", n_row, coef_y, cy_send, cy_recv)
    gather_ry = Gather("row", n_row, rhs_y, ry_send, ry_recv)

    for load in parameters:
        load.wait()
    m0, m1, m2 = mag[0], mag[1], mag[2]
    k0, k1, k2 = rate[0], rate[1], rate[2]

    def conductivity(kelvin, kind):
        first, second = kind == 0, kind == 1
        scale = jnp.where(first, m0, jnp.where(second, m1, m2))
        soft = jnp.where(first, k0, jnp.where(second, k1, k2))
        return scale * jnp.exp(-soft * kelvin)

    for z in range(NZ):
        rows = pl.ds(z * L, L)
        for load in loads[z]:
            load.wait()
        cond[rows, :] = conductivity(field[rows, :], region[rows, :])
    for side, y in ((0, 0), (1, L - 1)):
        edges_y[side, :NZ, :] = field[pl.ds(y, NZ, stride=L), :]
        edges_y[side, NZ:, :] = cond[pl.ds(y, NZ, stride=L), :]
    pl.semaphore_wait(barrier, n_row + n_col - 2)
    share_y.start()

    for z in range(NZ):
        rows = pl.ds(z * L, L)
        field_x[pl.ds(z, L, stride=NZ), :] = field[rows, :].T
        cond_x[pl.ds(z, L, stride=NZ), :] = cond[rows, :].T
    for side, x in ((0, 0), (1, L - 1)):
        edges_x[side, :NZ, :] = field_x[pl.ds(x * NZ, NZ), :]
        edges_x[side, NZ:, :] = cond_x[pl.ds(x * NZ, NZ), :]
    share_x.start()

    share_y.wait()
    t_before, c_before = halo_y[0, :NZ, :][None], halo_y[0, NZ:, :][None]
    flux_before = None
    for first in range(0, L + 1, BLOCK):
        if first < L:
            t = jnp.stack([field[pl.ds(first + i, NZ, stride=L), :] for i in range(BLOCK)])
            c = jnp.stack([cond[pl.ds(first + i, NZ, stride=L), :] for i in range(BLOCK)])
        else:
            t, c = halo_y[1, :NZ, :][None], halo_y[1, NZ:, :][None]
        weight, flux = links(c, t, c_before, t_before)
        if first < L:
            put_nodes(link_y, first, weight)
            put_nodes(half_y, first, shifted_up(flux, flux[-1:]) - flux)
        if flux_before is not None:
            half_y[pl.ds((first - 1) * NZ, NZ), :] = flux[0] - flux_before
        t_before, c_before, flux_before = t[-1:], c[-1:], flux[-1]

    for load in source_loads:
        load.wait()
    lower = None
    for z in range(NZ):
        rows = pl.ds(z * L, L)
        t, c = field[rows, :], cond[rows, :]
        if z == 0:
            lower = depth_ratio * c * t
        if z < NZ - 1:
            above = pl.ds((z + 1) * L, L)
            ta, ca = field[above, :], cond[above, :]
            upper = (2.0 * depth_ratio) * c * ca * inverse(c + ca) * (ta - t)
            along_z = upper - lower
            lower = upper
        else:
            along_z = -lower
        total = t + 2.0 * half_y[pl.ds(z, L, stride=NZ), :] + along_z + source[rows, :]
        side_x[pl.ds(z, L, stride=NZ), :] = total.T

    share_x.wait()
    t_before, c_before = halo_x[0, :NZ, :][None], halo_x[0, NZ:, :][None]
    flux_before = None
    for first in range(0, L + 1, BLOCK):
        if first < L:
            t, c = nodes(field_x, first, BLOCK), nodes(cond_x, first, BLOCK)
        else:
            t, c = halo_x[1, :NZ, :][None], halo_x[1, NZ:, :][None]
        weight, flux = links(c, t, c_before, t_before)
        if first < L:
            put_nodes(link_x, first, weight)
            extra = shifted_up(flux, jnp.zeros((1, NZ, L), jnp.float32)) - flux
            put_nodes(side_x, first, nodes(side_x, first, BLOCK) + extra)
        if first > 0:
            at = pl.ds((first - 1) * NZ, NZ)
            side_x[at, :] = side_x[at, :] + flux[0]
        t_before, c_before = t[-1:], c[-1:]
    w, s, push = eliminate_coefficients(link_x, gl_x, gr_x, r_x, work_a, work_b)
    coef_x[my_col, :NZ, :] = w
    coef_x[my_col, NZ : 2 * NZ, :] = s
    coef_x[my_col, 2 * NZ :, :] = push
    gather_cx.start()
    d, push = eliminate_right_side(side_x, gl_x, gr_x, r_x, work_a, work_b)
    rhs_x[my_col, :NZ, :] = d
    rhs_x[my_col, NZ:, :] = push
    gather_rx.start()

    w, s, push = eliminate_coefficients(link_y, gl_y, gr_y, r_y, work_c, work_d)
    coef_y[my_row, :NZ, :] = w
    coef_y[my_row, NZ : 2 * NZ, :] = s
    coef_y[my_row, 2 * NZ :, :] = push
    gather_cy.start()
    gather_cx.wait()
    factor_chain(n_col, coef_x, chain_gx, chain_rx)
    gather_rx.wait()
    solve_chain(n_col, rhs_x, chain_gx, chain_rx, chain_vx)

    def store_x(first, values):
        put_nodes(solved, first, values)

    substitute(chain_vx[my_col], chain_vx[my_col + 1], gl_x, gr_x, work_b, work_a, store_x)

    for z in range(NZ):
        at = pl.ds(z, L, stride=NZ)
        side_x[at, :] = solved[at, :].T - half_y[at, :]
    d, push = eliminate_right_side(side_x, gl_y, gr_y, r_y, work_a, work_b)
    rhs_y[my_row, :NZ, :] = d
    rhs_y[my_row, NZ:, :] = push
    gather_ry.start()
    gather_cy.wait()
    factor_chain(n_row, coef_y, chain_gy, chain_ry)
    gather_ry.wait()
    solve_chain(n_row, rhs_y, chain_gy, chain_ry, chain_vy)

    def store_y(first, values):
        for i in range(values.shape[0]):
            out[pl.ds(first + i, NZ, stride=L), :] = values[i]

    substitute(chain_vy[my_row], chain_vy[my_row + 1], gl_y, gr_y, work_b, work_a, store_y)
    for transfer in (share_y, share_x, gather_cx, gather_rx, gather_cy, gather_ry):
        transfer.finish()


def solution(mesh):
    n_row, n_col = mesh.shape["row"], mesh.shape["col"]

    def local(field, region, source, mag, rate):
        def flat(values):
            return values.reshape(NZ * L, L)

        whole = pltpu.VMEM((NZ * L, L), jnp.float32)
        integer = pltpu.VMEM((NZ * L, L), jnp.int32)

        parameter = pltpu.SMEM((3,), jnp.float32)

        def stack(count, height):
            return pltpu.VMEM((count, height * NZ, L), jnp.float32)

        def dma(count):
            return pltpu.SemaphoreType.DMA((count,))

        result = pl.pallas_call(
            functools.partial(kernel, n_row, n_col),
            out_shape=pltpu.VMEM((NZ * L, L), jnp.float32),
            in_specs=[pl.BlockSpec(memory_space=pltpu.HBM)] * 5,
            out_specs=pl.BlockSpec(memory_space=pltpu.VMEM),
            scratch_shapes=[parameter, parameter, whole, integer]
            + [whole] * 19
            + [stack(2, 2)] * 4
            + [stack(n_col, 3), stack(n_col, 2), stack(n_row, 3), stack(n_row, 2)]
            + [stack(n_col, 1), stack(n_col, 1), stack(n_col + 1, 1)]
            + [stack(n_row, 1), stack(n_row, 1), stack(n_row + 1, 1)]
            + [dma(2), pltpu.SemaphoreType.DMA((3, NZ))]
            + [dma(2)] * 4
            + [dma(n_col - 1)] * 4
            + [dma(n_row - 1)] * 4,
            compiler_params=pltpu.CompilerParams(
                collective_id=0, has_side_effects=True, vmem_limit_bytes=40 * 1024 * 1024
            ),
            cost_estimate=pl.CostEstimate(
                flops=20_000_000, bytes_accessed=2_200_000, transcendentals=400_000
            ),
        )(*[pltpu.with_memory_space_constraint(v, pltpu.HBM) for v in (mag, rate, flat(field), flat(region), flat(source))])
        return result.reshape(NZ, L, L)

    spec = P(None, "row", "col")
    return jax.shard_map(
        local, mesh=mesh, in_specs=(spec, spec, spec, P(), P()), out_specs=spec, check_vma=False
    )
```

```python
import functools

import jax
import jax.numpy as jnp
from jax import lax
from jax.experimental import pallas as pl
from jax.experimental.pallas import tpu as pltpu
from jax.sharding import PartitionSpec as P

MESH = pl.DeviceIdType.MESH
inplane_half = 500.0
depth_ratio = 0.08

NZ = 8
L = 128
BLOCK = 16


def inverse(value):
    guess = pl.reciprocal(value, approx=True)
    return guess * (2.0 - value * guess)


def pairs(values):
    split = values.reshape((values.shape[0] // 2, 2) + values.shape[1:])
    return split[:, 0], split[:, 1]


def shifted_up(values, last):
    if values.shape[0] == 1:
        return last
    return jnp.concatenate([values[1:], last], axis=0)


def shifted_down(values, first):
    if values.shape[0] == 1:
        return first
    return jnp.concatenate([first, values[:-1]], axis=0)


def nodes(ref, first, count):
    return ref[pl.ds(first * NZ, count * NZ), :].reshape(count, NZ, L)


def put_nodes(ref, first, values):
    count = values.shape[0]
    ref[pl.ds(first * NZ, count * NZ), :] = values.reshape(count * NZ, L)


def levels():
    count = L
    while count > 1:
        half = count // 2
        yield count, half, L - 2 * count, L - 2 * half
        count = half


def eliminate_coefficients(link_ref, gl_ref, gr_ref, r_ref, w_ref, s_ref):
    pushed_out = jnp.zeros((1, NZ, L), jnp.float32)
    for count, half, node_at, pair_at in levels():
        block = min(half, BLOCK)
        carry = jnp.zeros((1, NZ, L), jnp.float32)
        for first in reversed(range(0, half, block)):
            if count == L:
                wl, wr = pairs(nodes(link_ref, 2 * first, 2 * block))
                inv = inverse(1.0 + wl + wr)
                gl, gr = wl * inv, wr * inv
                push = gl
                surplus = 1.0 + gr + shifted_up(push, carry)
            else:
                wl, wr = pairs(nodes(w_ref, node_at + 2 * first, 2 * block))
                se, so = pairs(nodes(s_ref, node_at + 2 * first, 2 * block))
                inv = inverse(se + wl + wr)
                gl, gr = wl * inv, wr * inv
                push = gl * se
                surplus = so + gr * se + shifted_up(push, carry)
            carry = push[:1]
            put_nodes(gl_ref, pair_at + first, gl)
            put_nodes(gr_ref, pair_at + first, gr)
            put_nodes(r_ref, pair_at + first, inv)
            put_nodes(w_ref, L - 2 * half + first, gl * wr)
            put_nodes(s_ref, L - 2 * half + first, surplus)
        pushed_out = pushed_out + carry
    return w_ref[pl.ds((L - 2) * NZ, NZ), :], s_ref[pl.ds((L - 2) * NZ, NZ), :], pushed_out[0]


def eliminate_right_side(load_side, gl_ref, gr_ref, r_ref, d_ref, q_ref):
    pushed_out = jnp.zeros((1, NZ, L), jnp.float32)
    for count, half, node_at, pair_at in levels():
        block = min(half, BLOCK)
        carry = jnp.zeros((1, NZ, L), jnp.float32)
        for first in reversed(range(0, half, block)):
            if count == L:
                de, do = pairs(load_side(2 * first, 2 * block))
            else:
                de, do = pairs(nodes(d_ref, node_at + 2 * first, 2 * block))
            push = nodes(gl_ref, pair_at + first, block) * de
            side = do + nodes(gr_ref, pair_at + first, block) * de + shifted_up(push, carry)
            carry = push[:1]
            put_nodes(q_ref, pair_at + first, nodes(r_ref, pair_at + first, block) * de)
            put_nodes(d_ref, L - 2 * half + first, side)
        pushed_out = pushed_out + carry
    return d_ref[pl.ds((L - 2) * NZ, NZ), :], pushed_out[0]


def substitute(before, last, gl_ref, gr_ref, q_ref, v_ref, store):
    v_ref[pl.ds((L - 2) * NZ, NZ), :] = last
    for count, half, node_at, pair_at in reversed(list(levels())):
        block = min(half, BLOCK)
        carry = before[None]
        for first in range(0, half, block):
            vo = nodes(v_ref, L - 2 * half + first, block)
            ve = (
                nodes(gl_ref, pair_at + first, block) * shifted_down(vo, carry)
                + nodes(gr_ref, pair_at + first, block) * vo
                + nodes(q_ref, pair_at + first, block)
            )
            carry = vo[block - 1 :]
            joined = jnp.stack([ve, vo], axis=1).reshape(2 * block, NZ, L)
            if count == L:
                store(2 * first, joined)
            else:
                put_nodes(v_ref, node_at + 2 * first, joined)


def factor_chain(n, coefficients, chain_g, chain_r):
    flow = None
    for p in range(n):
        surplus = coefficients[p, NZ : 2 * NZ, :]
        if p < n - 1:
            surplus = surplus + coefficients[p + 1, 2 * NZ :, :]
        if flow is not None:
            surplus = surplus + flow
        if p < n - 1:
            weight = coefficients[p + 1, :NZ, :]
            inv = inverse(surplus + weight)
            share = weight * inv
            chain_g[p] = share
            flow = share * surplus
        else:
            inv = inverse(surplus)
        chain_r[p] = inv


def solve_chain(n, sides, chain_g, chain_r, chain_v):
    flow = None
    scaled = []
    for p in range(n):
        side = sides[p, :NZ, :]
        if p < n - 1:
            side = side + sides[p + 1, NZ:, :]
        if flow is not None:
            side = side + flow
        if p < n - 1:
            flow = chain_g[p] * side
        scaled.append(side * chain_r[p])
    value = scaled[n - 1]
    chain_v[0] = jnp.zeros((NZ, L), jnp.float32)
    chain_v[n] = value
    for p in reversed(range(n - 1)):
        value = scaled[p] + chain_g[p] * value
        chain_v[p + 1] = value


class Gather:
    def __init__(self, axis, n, buffer, send, recv):
        self.axis, self.n, self.buffer, self.send, self.recv = axis, n, buffer, send, recv
        self.me = lax.axis_index(axis)

    def copy(self, step, slot):
        return pltpu.make_async_remote_copy(
            src_ref=self.buffer.at[slot],
            dst_ref=self.buffer.at[slot],
            send_sem=self.send.at[step - 1],
            recv_sem=self.recv.at[step - 1],
            device_id={self.axis: lax.rem(self.me + step, self.n)},
            device_id_type=MESH,
        )

    def start(self):
        for step in range(1, self.n):
            self.copy(step, self.me).start()

    def wait(self):
        for step in range(1, self.n):
            self.copy(step, lax.rem(self.me + self.n - step, self.n)).wait_recv()

    def finish(self):
        for step in range(1, self.n):
            self.copy(step, self.me).wait_send()


class Halo:
    def __init__(self, axis, n, edges, halo, send, recv):
        self.axis, self.n, self.edges, self.halo, self.send, self.recv = axis, n, edges, halo, send, recv
        self.me = lax.axis_index(axis)

    def copy(self, side):
        to = self.me - 1 if side == 0 else self.me + 1
        return pltpu.make_async_remote_copy(
            src_ref=self.edges.at[side],
            dst_ref=self.halo.at[1 - side],
            send_sem=self.send.at[side],
            recv_sem=self.recv.at[1 - side],
            device_id={self.axis: to},
            device_id_type=MESH,
        )

    def start(self):
        @pl.when(self.me > 0)
        def _():
            self.copy(0).start()

        @pl.when(self.me < self.n - 1)
        def _():
            self.copy(1).start()

    def wait(self):
        @pl.when(self.me > 0)
        def _():
            self.copy(1).wait_recv()

        @pl.when(self.me == 0)
        def _():
            self.halo[0] = jnp.zeros((2 * NZ, L), jnp.float32)

        @pl.when(self.me < self.n - 1)
        def _():
            self.copy(0).wait_recv()

        @pl.when(self.me == self.n - 1)
        def _():
            self.halo[1] = jnp.zeros((2 * NZ, L), jnp.float32)

    def finish(self):
        @pl.when(self.me > 0)
        def _():
            self.copy(0).wait_send()

        @pl.when(self.me < self.n - 1)
        def _():
            self.copy(1).wait_send()


def links(cond, field, cond_before, field_before):
    beside = shifted_down(cond, cond_before)
    weight = (2.0 * inplane_half) * cond * beside * inverse(cond + beside)
    return weight, weight * (field - shifted_down(field, field_before))


def kernel(
    n_row,
    n_col,
    mag_hbm,
    rate_hbm,
    field_hbm,
    region_hbm,
    source_hbm,
    out,
    mag,
    rate,
    field,
    region,
    source,
    cond,
    half_y,
    link_y,
    field_x,
    cond_x,
    side_x,
    extra_x,
    link_x,
    solved,
    gl_x,
    gr_x,
    r_x,
    gl_y,
    gr_y,
    r_y,
    work_a,
    work_b,
    work_c,
    work_d,
    edges_y,
    halo_y,
    edges_x,
    halo_x,
    coef_x,
    rhs_x,
    coef_y,
    rhs_y,
    chain_gx,
    chain_rx,
    chain_vx,
    chain_gy,
    chain_ry,
    chain_vy,
    par_sem,
    in_sem,
    hy_send,
    hy_recv,
    hx_send,
    hx_recv,
    cx_send,
    cx_recv,
    rx_send,
    rx_recv,
    cy_send,
    cy_recv,
    ry_send,
    ry_recv,
):
    my_row, my_col = lax.axis_index("row"), lax.axis_index("col")
    barrier = pltpu.get_barrier_semaphore()
    for step in range(1, n_row):
        pl.semaphore_signal(
            barrier, inc=1, device_id={"row": lax.rem(my_row + step, n_row)}, device_id_type=MESH
        )
    for step in range(1, n_col):
        pl.semaphore_signal(
            barrier, inc=1, device_id={"col": lax.rem(my_col + step, n_col)}, device_id_type=MESH
        )

    parameters = [
        pltpu.make_async_copy(mag_hbm, mag, par_sem.at[0]),
        pltpu.make_async_copy(rate_hbm, rate, par_sem.at[1]),
    ]
    for load in parameters:
        load.start()

    def layers(source_ref, target_ref, kind, z, count=2):
        rows = pl.ds(z * L, count * L)
        return pltpu.make_async_copy(source_ref.at[rows], target_ref.at[rows], in_sem.at[kind, z])

    loads = [
        (layers(field_hbm, field, 0, z), layers(region_hbm, region, 1, z)) for z in range(0, NZ, 2)
    ]
    source_load = layers(source_hbm, source, 2, 0, NZ)
    for field_load, region_load in loads:
        field_load.start()
        region_load.start()
    source_load.start()

    share_y = Halo("row", n_row, edges_y, halo_y, hy_send, hy_recv)
    share_x = Halo("col", n_col, edges_x, halo_x, hx_send, hx_recv)
    gather_cx = Gather("col", n_col, coef_x, cx_send, cx_recv)
    gather_rx = Gather("col", n_col, rhs_x, rx_send, rx_recv)
    gather_cy = Gather("row", n_row, coef_y, cy_send, cy_recv)
    gather_ry = Gather("row", n_row, rhs_y, ry_send, ry_recv)

    for load in parameters:
        load.wait()
    m0, m1, m2 = mag[0], mag[1], mag[2]
    k0, k1, k2 = rate[0], rate[1], rate[2]

    def conductivity(kelvin, kind):
        first, second = kind == 0, kind == 1
        scale = jnp.where(first, m0, jnp.where(second, m1, m2))
        soft = jnp.where(first, k0, jnp.where(second, k1, k2))
        return scale * jnp.exp(-soft * kelvin)

    for z in range(NZ):
        rows = pl.ds(z * L, L)
        if z % 2 == 0:
            for load in loads[z // 2]:
                load.wait()
        cond[rows, :] = conductivity(field[rows, :], region[rows, :])
    for side, y in ((0, 0), (1, L - 1)):
        edges_y[side, :NZ, :] = field[pl.ds(y, NZ, stride=L), :]
        edges_y[side, NZ:, :] = cond[pl.ds(y, NZ, stride=L), :]
    pl.semaphore_wait(barrier, n_row + n_col - 2)
    share_y.start()

    for z in range(NZ):
        rows = pl.ds(z * L, L)
        field_x[pl.ds(z, L, stride=NZ), :] = field[rows, :].T
        cond_x[pl.ds(z, L, stride=NZ), :] = cond[rows, :].T
    for side, x in ((0, 0), (1, L - 1)):
        edges_x[side, :NZ, :] = field_x[pl.ds(x * NZ, NZ), :]
        edges_x[side, NZ:, :] = cond_x[pl.ds(x * NZ, NZ), :]
    share_x.start()

    share_y.wait()
    t_before, c_before = halo_y[0, :NZ, :][None], halo_y[0, NZ:, :][None]
    flux_before = None
    for first in range(0, L + 1, BLOCK):
        if first < L:
            t = jnp.stack([field[pl.ds(first + i, NZ, stride=L), :] for i in range(BLOCK)])
            c = jnp.stack([cond[pl.ds(first + i, NZ, stride=L), :] for i in range(BLOCK)])
        else:
            t, c = halo_y[1, :NZ, :][None], halo_y[1, NZ:, :][None]
        weight, flux = links(c, t, c_before, t_before)
        if first < L:
            put_nodes(link_y, first, weight)
            put_nodes(half_y, first, shifted_up(flux, flux[-1:]) - flux)
        if flux_before is not None:
            half_y[pl.ds((first - 1) * NZ, NZ), :] = flux[0] - flux_before
        t_before, c_before, flux_before = t[-1:], c[-1:], flux[-1]

    share_x.wait()
    t_before, c_before = halo_x[0, :NZ, :][None], halo_x[0, NZ:, :][None]
    flux_before = None
    for first in range(0, L + 1, BLOCK):
        if first < L:
            t, c = nodes(field_x, first, BLOCK), nodes(cond_x, first, BLOCK)
        else:
            t, c = halo_x[1, :NZ, :][None], halo_x[1, NZ:, :][None]
        weight, flux = links(c, t, c_before, t_before)
        if first < L:
            put_nodes(link_x, first, weight)
            extra = shifted_up(flux, jnp.zeros((1, NZ, L), jnp.float32)) - flux
            put_nodes(extra_x, first, extra)
        if first > 0:
            at = pl.ds((first - 1) * NZ, NZ)
            extra_x[at, :] = extra_x[at, :] + flux[0]
        t_before, c_before = t[-1:], c[-1:]
    w, s, push = eliminate_coefficients(link_x, gl_x, gr_x, r_x, work_a, work_b)
    coef_x[my_col, :NZ, :] = w
    coef_x[my_col, NZ : 2 * NZ, :] = s
    coef_x[my_col, 2 * NZ :, :] = push
    gather_cx.start()
    source_load.wait()
    lower = None
    for z in range(NZ):
        rows = pl.ds(z * L, L)
        t, c = field[rows, :], cond[rows, :]
        if z == 0:
            lower = depth_ratio * c * t
        if z < NZ - 1:
            above = pl.ds((z + 1) * L, L)
            ta, ca = field[above, :], cond[above, :]
            upper = (2.0 * depth_ratio) * c * ca * inverse(c + ca) * (ta - t)
            along_z = upper - lower
            lower = upper
        else:
            along_z = -lower
        total = t + 2.0 * half_y[pl.ds(z, L, stride=NZ), :] + along_z + source[rows, :]
        side_x[pl.ds(z, L, stride=NZ), :] = total.T

    def side_of_x(first, count):
        return nodes(side_x, first, count) + nodes(extra_x, first, count)

    d, push = eliminate_right_side(side_of_x, gl_x, gr_x, r_x, work_a, work_b)
    rhs_x[my_col, :NZ, :] = d
    rhs_x[my_col, NZ:, :] = push
    gather_rx.start()

    w, s, push = eliminate_coefficients(link_y, gl_y, gr_y, r_y, work_c, work_d)
    coef_y[my_row, :NZ, :] = w
    coef_y[my_row, NZ : 2 * NZ, :] = s
    coef_y[my_row, 2 * NZ :, :] = push
    gather_cy.start()
    gather_cx.wait()
    factor_chain(n_col, coef_x, chain_gx, chain_rx)
    gather_rx.wait()
    solve_chain(n_col, rhs_x, chain_gx, chain_rx, chain_vx)

    def store_x(first, values):
        put_nodes(solved, first, values)

    substitute(chain_vx[my_col], chain_vx[my_col + 1], gl_x, gr_x, work_b, work_a, store_x)

    for z in range(NZ):
        at = pl.ds(z, L, stride=NZ)
        side_x[at, :] = solved[at, :].T - half_y[at, :]
    def side_of_y(first, count):
        return nodes(side_x, first, count)

    d, push = eliminate_right_side(side_of_y, gl_y, gr_y, r_y, work_a, work_b)
    rhs_y[my_row, :NZ, :] = d
    rhs_y[my_row, NZ:, :] = push
    gather_ry.start()
    gather_cy.wait()
    factor_chain(n_row, coef_y, chain_gy, chain_ry)
    gather_ry.wait()
    solve_chain(n_row, rhs_y, chain_gy, chain_ry, chain_vy)

    def store_y(first, values):
        for i in range(values.shape[0]):
            out[pl.ds(first + i, NZ, stride=L), :] = values[i]

    substitute(chain_vy[my_row], chain_vy[my_row + 1], gl_y, gr_y, work_b, work_a, store_y)
    for transfer in (share_y, share_x, gather_cx, gather_rx, gather_cy, gather_ry):
        transfer.finish()


def solution(mesh):
    n_row, n_col = mesh.shape["row"], mesh.shape["col"]

    def local(field, region, source, mag, rate):
        def flat(values):
            return values.reshape(NZ * L, L)

        whole = pltpu.VMEM((NZ * L, L), jnp.float32)
        integer = pltpu.VMEM((NZ * L, L), jnp.int32)

        parameter = pltpu.SMEM((3,), jnp.float32)

        def stack(count, height):
            return pltpu.VMEM((count, height * NZ, L), jnp.float32)

        def dma(count):
            return pltpu.SemaphoreType.DMA((count,))

        result = pl.pallas_call(
            functools.partial(kernel, n_row, n_col),
            out_shape=pltpu.VMEM((NZ * L, L), jnp.float32),
            in_specs=[pl.BlockSpec(memory_space=pltpu.HBM)] * 5,
            out_specs=pl.BlockSpec(memory_space=pltpu.VMEM),
            scratch_shapes=[parameter, parameter, whole, integer]
            + [whole] * 20
            + [stack(2, 2)] * 4
            + [stack(n_col, 3), stack(n_col, 2), stack(n_row, 3), stack(n_row, 2)]
            + [stack(n_col, 1), stack(n_col, 1), stack(n_col + 1, 1)]
            + [stack(n_row, 1), stack(n_row, 1), stack(n_row + 1, 1)]
            + [dma(2), pltpu.SemaphoreType.DMA((3, NZ))]
            + [dma(2)] * 4
            + [dma(n_col - 1)] * 4
            + [dma(n_row - 1)] * 4,
            compiler_params=pltpu.CompilerParams(
                collective_id=0, has_side_effects=True, vmem_limit_bytes=40 * 1024 * 1024
            ),
            cost_estimate=pl.CostEstimate(
                flops=20_000_000, bytes_accessed=2_200_000, transcendentals=400_000
            ),
        )(*[pltpu.with_memory_space_constraint(v, pltpu.HBM) for v in (mag, rate, flat(field), flat(region), flat(source))])
        return result.reshape(NZ, L, L)

    spec = P(None, "row", "col")
    return jax.shard_map(
        local, mesh=mesh, in_specs=(spec, spec, spec, P(), P()), out_specs=spec, check_vma=False
    )
```

```python
import functools

import jax
import jax.numpy as jnp
from jax import lax
from jax.experimental import pallas as pl
from jax.experimental.pallas import tpu as pltpu
from jax.sharding import PartitionSpec as P

MESH = pl.DeviceIdType.MESH
inplane_half = 500.0
depth_ratio = 0.08

NZ = 8
L = 128
PITCH = L + 8
BLOCK = 16


def inverse(value):
    guess = pl.reciprocal(value, approx=True)
    return guess * (2.0 - value * guess)


def pairs(values):
    split = values.reshape((values.shape[0] // 2, 2) + values.shape[1:])
    return split[:, 0], split[:, 1]


def shifted_up(values, last):
    if values.shape[0] == 1:
        return last
    return jnp.concatenate([values[1:], last], axis=0)


def shifted_down(values, first):
    if values.shape[0] == 1:
        return first
    return jnp.concatenate([first, values[:-1]], axis=0)


def nodes(ref, first, count):
    return ref[pl.ds(first * NZ, count * NZ), :].reshape(count, NZ, L)


def put_nodes(ref, first, values):
    count = values.shape[0]
    ref[pl.ds(first * NZ, count * NZ), :] = values.reshape(count * NZ, L)


def levels():
    count = L
    while count > 1:
        half = count // 2
        yield count, half, L - 2 * count, L - 2 * half
        count = half


def eliminate_coefficients(link_ref, gl_ref, gr_ref, r_ref, w_ref, s_ref):
    pushed_out = jnp.zeros((1, NZ, L), jnp.float32)
    for count, half, node_at, pair_at in levels():
        block = min(half, BLOCK)
        carry = jnp.zeros((1, NZ, L), jnp.float32)
        for first in reversed(range(0, half, block)):
            if count == L:
                wl, wr = pairs(nodes(link_ref, 2 * first, 2 * block))
                inv = inverse(1.0 + wl + wr)
                gl, gr = wl * inv, wr * inv
                push = gl
                surplus = 1.0 + gr + shifted_up(push, carry)
            else:
                wl, wr = pairs(nodes(w_ref, node_at + 2 * first, 2 * block))
                se, so = pairs(nodes(s_ref, node_at + 2 * first, 2 * block))
                inv = inverse(se + wl + wr)
                gl, gr = wl * inv, wr * inv
                push = gl * se
                surplus = so + gr * se + shifted_up(push, carry)
            carry = push[:1]
            put_nodes(gl_ref, pair_at + first, gl)
            put_nodes(gr_ref, pair_at + first, gr)
            put_nodes(r_ref, pair_at + first, inv)
            put_nodes(w_ref, L - 2 * half + first, gl * wr)
            put_nodes(s_ref, L - 2 * half + first, surplus)
        pushed_out = pushed_out + carry
    return w_ref[pl.ds((L - 2) * NZ, NZ), :], s_ref[pl.ds((L - 2) * NZ, NZ), :], pushed_out[0]


def eliminate_right_side(load_side, gl_ref, gr_ref, r_ref, d_ref, q_ref):
    pushed_out = jnp.zeros((1, NZ, L), jnp.float32)
    for count, half, node_at, pair_at in levels():
        block = min(half, BLOCK)
        carry = jnp.zeros((1, NZ, L), jnp.float32)
        for first in reversed(range(0, half, block)):
            if count == L:
                de, do = pairs(load_side(2 * first, 2 * block))
            else:
                de, do = pairs(nodes(d_ref, node_at + 2 * first, 2 * block))
            push = nodes(gl_ref, pair_at + first, block) * de
            side = do + nodes(gr_ref, pair_at + first, block) * de + shifted_up(push, carry)
            carry = push[:1]
            put_nodes(q_ref, pair_at + first, nodes(r_ref, pair_at + first, block) * de)
            put_nodes(d_ref, L - 2 * half + first, side)
        pushed_out = pushed_out + carry
    return d_ref[pl.ds((L - 2) * NZ, NZ), :], pushed_out[0]


def substitute(before, last, gl_ref, gr_ref, q_ref, v_ref, store):
    v_ref[pl.ds((L - 2) * NZ, NZ), :] = last
    for count, half, node_at, pair_at in reversed(list(levels())):
        block = min(half, BLOCK)
        carry = before[None]
        for first in range(0, half, block):
            vo = nodes(v_ref, L - 2 * half + first, block)
            ve = (
                nodes(gl_ref, pair_at + first, block) * shifted_down(vo, carry)
                + nodes(gr_ref, pair_at + first, block) * vo
                + nodes(q_ref, pair_at + first, block)
            )
            carry = vo[block - 1 :]
            joined = jnp.stack([ve, vo], axis=1).reshape(2 * block, NZ, L)
            if count == L:
                store(2 * first, joined)
            else:
                put_nodes(v_ref, node_at + 2 * first, joined)


def factor_chain(n, coefficients, chain_g, chain_r):
    flow = None
    for p in range(n):
        surplus = coefficients[p, NZ : 2 * NZ, :]
        if p < n - 1:
            surplus = surplus + coefficients[p + 1, 2 * NZ :, :]
        if flow is not None:
            surplus = surplus + flow
        if p < n - 1:
            weight = coefficients[p + 1, :NZ, :]
            inv = inverse(surplus + weight)
            share = weight * inv
            chain_g[p] = share
            flow = share * surplus
        else:
            inv = inverse(surplus)
        chain_r[p] = inv


def solve_chain(n, sides, chain_g, chain_r, chain_v):
    flow = None
    scaled = []
    for p in range(n):
        side = sides[p, :NZ, :]
        if p < n - 1:
            side = side + sides[p + 1, NZ:, :]
        if flow is not None:
            side = side + flow
        if p < n - 1:
            flow = chain_g[p] * side
        scaled.append(side * chain_r[p])
    value = scaled[n - 1]
    chain_v[0] = jnp.zeros((NZ, L), jnp.float32)
    chain_v[n] = value
    for p in reversed(range(n - 1)):
        value = scaled[p] + chain_g[p] * value
        chain_v[p + 1] = value


class Gather:
    def __init__(self, axis, n, buffer, send, recv):
        self.axis, self.n, self.buffer, self.send, self.recv = axis, n, buffer, send, recv
        self.me = lax.axis_index(axis)

    def copy(self, step, slot):
        return pltpu.make_async_remote_copy(
            src_ref=self.buffer.at[slot],
            dst_ref=self.buffer.at[slot],
            send_sem=self.send.at[step - 1],
            recv_sem=self.recv.at[step - 1],
            device_id={self.axis: lax.rem(self.me + step, self.n)},
            device_id_type=MESH,
        )

    def start(self):
        for step in range(1, self.n):
            self.copy(step, self.me).start()

    def wait(self):
        for step in range(1, self.n):
            self.copy(step, lax.rem(self.me + self.n - step, self.n)).wait_recv()

    def finish(self):
        for step in range(1, self.n):
            self.copy(step, self.me).wait_send()


class Halo:
    def __init__(self, axis, n, edges, halo, send, recv):
        self.axis, self.n, self.edges, self.halo, self.send, self.recv = axis, n, edges, halo, send, recv
        self.me = lax.axis_index(axis)

    def copy(self, side):
        to = self.me - 1 if side == 0 else self.me + 1
        return pltpu.make_async_remote_copy(
            src_ref=self.edges.at[side],
            dst_ref=self.halo.at[1 - side],
            send_sem=self.send.at[side],
            recv_sem=self.recv.at[1 - side],
            device_id={self.axis: to},
            device_id_type=MESH,
        )

    def start(self):
        @pl.when(self.me > 0)
        def _():
            self.copy(0).start()

        @pl.when(self.me < self.n - 1)
        def _():
            self.copy(1).start()

    def wait(self):
        @pl.when(self.me > 0)
        def _():
            self.copy(1).wait_recv()

        @pl.when(self.me == 0)
        def _():
            self.halo[0] = jnp.zeros((2 * NZ, L), jnp.float32)

        @pl.when(self.me < self.n - 1)
        def _():
            self.copy(0).wait_recv()

        @pl.when(self.me == self.n - 1)
        def _():
            self.halo[1] = jnp.zeros((2 * NZ, L), jnp.float32)

    def finish(self):
        @pl.when(self.me > 0)
        def _():
            self.copy(0).wait_send()

        @pl.when(self.me < self.n - 1)
        def _():
            self.copy(1).wait_send()


def links(cond, field, cond_before, field_before):
    beside = shifted_down(cond, cond_before)
    weight = (2.0 * inplane_half) * cond * beside * inverse(cond + beside)
    return weight, weight * (field - shifted_down(field, field_before))


def kernel(
    n_row,
    n_col,
    mag_hbm,
    rate_hbm,
    field_hbm,
    region_hbm,
    source_hbm,
    out,
    mag,
    rate,
    field,
    region,
    source,
    cond,
    wide,
    half_y,
    link_y,
    field_x,
    cond_x,
    side_x,
    extra_x,
    link_x,
    solved,
    gl_x,
    gr_x,
    r_x,
    gl_y,
    gr_y,
    r_y,
    work_a,
    work_b,
    work_c,
    work_d,
    edges_y,
    halo_y,
    edges_x,
    halo_x,
    coef_x,
    rhs_x,
    coef_y,
    rhs_y,
    chain_gx,
    chain_rx,
    chain_vx,
    chain_gy,
    chain_ry,
    chain_vy,
    par_sem,
    in_sem,
    hy_send,
    hy_recv,
    hx_send,
    hx_recv,
    cx_send,
    cx_recv,
    rx_send,
    rx_recv,
    cy_send,
    cy_recv,
    ry_send,
    ry_recv,
):
    my_row, my_col = lax.axis_index("row"), lax.axis_index("col")
    barrier = pltpu.get_barrier_semaphore()
    for step in range(1, n_row):
        pl.semaphore_signal(
            barrier, inc=1, device_id={"row": lax.rem(my_row + step, n_row)}, device_id_type=MESH
        )
    for step in range(1, n_col):
        pl.semaphore_signal(
            barrier, inc=1, device_id={"col": lax.rem(my_col + step, n_col)}, device_id_type=MESH
        )

    parameters = [
        pltpu.make_async_copy(mag_hbm, mag, par_sem.at[0]),
        pltpu.make_async_copy(rate_hbm, rate, par_sem.at[1]),
    ]
    for load in parameters:
        load.start()

    def layer(source_ref, target_ref, kind, z):
        return pltpu.make_async_copy(
            source_ref.at[pl.ds(z * L, L)], target_ref.at[pl.ds(z * PITCH, L)], in_sem.at[kind, z]
        )

    loads = [
        (layer(field_hbm, field, 0, z), layer(region_hbm, region, 1, z)) for z in range(NZ)
    ]
    source_loads = [layer(source_hbm, source, 2, z) for z in range(NZ)]
    for field_load, region_load in loads:
        field_load.start()
        region_load.start()
    for load in source_loads:
        load.start()

    share_y = Halo("row", n_row, edges_y, halo_y, hy_send, hy_recv)
    share_x = Halo("col", n_col, edges_x, halo_x, hx_send, hx_recv)
    gather_cx = Gather("col", n_col, coef_x, cx_send, cx_recv)
    gather_rx = Gather("col", n_col, rhs_x, rx_send, rx_recv)
    gather_cy = Gather("row", n_row, coef_y, cy_send, cy_recv)
    gather_ry = Gather("row", n_row, rhs_y, ry_send, ry_recv)

    for load in parameters:
        load.wait()
    m0, m1, m2 = mag[0], mag[1], mag[2]
    k0, k1, k2 = rate[0], rate[1], rate[2]

    def conductivity(kelvin, kind):
        first, second = kind == 0, kind == 1
        scale = jnp.where(first, m0, jnp.where(second, m1, m2))
        soft = jnp.where(first, k0, jnp.where(second, k1, k2))
        return scale * jnp.exp(-soft * kelvin)

    for z in range(NZ):
        rows = pl.ds(z * PITCH, L)
        for load in loads[z]:
            load.wait()
        cond[rows, :] = conductivity(field[rows, :], region[rows, :])
    for side, y in ((0, 0), (1, L - 1)):
        edges_y[side, :NZ, :] = field[pl.ds(y, NZ, stride=PITCH), :]
        edges_y[side, NZ:, :] = cond[pl.ds(y, NZ, stride=PITCH), :]
    pl.semaphore_wait(barrier, n_row + n_col - 2)
    share_y.start()

    for z in range(NZ):
        rows = pl.ds(z * PITCH, L)
        field_x[pl.ds(z, L, stride=NZ), :] = field[rows, :].T
        cond_x[pl.ds(z, L, stride=NZ), :] = cond[rows, :].T
    for side, x in ((0, 0), (1, L - 1)):
        edges_x[side, :NZ, :] = field_x[pl.ds(x * NZ, NZ), :]
        edges_x[side, NZ:, :] = cond_x[pl.ds(x * NZ, NZ), :]
    share_x.start()

    share_y.wait()
    t_before, c_before = halo_y[0, :NZ, :][None], halo_y[0, NZ:, :][None]
    flux_before = None
    for first in range(0, L + 1, BLOCK):
        if first < L:
            t = jnp.stack([field[pl.ds(first + i, NZ, stride=PITCH), :] for i in range(BLOCK)])
            c = jnp.stack([cond[pl.ds(first + i, NZ, stride=PITCH), :] for i in range(BLOCK)])
        else:
            t, c = halo_y[1, :NZ, :][None], halo_y[1, NZ:, :][None]
        weight, flux = links(c, t, c_before, t_before)
        if first < L:
            put_nodes(link_y, first, weight)
            put_nodes(half_y, first, shifted_up(flux, flux[-1:]) - flux)
        if flux_before is not None:
            half_y[pl.ds((first - 1) * NZ, NZ), :] = flux[0] - flux_before
        t_before, c_before, flux_before = t[-1:], c[-1:], flux[-1]

    share_x.wait()
    t_before, c_before = halo_x[0, :NZ, :][None], halo_x[0, NZ:, :][None]
    flux_before = None
    for first in range(0, L + 1, BLOCK):
        if first < L:
            t, c = nodes(field_x, first, BLOCK), nodes(cond_x, first, BLOCK)
        else:
            t, c = halo_x[1, :NZ, :][None], halo_x[1, NZ:, :][None]
        weight, flux = links(c, t, c_before, t_before)
        if first < L:
            put_nodes(link_x, first, weight)
            extra = shifted_up(flux, jnp.zeros((1, NZ, L), jnp.float32)) - flux
            put_nodes(extra_x, first, extra)
        if first > 0:
            at = pl.ds((first - 1) * NZ, NZ)
            extra_x[at, :] = extra_x[at, :] + flux[0]
        t_before, c_before = t[-1:], c[-1:]
    w, s, push = eliminate_coefficients(link_x, gl_x, gr_x, r_x, work_a, work_b)
    coef_x[my_col, :NZ, :] = w
    coef_x[my_col, NZ : 2 * NZ, :] = s
    coef_x[my_col, 2 * NZ :, :] = push
    gather_cx.start()
    for load in source_loads:
        load.wait()
    lower = None
    for z in range(NZ):
        rows = pl.ds(z * PITCH, L)
        t, c = field[rows, :], cond[rows, :]
        if z == 0:
            lower = depth_ratio * c * t
        if z < NZ - 1:
            above = pl.ds((z + 1) * PITCH, L)
            ta, ca = field[above, :], cond[above, :]
            upper = (2.0 * depth_ratio) * c * ca * inverse(c + ca) * (ta - t)
            along_z = upper - lower
            lower = upper
        else:
            along_z = -lower
        total = t + 2.0 * half_y[pl.ds(z, L, stride=NZ), :] + along_z + source[rows, :]
        side_x[pl.ds(z, L, stride=NZ), :] = total.T

    def side_of_x(first, count):
        return nodes(side_x, first, count) + nodes(extra_x, first, count)

    d, push = eliminate_right_side(side_of_x, gl_x, gr_x, r_x, work_a, work_b)
    rhs_x[my_col, :NZ, :] = d
    rhs_x[my_col, NZ:, :] = push
    gather_rx.start()

    w, s, push = eliminate_coefficients(link_y, gl_y, gr_y, r_y, work_c, work_d)
    coef_y[my_row, :NZ, :] = w
    coef_y[my_row, NZ : 2 * NZ, :] = s
    coef_y[my_row, 2 * NZ :, :] = push
    gather_cy.start()
    gather_cx.wait()
    factor_chain(n_col, coef_x, chain_gx, chain_rx)
    gather_rx.wait()
    solve_chain(n_col, rhs_x, chain_gx, chain_rx, chain_vx)

    def store_x(first, values):
        put_nodes(solved, first, values)

    substitute(chain_vx[my_col], chain_vx[my_col + 1], gl_x, gr_x, work_b, work_a, store_x)

    for z in range(NZ):
        at = pl.ds(z, L, stride=NZ)
        side_x[at, :] = solved[at, :].T - half_y[at, :]
    def side_of_y(first, count):
        return nodes(side_x, first, count)

    d, push = eliminate_right_side(side_of_y, gl_y, gr_y, r_y, work_a, work_b)
    rhs_y[my_row, :NZ, :] = d
    rhs_y[my_row, NZ:, :] = push
    gather_ry.start()
    gather_cy.wait()
    factor_chain(n_row, coef_y, chain_gy, chain_ry)
    gather_ry.wait()
    solve_chain(n_row, rhs_y, chain_gy, chain_ry, chain_vy)

    def store_y(first, values):
        for i in range(values.shape[0]):
            wide[pl.ds(first + i, NZ, stride=PITCH), :] = values[i]

    substitute(chain_vy[my_row], chain_vy[my_row + 1], gl_y, gr_y, work_b, work_a, store_y)
    for z in range(NZ):
        out[pl.ds(z * L, L), :] = wide[pl.ds(z * PITCH, L), :]
    for transfer in (share_y, share_x, gather_cx, gather_rx, gather_cy, gather_ry):
        transfer.finish()


def solution(mesh):
    n_row, n_col = mesh.shape["row"], mesh.shape["col"]

    def local(field, region, source, mag, rate):
        def flat(values):
            return values.reshape(NZ * L, L)

        whole = pltpu.VMEM((NZ * L, L), jnp.float32)
        pitched = pltpu.VMEM((NZ * PITCH, L), jnp.float32)
        integer = pltpu.VMEM((NZ * PITCH, L), jnp.int32)

        parameter = pltpu.SMEM((3,), jnp.float32)

        def stack(count, height):
            return pltpu.VMEM((count, height * NZ, L), jnp.float32)

        def dma(count):
            return pltpu.SemaphoreType.DMA((count,))

        result = pl.pallas_call(
            functools.partial(kernel, n_row, n_col),
            out_shape=pltpu.VMEM((NZ * L, L), jnp.float32),
            in_specs=[pl.BlockSpec(memory_space=pltpu.HBM)] * 5,
            out_specs=pl.BlockSpec(memory_space=pltpu.VMEM),
            scratch_shapes=[parameter, parameter, pitched, integer]
            + [pitched] * 3
            + [whole] * 18
            + [stack(2, 2)] * 4
            + [stack(n_col, 3), stack(n_col, 2), stack(n_row, 3), stack(n_row, 2)]
            + [stack(n_col, 1), stack(n_col, 1), stack(n_col + 1, 1)]
            + [stack(n_row, 1), stack(n_row, 1), stack(n_row + 1, 1)]
            + [dma(2), pltpu.SemaphoreType.DMA((3, NZ))]
            + [dma(2)] * 4
            + [dma(n_col - 1)] * 4
            + [dma(n_row - 1)] * 4,
            compiler_params=pltpu.CompilerParams(
                collective_id=0, has_side_effects=True, vmem_limit_bytes=40 * 1024 * 1024
            ),
            cost_estimate=pl.CostEstimate(
                flops=20_000_000, bytes_accessed=2_200_000, transcendentals=400_000
            ),
        )(*[pltpu.with_memory_space_constraint(v, pltpu.HBM) for v in (mag, rate, flat(field), flat(region), flat(source))])
        return result.reshape(NZ, L, L)

    spec = P(None, "row", "col")
    return jax.shard_map(
        local, mesh=mesh, in_specs=(spec, spec, spec, P(), P()), out_specs=spec, check_vma=False
    )
```

```python
import functools

import jax
import jax.numpy as jnp
from jax import lax
from jax.experimental import pallas as pl
from jax.experimental.pallas import tpu as pltpu
from jax.sharding import PartitionSpec as P

MESH = pl.DeviceIdType.MESH
inplane_half = 500.0
depth_ratio = 0.08

NZ = 8
L = 128
PITCH = L + 8
BLOCK = 16


def inverse(value):
    guess = pl.reciprocal(value, approx=True)
    return guess * (2.0 - value * guess)


def pairs(values):
    split = values.reshape((values.shape[0] // 2, 2) + values.shape[1:])
    return split[:, 0], split[:, 1]


def shifted_up(values, last):
    if values.shape[0] == 1:
        return last
    return jnp.concatenate([values[1:], last], axis=0)


def shifted_down(values, first):
    if values.shape[0] == 1:
        return first
    return jnp.concatenate([first, values[:-1]], axis=0)


def nodes(ref, first, count):
    return ref[pl.ds(first * NZ, count * NZ), :].reshape(count, NZ, L)


def put_nodes(ref, first, values):
    count = values.shape[0]
    ref[pl.ds(first * NZ, count * NZ), :] = values.reshape(count * NZ, L)


def levels():
    count = L
    while count > 1:
        half = count // 2
        yield count, half, L - 2 * count, L - 2 * half
        count = half


def eliminate_coefficients(link_ref, gl_ref, gr_ref, r_ref, w_ref, s_ref):
    pushed_out = jnp.zeros((1, NZ, L), jnp.float32)
    for count, half, node_at, pair_at in levels():
        block = min(half, BLOCK)
        carry = jnp.zeros((1, NZ, L), jnp.float32)
        for first in reversed(range(0, half, block)):
            if count == L:
                wl, wr = pairs(nodes(link_ref, 2 * first, 2 * block))
                inv = inverse(1.0 + wl + wr)
                gl, gr = wl * inv, wr * inv
                push = gl
                surplus = 1.0 + gr + shifted_up(push, carry)
            else:
                wl, wr = pairs(nodes(w_ref, node_at + 2 * first, 2 * block))
                se, so = pairs(nodes(s_ref, node_at + 2 * first, 2 * block))
                inv = inverse(se + wl + wr)
                gl, gr = wl * inv, wr * inv
                push = gl * se
                surplus = so + gr * se + shifted_up(push, carry)
            carry = push[:1]
            put_nodes(gl_ref, pair_at + first, gl)
            put_nodes(gr_ref, pair_at + first, gr)
            put_nodes(r_ref, pair_at + first, inv)
            put_nodes(w_ref, L - 2 * half + first, gl * wr)
            put_nodes(s_ref, L - 2 * half + first, surplus)
        pushed_out = pushed_out + carry
    return w_ref[pl.ds((L - 2) * NZ, NZ), :], s_ref[pl.ds((L - 2) * NZ, NZ), :], pushed_out[0]


def eliminate_right_side(load_side, gl_ref, gr_ref, r_ref, d_ref, q_ref):
    pushed_out = jnp.zeros((1, NZ, L), jnp.float32)
    for count, half, node_at, pair_at in levels():
        block = min(half, BLOCK)
        carry = jnp.zeros((1, NZ, L), jnp.float32)
        for first in reversed(range(0, half, block)):
            if count == L:
                de, do = pairs(load_side(2 * first, 2 * block))
            else:
                de, do = pairs(nodes(d_ref, node_at + 2 * first, 2 * block))
            push = nodes(gl_ref, pair_at + first, block) * de
            side = do + nodes(gr_ref, pair_at + first, block) * de + shifted_up(push, carry)
            carry = push[:1]
            put_nodes(q_ref, pair_at + first, nodes(r_ref, pair_at + first, block) * de)
            put_nodes(d_ref, L - 2 * half + first, side)
        pushed_out = pushed_out + carry
    return d_ref[pl.ds((L - 2) * NZ, NZ), :], pushed_out[0]


def substitute(before, last, gl_ref, gr_ref, q_ref, v_ref, store):
    v_ref[pl.ds((L - 2) * NZ, NZ), :] = last
    for count, half, node_at, pair_at in reversed(list(levels())):
        block = min(half, BLOCK)
        carry = before[None]
        for first in range(0, half, block):
            vo = nodes(v_ref, L - 2 * half + first, block)
            ve = (
                nodes(gl_ref, pair_at + first, block) * shifted_down(vo, carry)
                + nodes(gr_ref, pair_at + first, block) * vo
                + nodes(q_ref, pair_at + first, block)
            )
            carry = vo[block - 1 :]
            joined = jnp.stack([ve, vo], axis=1).reshape(2 * block, NZ, L)
            if count == L:
                store(2 * first, joined)
            else:
                put_nodes(v_ref, node_at + 2 * first, joined)


def factor_chain(n, coefficients, chain_g, chain_r):
    flow = None
    for p in range(n):
        surplus = coefficients[p, NZ : 2 * NZ, :]
        if p < n - 1:
            surplus = surplus + coefficients[p + 1, 2 * NZ :, :]
        if flow is not None:
            surplus = surplus + flow
        if p < n - 1:
            weight = coefficients[p + 1, :NZ, :]
            inv = inverse(surplus + weight)
            share = weight * inv
            chain_g[p] = share
            flow = share * surplus
        else:
            inv = inverse(surplus)
        chain_r[p] = inv


def solve_chain(n, sides, chain_g, chain_r, chain_v):
    flow = None
    scaled = []
    for p in range(n):
        side = sides[p, :NZ, :]
        if p < n - 1:
            side = side + sides[p + 1, NZ:, :]
        if flow is not None:
            side = side + flow
        if p < n - 1:
            flow = chain_g[p] * side
        scaled.append(side * chain_r[p])
    value = scaled[n - 1]
    chain_v[0] = jnp.zeros((NZ, L), jnp.float32)
    chain_v[n] = value
    for p in reversed(range(n - 1)):
        value = scaled[p] + chain_g[p] * value
        chain_v[p + 1] = value


class Gather:
    def __init__(self, axis, n, buffer, send, recv):
        self.axis, self.n, self.buffer, self.send, self.recv = axis, n, buffer, send, recv
        self.me = lax.axis_index(axis)

    def copy(self, step, slot):
        return pltpu.make_async_remote_copy(
            src_ref=self.buffer.at[slot],
            dst_ref=self.buffer.at[slot],
            send_sem=self.send.at[step - 1],
            recv_sem=self.recv.at[step - 1],
            device_id={self.axis: lax.rem(self.me + step, self.n)},
            device_id_type=MESH,
        )

    def start(self):
        for step in range(1, self.n):
            self.copy(step, self.me).start()

    def wait(self):
        for step in range(1, self.n):
            self.copy(step, lax.rem(self.me + self.n - step, self.n)).wait_recv()

    def finish(self):
        for step in range(1, self.n):
            self.copy(step, self.me).wait_send()


class Halo:
    def __init__(self, axis, n, edges, halo, send, recv):
        self.axis, self.n, self.edges, self.halo, self.send, self.recv = axis, n, edges, halo, send, recv
        self.me = lax.axis_index(axis)

    def copy(self, side):
        to = self.me - 1 if side == 0 else self.me + 1
        return pltpu.make_async_remote_copy(
            src_ref=self.edges.at[side],
            dst_ref=self.halo.at[1 - side],
            send_sem=self.send.at[side],
            recv_sem=self.recv.at[1 - side],
            device_id={self.axis: to},
            device_id_type=MESH,
        )

    def start(self):
        @pl.when(self.me > 0)
        def _():
            self.copy(0).start()

        @pl.when(self.me < self.n - 1)
        def _():
            self.copy(1).start()

    def wait(self):
        @pl.when(self.me > 0)
        def _():
            self.copy(1).wait_recv()

        @pl.when(self.me == 0)
        def _():
            self.halo[0] = jnp.zeros((2 * NZ, L), jnp.float32)

        @pl.when(self.me < self.n - 1)
        def _():
            self.copy(0).wait_recv()

        @pl.when(self.me == self.n - 1)
        def _():
            self.halo[1] = jnp.zeros((2 * NZ, L), jnp.float32)

    def finish(self):
        @pl.when(self.me > 0)
        def _():
            self.copy(0).wait_send()

        @pl.when(self.me < self.n - 1)
        def _():
            self.copy(1).wait_send()


def link_between(cond, field, cond_before, field_before):
    weight = (2.0 * inplane_half) * cond * cond_before * inverse(cond + cond_before)
    return weight, weight * (field - field_before)


def inner_links(field_rows, cond_rows, link_ref, sum_ref):
    flux_before = None
    for first in range(0, L, BLOCK):
        t, c = field_rows(first), cond_rows(first)
        if first == 0:
            t_before, c_before = t[:1], c[:1]
        weight, flux = link_between(
            c, t, shifted_down(c, c_before), shifted_down(t, t_before)
        )
        put_nodes(link_ref, first, weight)
        put_nodes(sum_ref, first, shifted_up(flux, jnp.zeros((1, NZ, L), jnp.float32)) - flux)
        if first > 0:
            at = pl.ds((first - 1) * NZ, NZ)
            sum_ref[at, :] = flux[0] - flux_before
        t_before, c_before, flux_before = t[-1:], c[-1:], flux[-1]


def edge_links(edges, halo, link_ref, sum_ref):
    weight, flux = link_between(
        edges[0, NZ:, :], edges[0, :NZ, :], halo[0, NZ:, :], halo[0, :NZ, :]
    )
    link_ref[pl.ds(0, NZ), :] = weight
    sum_ref[pl.ds(0, NZ), :] = sum_ref[pl.ds(0, NZ), :] - flux
    weight, flux = link_between(
        halo[1, NZ:, :], halo[1, :NZ, :], edges[1, NZ:, :], edges[1, :NZ, :]
    )
    at = pl.ds((L - 1) * NZ, NZ)
    sum_ref[at, :] = sum_ref[at, :] + flux


def kernel(
    n_row,
    n_col,
    mag_hbm,
    rate_hbm,
    field_hbm,
    region_hbm,
    source_hbm,
    out,
    mag,
    rate,
    field,
    region,
    source,
    cond,
    wide,
    half_y,
    link_y,
    field_x,
    cond_x,
    side_x,
    extra_x,
    link_x,
    solved,
    gl_x,
    gr_x,
    r_x,
    gl_y,
    gr_y,
    r_y,
    work_a,
    work_b,
    work_c,
    work_d,
    edges_y,
    halo_y,
    edges_x,
    halo_x,
    coef_x,
    rhs_x,
    coef_y,
    rhs_y,
    chain_gx,
    chain_rx,
    chain_vx,
    chain_gy,
    chain_ry,
    chain_vy,
    par_sem,
    in_sem,
    hy_send,
    hy_recv,
    hx_send,
    hx_recv,
    cx_send,
    cx_recv,
    rx_send,
    rx_recv,
    cy_send,
    cy_recv,
    ry_send,
    ry_recv,
):
    my_row, my_col = lax.axis_index("row"), lax.axis_index("col")
    barrier = pltpu.get_barrier_semaphore()
    for step in range(1, n_row):
        pl.semaphore_signal(
            barrier, inc=1, device_id={"row": lax.rem(my_row + step, n_row)}, device_id_type=MESH
        )
    for step in range(1, n_col):
        pl.semaphore_signal(
            barrier, inc=1, device_id={"col": lax.rem(my_col + step, n_col)}, device_id_type=MESH
        )

    parameters = [
        pltpu.make_async_copy(mag_hbm, mag, par_sem.at[0]),
        pltpu.make_async_copy(rate_hbm, rate, par_sem.at[1]),
    ]
    for load in parameters:
        load.start()

    def layer(source_ref, target_ref, kind, z):
        return pltpu.make_async_copy(
            source_ref.at[pl.ds(z * L, L)], target_ref.at[pl.ds(z * PITCH, L)], in_sem.at[kind, z]
        )

    loads = [
        (layer(field_hbm, field, 0, z), layer(region_hbm, region, 1, z)) for z in range(NZ)
    ]
    source_loads = [layer(source_hbm, source, 2, z) for z in range(NZ)]
    for field_load, region_load in loads:
        field_load.start()
        region_load.start()
    for load in source_loads:
        load.start()

    share_y = Halo("row", n_row, edges_y, halo_y, hy_send, hy_recv)
    share_x = Halo("col", n_col, edges_x, halo_x, hx_send, hx_recv)
    gather_cx = Gather("col", n_col, coef_x, cx_send, cx_recv)
    gather_rx = Gather("col", n_col, rhs_x, rx_send, rx_recv)
    gather_cy = Gather("row", n_row, coef_y, cy_send, cy_recv)
    gather_ry = Gather("row", n_row, rhs_y, ry_send, ry_recv)

    for load in parameters:
        load.wait()
    m0, m1, m2 = mag[0], mag[1], mag[2]
    k0, k1, k2 = rate[0], rate[1], rate[2]

    def conductivity(kelvin, kind):
        first, second = kind == 0, kind == 1
        scale = jnp.where(first, m0, jnp.where(second, m1, m2))
        soft = jnp.where(first, k0, jnp.where(second, k1, k2))
        return scale * jnp.exp(-soft * kelvin)

    for z in range(NZ):
        rows = pl.ds(z * PITCH, L)
        for load in loads[z]:
            load.wait()
        kelvin = field[rows, :]
        value = conductivity(kelvin, region[rows, :])
        cond[rows, :] = value
        field_x[pl.ds(z, L, stride=NZ), :] = kelvin.T
        cond_x[pl.ds(z, L, stride=NZ), :] = value.T
    for side, at in ((0, 0), (1, L - 1)):
        edges_y[side, :NZ, :] = field[pl.ds(at, NZ, stride=PITCH), :]
        edges_y[side, NZ:, :] = cond[pl.ds(at, NZ, stride=PITCH), :]
        edges_x[side, :NZ, :] = field_x[pl.ds(at * NZ, NZ), :]
        edges_x[side, NZ:, :] = cond_x[pl.ds(at * NZ, NZ), :]
    pl.semaphore_wait(barrier, n_row + n_col - 2)
    share_x.start()
    share_y.start()

    def y_rows(ref, first):
        return jnp.stack([ref[pl.ds(first + i, NZ, stride=PITCH), :] for i in range(BLOCK)])

    def x_rows(ref, first):
        return nodes(ref, first, BLOCK)

    inner_links(functools.partial(y_rows, field), functools.partial(y_rows, cond), link_y, half_y)
    inner_links(
        functools.partial(x_rows, field_x), functools.partial(x_rows, cond_x), link_x, extra_x
    )
    for load in source_loads:
        load.wait()
    lower = None
    for z in range(NZ):
        rows = pl.ds(z * PITCH, L)
        t, c = field[rows, :], cond[rows, :]
        if z == 0:
            lower = depth_ratio * c * t
        if z < NZ - 1:
            above = pl.ds((z + 1) * PITCH, L)
            ta, ca = field[above, :], cond[above, :]
            upper = (2.0 * depth_ratio) * c * ca * inverse(c + ca) * (ta - t)
            along_z = upper - lower
            lower = upper
        else:
            along_z = -lower
        source[rows, :] = t + along_z + source[rows, :]

    share_x.wait()
    edge_links(edges_x, halo_x, link_x, extra_x)
    w, s, push = eliminate_coefficients(link_x, gl_x, gr_x, r_x, work_a, work_b)
    coef_x[my_col, :NZ, :] = w
    coef_x[my_col, NZ : 2 * NZ, :] = s
    coef_x[my_col, 2 * NZ :, :] = push
    gather_cx.start()

    share_y.wait()
    edge_links(edges_y, halo_y, link_y, half_y)
    for z in range(NZ):
        total = source[pl.ds(z * PITCH, L), :] + 2.0 * half_y[pl.ds(z, L, stride=NZ), :]
        side_x[pl.ds(z, L, stride=NZ), :] = total.T

    def side_of_x(first, count):
        return nodes(side_x, first, count) + nodes(extra_x, first, count)

    d, push = eliminate_right_side(side_of_x, gl_x, gr_x, r_x, work_a, work_b)
    rhs_x[my_col, :NZ, :] = d
    rhs_x[my_col, NZ:, :] = push
    gather_rx.start()

    w, s, push = eliminate_coefficients(link_y, gl_y, gr_y, r_y, work_c, work_d)
    coef_y[my_row, :NZ, :] = w
    coef_y[my_row, NZ : 2 * NZ, :] = s
    coef_y[my_row, 2 * NZ :, :] = push
    gather_cy.start()
    gather_cx.wait()
    factor_chain(n_col, coef_x, chain_gx, chain_rx)
    gather_rx.wait()
    solve_chain(n_col, rhs_x, chain_gx, chain_rx, chain_vx)

    def store_x(first, values):
        put_nodes(solved, first, values)

    substitute(chain_vx[my_col], chain_vx[my_col + 1], gl_x, gr_x, work_b, work_a, store_x)

    for z in range(NZ):
        at = pl.ds(z, L, stride=NZ)
        side_x[at, :] = solved[at, :].T - half_y[at, :]
    def side_of_y(first, count):
        return nodes(side_x, first, count)

    d, push = eliminate_right_side(side_of_y, gl_y, gr_y, r_y, work_a, work_b)
    rhs_y[my_row, :NZ, :] = d
    rhs_y[my_row, NZ:, :] = push
    gather_ry.start()
    gather_cy.wait()
    factor_chain(n_row, coef_y, chain_gy, chain_ry)
    gather_ry.wait()
    solve_chain(n_row, rhs_y, chain_gy, chain_ry, chain_vy)

    def store_y(first, values):
        for i in range(values.shape[0]):
            wide[pl.ds(first + i, NZ, stride=PITCH), :] = values[i]

    substitute(chain_vy[my_row], chain_vy[my_row + 1], gl_y, gr_y, work_b, work_a, store_y)
    for z in range(NZ):
        out[pl.ds(z * L, L), :] = wide[pl.ds(z * PITCH, L), :]
    for transfer in (share_y, share_x, gather_cx, gather_rx, gather_cy, gather_ry):
        transfer.finish()


def solution(mesh):
    n_row, n_col = mesh.shape["row"], mesh.shape["col"]

    def local(field, region, source, mag, rate):
        def flat(values):
            return values.reshape(NZ * L, L)

        whole = pltpu.VMEM((NZ * L, L), jnp.float32)
        pitched = pltpu.VMEM((NZ * PITCH, L), jnp.float32)
        integer = pltpu.VMEM((NZ * PITCH, L), jnp.int32)

        parameter = pltpu.SMEM((3,), jnp.float32)

        def stack(count, height):
            return pltpu.VMEM((count, height * NZ, L), jnp.float32)

        def dma(count):
            return pltpu.SemaphoreType.DMA((count,))

        result = pl.pallas_call(
            functools.partial(kernel, n_row, n_col),
            out_shape=pltpu.VMEM((NZ * L, L), jnp.float32),
            in_specs=[pl.BlockSpec(memory_space=pltpu.HBM)] * 5,
            out_specs=pl.BlockSpec(memory_space=pltpu.VMEM),
            scratch_shapes=[parameter, parameter, pitched, integer]
            + [pitched] * 3
            + [whole] * 18
            + [stack(2, 2)] * 4
            + [stack(n_col, 3), stack(n_col, 2), stack(n_row, 3), stack(n_row, 2)]
            + [stack(n_col, 1), stack(n_col, 1), stack(n_col + 1, 1)]
            + [stack(n_row, 1), stack(n_row, 1), stack(n_row + 1, 1)]
            + [dma(2), pltpu.SemaphoreType.DMA((3, NZ))]
            + [dma(2)] * 4
            + [dma(n_col - 1)] * 4
            + [dma(n_row - 1)] * 4,
            compiler_params=pltpu.CompilerParams(
                collective_id=0, has_side_effects=True, vmem_limit_bytes=40 * 1024 * 1024
            ),
            cost_estimate=pl.CostEstimate(
                flops=20_000_000, bytes_accessed=2_200_000, transcendentals=400_000
            ),
        )(*[pltpu.with_memory_space_constraint(v, pltpu.HBM) for v in (mag, rate, flat(field), flat(region), flat(source))])
        return result.reshape(NZ, L, L)

    spec = P(None, "row", "col")
    return jax.shard_map(
        local, mesh=mesh, in_specs=(spec, spec, spec, P(), P()), out_specs=spec, check_vma=False
    )
```

```python
import functools

import jax
import jax.numpy as jnp
from jax import lax
from jax.experimental import pallas as pl
from jax.experimental.pallas import tpu as pltpu
from jax.sharding import PartitionSpec as P

MESH = pl.DeviceIdType.MESH
inplane_half = 500.0
depth_ratio = 0.08

NZ = 8
L = 128
PITCH = L + 8
BLOCK = 16


def inverse(value):
    guess = pl.reciprocal(value, approx=True)
    return guess * (2.0 - value * guess)


def pairs(values):
    split = values.reshape((values.shape[0] // 2, 2) + values.shape[1:])
    return split[:, 0], split[:, 1]


def shifted_up(values, last):
    if values.shape[0] == 1:
        return last
    return jnp.concatenate([values[1:], last], axis=0)


def shifted_down(values, first):
    if values.shape[0] == 1:
        return first
    return jnp.concatenate([first, values[:-1]], axis=0)


def nodes(ref, first, count):
    return ref[pl.ds(first * NZ, count * NZ), :].reshape(count, NZ, L)


def put_nodes(ref, first, values):
    count = values.shape[0]
    ref[pl.ds(first * NZ, count * NZ), :] = values.reshape(count * NZ, L)


def levels():
    count = L
    while count > 1:
        half = count // 2
        yield count, half, L - 2 * count, L - 2 * half
        count = half


def eliminate_coefficients(link_ref, gl_ref, gr_ref, r_ref, w_ref, s_ref):
    pushed_out = jnp.zeros((1, NZ, L), jnp.float32)
    for count, half, node_at, pair_at in levels():
        block = min(half, BLOCK)
        carry = jnp.zeros((1, NZ, L), jnp.float32)
        for first in reversed(range(0, half, block)):
            if count == L:
                wl, wr = pairs(nodes(link_ref, 2 * first, 2 * block))
                inv = inverse(1.0 + wl + wr)
                gl, gr = wl * inv, wr * inv
                push = gl
                surplus = 1.0 + gr + shifted_up(push, carry)
            else:
                wl, wr = pairs(nodes(w_ref, node_at + 2 * first, 2 * block))
                se, so = pairs(nodes(s_ref, node_at + 2 * first, 2 * block))
                inv = inverse(se + wl + wr)
                gl, gr = wl * inv, wr * inv
                push = gl * se
                surplus = so + gr * se + shifted_up(push, carry)
            carry = push[:1]
            put_nodes(gl_ref, pair_at + first, gl)
            put_nodes(gr_ref, pair_at + first, gr)
            put_nodes(r_ref, pair_at + first, inv)
            put_nodes(w_ref, L - 2 * half + first, gl * wr)
            put_nodes(s_ref, L - 2 * half + first, surplus)
        pushed_out = pushed_out + carry
    return w_ref[pl.ds((L - 2) * NZ, NZ), :], s_ref[pl.ds((L - 2) * NZ, NZ), :], pushed_out[0]


def eliminate_right_side(load_side, gl_ref, gr_ref, r_ref, d_ref, q_ref):
    pushed_out = jnp.zeros((1, NZ, L), jnp.float32)
    for count, half, node_at, pair_at in levels():
        block = min(half, BLOCK)
        carry = jnp.zeros((1, NZ, L), jnp.float32)
        for first in reversed(range(0, half, block)):
            if count == L:
                de, do = pairs(load_side(2 * first, 2 * block))
            else:
                de, do = pairs(nodes(d_ref, node_at + 2 * first, 2 * block))
            push = nodes(gl_ref, pair_at + first, block) * de
            side = do + nodes(gr_ref, pair_at + first, block) * de + shifted_up(push, carry)
            carry = push[:1]
            put_nodes(q_ref, pair_at + first, nodes(r_ref, pair_at + first, block) * de)
            put_nodes(d_ref, L - 2 * half + first, side)
        pushed_out = pushed_out + carry
    return d_ref[pl.ds((L - 2) * NZ, NZ), :], pushed_out[0]


def substitute(before, last, gl_ref, gr_ref, q_ref, v_ref, store):
    v_ref[pl.ds((L - 2) * NZ, NZ), :] = last
    for count, half, node_at, pair_at in reversed(list(levels())):
        block = min(half, BLOCK)
        carry = before[None]
        for first in range(0, half, block):
            vo = nodes(v_ref, L - 2 * half + first, block)
            ve = (
                nodes(gl_ref, pair_at + first, block) * shifted_down(vo, carry)
                + nodes(gr_ref, pair_at + first, block) * vo
                + nodes(q_ref, pair_at + first, block)
            )
            carry = vo[block - 1 :]
            joined = jnp.stack([ve, vo], axis=1).reshape(2 * block, NZ, L)
            if count == L:
                store(2 * first, joined)
            else:
                put_nodes(v_ref, node_at + 2 * first, joined)


def factor_chain(n, coefficients, chain_g, chain_r):
    flow = None
    for p in range(n):
        surplus = coefficients[p, NZ : 2 * NZ, :]
        if p < n - 1:
            surplus = surplus + coefficients[p + 1, 2 * NZ :, :]
        if flow is not None:
            surplus = surplus + flow
        if p < n - 1:
            weight = coefficients[p + 1, :NZ, :]
            inv = inverse(surplus + weight)
            share = weight * inv
            chain_g[p] = share
            flow = share * surplus
        else:
            inv = inverse(surplus)
        chain_r[p] = inv


def solve_chain(n, sides, chain_g, chain_r, chain_v):
    flow = None
    scaled = []
    for p in range(n):
        side = sides[p, :NZ, :]
        if p < n - 1:
            side = side + sides[p + 1, NZ:, :]
        if flow is not None:
            side = side + flow
        if p < n - 1:
            flow = chain_g[p] * side
        scaled.append(side * chain_r[p])
    value = scaled[n - 1]
    chain_v[0] = jnp.zeros((NZ, L), jnp.float32)
    chain_v[n] = value
    for p in reversed(range(n - 1)):
        value = scaled[p] + chain_g[p] * value
        chain_v[p + 1] = value


class Gather:
    def __init__(self, axis, n, buffer, send, recv):
        self.axis, self.n, self.buffer, self.send, self.recv = axis, n, buffer, send, recv
        self.me = lax.axis_index(axis)

    def copy(self, step, slot):
        return pltpu.make_async_remote_copy(
            src_ref=self.buffer.at[slot],
            dst_ref=self.buffer.at[slot],
            send_sem=self.send.at[step - 1],
            recv_sem=self.recv.at[step - 1],
            device_id={self.axis: lax.rem(self.me + step, self.n)},
            device_id_type=MESH,
        )

    def start(self):
        for step in range(1, self.n):
            self.copy(step, self.me).start()

    def wait(self):
        for step in range(1, self.n):
            self.copy(step, lax.rem(self.me + self.n - step, self.n)).wait_recv()

    def finish(self):
        for step in range(1, self.n):
            self.copy(step, self.me).wait_send()


class Halo:
    def __init__(self, axis, n, edges, halo, send, recv):
        self.axis, self.n, self.edges, self.halo, self.send, self.recv = axis, n, edges, halo, send, recv
        self.me = lax.axis_index(axis)

    def copy(self, side):
        to = self.me - 1 if side == 0 else self.me + 1
        return pltpu.make_async_remote_copy(
            src_ref=self.edges.at[side],
            dst_ref=self.halo.at[1 - side],
            send_sem=self.send.at[side],
            recv_sem=self.recv.at[1 - side],
            device_id={self.axis: to},
            device_id_type=MESH,
        )

    def start(self):
        @pl.when(self.me > 0)
        def _():
            self.copy(0).start()

        @pl.when(self.me < self.n - 1)
        def _():
            self.copy(1).start()

    def wait(self):
        @pl.when(self.me > 0)
        def _():
            self.copy(1).wait_recv()

        @pl.when(self.me == 0)
        def _():
            self.halo[0] = jnp.zeros((2 * NZ, L), jnp.float32)

        @pl.when(self.me < self.n - 1)
        def _():
            self.copy(0).wait_recv()

        @pl.when(self.me == self.n - 1)
        def _():
            self.halo[1] = jnp.zeros((2 * NZ, L), jnp.float32)

    def finish(self):
        @pl.when(self.me > 0)
        def _():
            self.copy(0).wait_send()

        @pl.when(self.me < self.n - 1)
        def _():
            self.copy(1).wait_send()


def link_between(cond, field, cond_before, field_before):
    weight = (2.0 * inplane_half) * cond * cond_before * inverse(cond + cond_before)
    return weight, weight * (field - field_before)


def inner_links(field_rows, cond_rows, link_ref, sum_ref):
    flux_before = None
    for first in range(0, L, BLOCK):
        t, c = field_rows(first), cond_rows(first)
        if first == 0:
            t_before, c_before = t[:1], c[:1]
        weight, flux = link_between(
            c, t, shifted_down(c, c_before), shifted_down(t, t_before)
        )
        put_nodes(link_ref, first, weight)
        put_nodes(sum_ref, first, shifted_up(flux, jnp.zeros((1, NZ, L), jnp.float32)) - flux)
        if first > 0:
            at = pl.ds((first - 1) * NZ, NZ)
            sum_ref[at, :] = flux[0] - flux_before
        t_before, c_before, flux_before = t[-1:], c[-1:], flux[-1]


def edge_links(edges, halo, link_ref, sum_ref):
    weight, flux = link_between(
        edges[0, NZ:, :], edges[0, :NZ, :], halo[0, NZ:, :], halo[0, :NZ, :]
    )
    link_ref[pl.ds(0, NZ), :] = weight
    sum_ref[pl.ds(0, NZ), :] = sum_ref[pl.ds(0, NZ), :] - flux
    weight, flux = link_between(
        halo[1, NZ:, :], halo[1, :NZ, :], edges[1, NZ:, :], edges[1, :NZ, :]
    )
    at = pl.ds((L - 1) * NZ, NZ)
    sum_ref[at, :] = sum_ref[at, :] + flux


def kernel(
    n_row,
    n_col,
    mag_hbm,
    rate_hbm,
    field_hbm,
    region_hbm,
    source_hbm,
    out,
    mag,
    rate,
    field,
    region,
    source,
    cond,
    wide,
    half_y,
    link_y,
    field_x,
    cond_x,
    side_x,
    extra_x,
    link_x,
    solved,
    gl_x,
    gr_x,
    r_x,
    gl_y,
    gr_y,
    r_y,
    work_a,
    work_b,
    work_c,
    work_d,
    edges_y,
    halo_y,
    edges_x,
    halo_x,
    coef_x,
    rhs_x,
    coef_y,
    rhs_y,
    chain_gx,
    chain_rx,
    chain_vx,
    chain_gy,
    chain_ry,
    chain_vy,
    par_sem,
    in_sem,
    hy_send,
    hy_recv,
    hx_send,
    hx_recv,
    cx_send,
    cx_recv,
    rx_send,
    rx_recv,
    cy_send,
    cy_recv,
    ry_send,
    ry_recv,
):
    my_row, my_col = lax.axis_index("row"), lax.axis_index("col")
    barrier = pltpu.get_barrier_semaphore()
    for step in range(1, n_row):
        pl.semaphore_signal(
            barrier, inc=1, device_id={"row": lax.rem(my_row + step, n_row)}, device_id_type=MESH
        )
    for step in range(1, n_col):
        pl.semaphore_signal(
            barrier, inc=1, device_id={"col": lax.rem(my_col + step, n_col)}, device_id_type=MESH
        )

    parameters = [
        pltpu.make_async_copy(mag_hbm, mag, par_sem.at[0]),
        pltpu.make_async_copy(rate_hbm, rate, par_sem.at[1]),
    ]
    for load in parameters:
        load.start()

    def layer(source_ref, target_ref, kind, z):
        return pltpu.make_async_copy(
            source_ref.at[pl.ds(z * L, L)], target_ref.at[pl.ds(z * PITCH, L)], in_sem.at[kind, z]
        )

    loads = [
        (layer(field_hbm, field, 0, z), layer(region_hbm, region, 1, z)) for z in range(NZ)
    ]
    source_loads = [layer(source_hbm, source, 2, z) for z in range(NZ)]
    for field_load, region_load in loads:
        field_load.start()
        region_load.start()
    for load in source_loads:
        load.start()

    share_y = Halo("row", n_row, edges_y, halo_y, hy_send, hy_recv)
    share_x = Halo("col", n_col, edges_x, halo_x, hx_send, hx_recv)
    gather_cx = Gather("col", n_col, coef_x, cx_send, cx_recv)
    gather_rx = Gather("col", n_col, rhs_x, rx_send, rx_recv)
    gather_cy = Gather("row", n_row, coef_y, cy_send, cy_recv)
    gather_ry = Gather("row", n_row, rhs_y, ry_send, ry_recv)

    for load in parameters:
        load.wait()
    for field_load, region_load in loads:
        field_load.wait()
        region_load.wait()
    m0, m1, m2 = mag[0], mag[1], mag[2]
    k0, k1, k2 = rate[0], rate[1], rate[2]

    def conductivity(kelvin, kind):
        first, second = kind == 0, kind == 1
        scale = jnp.where(first, m0, jnp.where(second, m1, m2))
        soft = jnp.where(first, k0, jnp.where(second, k1, k2))
        return scale * jnp.exp(-soft * kelvin)

    for z in range(NZ):
        rows = pl.ds(z * PITCH, L)
        kelvin = field[rows, :]
        value = conductivity(kelvin, region[rows, :])
        cond[rows, :] = value
        field_x[pl.ds(z, L, stride=NZ), :] = kelvin.T
        cond_x[pl.ds(z, L, stride=NZ), :] = value.T
    for side, at in ((0, 0), (1, L - 1)):
        edges_y[side, :NZ, :] = field[pl.ds(at, NZ, stride=PITCH), :]
        edges_y[side, NZ:, :] = cond[pl.ds(at, NZ, stride=PITCH), :]
        edges_x[side, :NZ, :] = field_x[pl.ds(at * NZ, NZ), :]
        edges_x[side, NZ:, :] = cond_x[pl.ds(at * NZ, NZ), :]
    pl.semaphore_wait(barrier, n_row + n_col - 2)
    share_x.start()
    share_y.start()

    def y_rows(ref, first):
        return jnp.stack([ref[pl.ds(first + i, NZ, stride=PITCH), :] for i in range(BLOCK)])

    def x_rows(ref, first):
        return nodes(ref, first, BLOCK)

    inner_links(functools.partial(y_rows, field), functools.partial(y_rows, cond), link_y, half_y)
    inner_links(
        functools.partial(x_rows, field_x), functools.partial(x_rows, cond_x), link_x, extra_x
    )
    for load in source_loads:
        load.wait()
    lower = None
    for z in range(NZ):
        rows = pl.ds(z * PITCH, L)
        t, c = field[rows, :], cond[rows, :]
        if z == 0:
            lower = depth_ratio * c * t
        if z < NZ - 1:
            above = pl.ds((z + 1) * PITCH, L)
            ta, ca = field[above, :], cond[above, :]
            upper = (2.0 * depth_ratio) * c * ca * inverse(c + ca) * (ta - t)
            along_z = upper - lower
            lower = upper
        else:
            along_z = -lower
        source[rows, :] = t + along_z + source[rows, :]

    share_x.wait()
    edge_links(edges_x, halo_x, link_x, extra_x)
    w, s, push = eliminate_coefficients(link_x, gl_x, gr_x, r_x, work_a, work_b)
    coef_x[my_col, :NZ, :] = w
    coef_x[my_col, NZ : 2 * NZ, :] = s
    coef_x[my_col, 2 * NZ :, :] = push
    gather_cx.start()

    share_y.wait()
    edge_links(edges_y, halo_y, link_y, half_y)
    for z in range(NZ):
        total = source[pl.ds(z * PITCH, L), :] + 2.0 * half_y[pl.ds(z, L, stride=NZ), :]
        side_x[pl.ds(z, L, stride=NZ), :] = total.T

    def side_of_x(first, count):
        return nodes(side_x, first, count) + nodes(extra_x, first, count)

    d, push = eliminate_right_side(side_of_x, gl_x, gr_x, r_x, work_a, work_b)
    rhs_x[my_col, :NZ, :] = d
    rhs_x[my_col, NZ:, :] = push
    gather_rx.start()

    w, s, push = eliminate_coefficients(link_y, gl_y, gr_y, r_y, work_c, work_d)
    coef_y[my_row, :NZ, :] = w
    coef_y[my_row, NZ : 2 * NZ, :] = s
    coef_y[my_row, 2 * NZ :, :] = push
    gather_cy.start()
    gather_cx.wait()
    factor_chain(n_col, coef_x, chain_gx, chain_rx)
    gather_rx.wait()
    solve_chain(n_col, rhs_x, chain_gx, chain_rx, chain_vx)

    def store_x(first, values):
        put_nodes(solved, first, values)

    substitute(chain_vx[my_col], chain_vx[my_col + 1], gl_x, gr_x, work_b, work_a, store_x)

    for z in range(NZ):
        at = pl.ds(z, L, stride=NZ)
        side_x[at, :] = solved[at, :].T - half_y[at, :]
    def side_of_y(first, count):
        return nodes(side_x, first, count)

    d, push = eliminate_right_side(side_of_y, gl_y, gr_y, r_y, work_a, work_b)
    rhs_y[my_row, :NZ, :] = d
    rhs_y[my_row, NZ:, :] = push
    gather_ry.start()
    gather_cy.wait()
    factor_chain(n_row, coef_y, chain_gy, chain_ry)
    gather_ry.wait()
    solve_chain(n_row, rhs_y, chain_gy, chain_ry, chain_vy)

    def store_y(first, values):
        for i in range(values.shape[0]):
            wide[pl.ds(first + i, NZ, stride=PITCH), :] = values[i]

    substitute(chain_vy[my_row], chain_vy[my_row + 1], gl_y, gr_y, work_b, work_a, store_y)
    for z in range(NZ):
        out[pl.ds(z * L, L), :] = wide[pl.ds(z * PITCH, L), :]
    for transfer in (share_y, share_x, gather_cx, gather_rx, gather_cy, gather_ry):
        transfer.finish()


def solution(mesh):
    n_row, n_col = mesh.shape["row"], mesh.shape["col"]

    def local(field, region, source, mag, rate):
        def flat(values):
            return values.reshape(NZ * L, L)

        whole = pltpu.VMEM((NZ * L, L), jnp.float32)
        pitched = pltpu.VMEM((NZ * PITCH, L), jnp.float32)
        integer = pltpu.VMEM((NZ * PITCH, L), jnp.int32)

        parameter = pltpu.SMEM((3,), jnp.float32)

        def stack(count, height):
            return pltpu.VMEM((count, height * NZ, L), jnp.float32)

        def dma(count):
            return pltpu.SemaphoreType.DMA((count,))

        result = pl.pallas_call(
            functools.partial(kernel, n_row, n_col),
            out_shape=pltpu.VMEM((NZ * L, L), jnp.float32),
            in_specs=[pl.BlockSpec(memory_space=pltpu.HBM)] * 5,
            out_specs=pl.BlockSpec(memory_space=pltpu.VMEM),
            scratch_shapes=[parameter, parameter, pitched, integer]
            + [pitched] * 3
            + [whole] * 18
            + [stack(2, 2)] * 4
            + [stack(n_col, 3), stack(n_col, 2), stack(n_row, 3), stack(n_row, 2)]
            + [stack(n_col, 1), stack(n_col, 1), stack(n_col + 1, 1)]
            + [stack(n_row, 1), stack(n_row, 1), stack(n_row + 1, 1)]
            + [dma(2), pltpu.SemaphoreType.DMA((3, NZ))]
            + [dma(2)] * 4
            + [dma(n_col - 1)] * 4
            + [dma(n_row - 1)] * 4,
            compiler_params=pltpu.CompilerParams(
                collective_id=0, has_side_effects=True, vmem_limit_bytes=40 * 1024 * 1024
            ),
            cost_estimate=pl.CostEstimate(
                flops=20_000_000, bytes_accessed=2_200_000, transcendentals=400_000
            ),
        )(*[pltpu.with_memory_space_constraint(v, pltpu.HBM) for v in (mag, rate, flat(field), flat(region), flat(source))])
        return result.reshape(NZ, L, L)

    spec = P(None, "row", "col")
    return jax.shard_map(
        local, mesh=mesh, in_specs=(spec, spec, spec, P(), P()), out_specs=spec, check_vma=False
    )
```

```python
import functools

import jax
import jax.numpy as jnp
from jax import lax
from jax.experimental import pallas as pl
from jax.experimental.pallas import tpu as pltpu
from jax.sharding import PartitionSpec as P

MESH = pl.DeviceIdType.MESH
inplane_half = 500.0
depth_ratio = 0.08

NZ = 8
L = 128
PITCH = L + 8
BLOCK = 16


def inverse(value):
    guess = pl.reciprocal(value, approx=True)
    return guess * (2.0 - value * guess)


def pairs(values):
    split = values.reshape((values.shape[0] // 2, 2) + values.shape[1:])
    return split[:, 0], split[:, 1]


def shifted_up(values, last):
    if values.shape[0] == 1:
        return last
    return jnp.concatenate([values[1:], last], axis=0)


def shifted_down(values, first):
    if values.shape[0] == 1:
        return first
    return jnp.concatenate([first, values[:-1]], axis=0)


def nodes(ref, first, count):
    return ref[pl.ds(first * NZ, count * NZ), :].reshape(count, NZ, L)


def put_nodes(ref, first, values):
    count = values.shape[0]
    ref[pl.ds(first * NZ, count * NZ), :] = values.reshape(count * NZ, L)


def levels():
    count = L
    while count > 1:
        half = count // 2
        yield count, half, L - 2 * count, L - 2 * half
        count = half


def eliminate_coefficients(link_ref, gl_ref, gr_ref, r_ref, w_ref, s_ref):
    pushed_out = jnp.zeros((1, NZ, L), jnp.float32)
    for count, half, node_at, pair_at in levels():
        block = min(half, BLOCK)
        carry = jnp.zeros((1, NZ, L), jnp.float32)
        for first in reversed(range(0, half, block)):
            if count == L:
                wl, wr = pairs(nodes(link_ref, 2 * first, 2 * block))
                inv = inverse(1.0 + wl + wr)
                gl, gr = wl * inv, wr * inv
                push = gl
                surplus = 1.0 + gr + shifted_up(push, carry)
            else:
                wl, wr = pairs(nodes(w_ref, node_at + 2 * first, 2 * block))
                se, so = pairs(nodes(s_ref, node_at + 2 * first, 2 * block))
                inv = inverse(se + wl + wr)
                gl, gr = wl * inv, wr * inv
                push = gl * se
                surplus = so + gr * se + shifted_up(push, carry)
            carry = push[:1]
            put_nodes(gl_ref, pair_at + first, gl)
            put_nodes(gr_ref, pair_at + first, gr)
            put_nodes(r_ref, pair_at + first, inv)
            put_nodes(w_ref, L - 2 * half + first, gl * wr)
            put_nodes(s_ref, L - 2 * half + first, surplus)
        pushed_out = pushed_out + carry
    return w_ref[pl.ds((L - 2) * NZ, NZ), :], s_ref[pl.ds((L - 2) * NZ, NZ), :], pushed_out[0]


def eliminate_right_side(load_side, gl_ref, gr_ref, r_ref, d_ref, q_ref):
    pushed_out = jnp.zeros((1, NZ, L), jnp.float32)
    for count, half, node_at, pair_at in levels():
        block = min(half, BLOCK)
        carry = jnp.zeros((1, NZ, L), jnp.float32)
        for first in reversed(range(0, half, block)):
            if count == L:
                de, do = pairs(load_side(2 * first, 2 * block))
            else:
                de, do = pairs(nodes(d_ref, node_at + 2 * first, 2 * block))
            push = nodes(gl_ref, pair_at + first, block) * de
            side = do + nodes(gr_ref, pair_at + first, block) * de + shifted_up(push, carry)
            carry = push[:1]
            put_nodes(q_ref, pair_at + first, nodes(r_ref, pair_at + first, block) * de)
            put_nodes(d_ref, L - 2 * half + first, side)
        pushed_out = pushed_out + carry
    return d_ref[pl.ds((L - 2) * NZ, NZ), :], pushed_out[0]


def substitute(before, last, gl_ref, gr_ref, q_ref, v_ref, store):
    v_ref[pl.ds((L - 2) * NZ, NZ), :] = last
    for count, half, node_at, pair_at in reversed(list(levels())):
        block = min(half, BLOCK)
        carry = before[None]
        for first in range(0, half, block):
            vo = nodes(v_ref, L - 2 * half + first, block)
            ve = (
                nodes(gl_ref, pair_at + first, block) * shifted_down(vo, carry)
                + nodes(gr_ref, pair_at + first, block) * vo
                + nodes(q_ref, pair_at + first, block)
            )
            carry = vo[block - 1 :]
            joined = jnp.stack([ve, vo], axis=1).reshape(2 * block, NZ, L)
            if count == L:
                store(2 * first, joined)
            else:
                put_nodes(v_ref, node_at + 2 * first, joined)


def factor_chain(n, coefficients, chain_g, chain_r):
    flow = None
    for p in range(n):
        surplus = coefficients[p, NZ : 2 * NZ, :]
        if p < n - 1:
            surplus = surplus + coefficients[p + 1, 2 * NZ :, :]
        if flow is not None:
            surplus = surplus + flow
        if p < n - 1:
            weight = coefficients[p + 1, :NZ, :]
            inv = inverse(surplus + weight)
            share = weight * inv
            chain_g[p] = share
            flow = share * surplus
        else:
            inv = inverse(surplus)
        chain_r[p] = inv


def solve_chain(n, sides, chain_g, chain_r, chain_v):
    flow = None
    scaled = []
    for p in range(n):
        side = sides[p, :NZ, :]
        if p < n - 1:
            side = side + sides[p + 1, NZ:, :]
        if flow is not None:
            side = side + flow
        if p < n - 1:
            flow = chain_g[p] * side
        scaled.append(side * chain_r[p])
    value = scaled[n - 1]
    chain_v[0] = jnp.zeros((NZ, L), jnp.float32)
    chain_v[n] = value
    for p in reversed(range(n - 1)):
        value = scaled[p] + chain_g[p] * value
        chain_v[p + 1] = value


class Gather:
    def __init__(self, axis, n, buffer, send, recv):
        self.axis, self.n, self.buffer, self.send, self.recv = axis, n, buffer, send, recv
        self.me = lax.axis_index(axis)

    def copy(self, step, slot):
        return pltpu.make_async_remote_copy(
            src_ref=self.buffer.at[slot],
            dst_ref=self.buffer.at[slot],
            send_sem=self.send.at[step - 1],
            recv_sem=self.recv.at[step - 1],
            device_id={self.axis: lax.rem(self.me + step, self.n)},
            device_id_type=MESH,
        )

    def start(self):
        for step in range(1, self.n):
            self.copy(step, self.me).start()

    def wait(self):
        for step in range(1, self.n):
            self.copy(step, lax.rem(self.me + self.n - step, self.n)).wait_recv()

    def finish(self):
        for step in range(1, self.n):
            self.copy(step, self.me).wait_send()


class PairedGather:
    def __init__(self, axis, n, buffer, send, recv):
        self.axis, self.n, self.buffer, self.send, self.recv = axis, n, buffer, send, recv
        self.me = lax.axis_index(axis)
        self.beside = self.me + 1 - 2 * lax.rem(self.me, 2)

    def copy(self, slot, to, at):
        return pltpu.make_async_remote_copy(
            src_ref=self.buffer.at[slot],
            dst_ref=self.buffer.at[slot],
            send_sem=self.send.at[at],
            recv_sem=self.recv.at[at],
            device_id={self.axis: to},
            device_id_type=MESH,
        )

    def out(self, step):
        return self.copy(self.me, lax.rem(self.me + step, self.n), step - 1)

    def relayed(self, step):
        return self.copy(lax.rem(self.me + self.n - step, self.n), self.beside, step)

    def start(self):
        for step in range(2, self.n, 2):
            self.out(step).start()
        self.copy(self.me, self.beside, 0).start()

    def relay(self):
        for step in range(2, self.n, 2):
            slot = lax.rem(self.me + self.n - step, self.n)
            self.copy(slot, self.beside, step - 1).wait_recv()
            self.relayed(step).start()

    def wait(self):
        self.copy(self.beside, self.beside, 0).wait_recv()
        for step in range(2, self.n, 2):
            slot = lax.rem(self.beside + self.n - step, self.n)
            self.copy(slot, self.beside, step).wait_recv()

    def finish(self):
        self.copy(self.me, self.beside, 0).wait_send()
        for step in range(2, self.n, 2):
            self.out(step).wait_send()
            self.relayed(step).wait_send()


class Halo:
    def __init__(self, axis, n, edges, halo, send, recv):
        self.axis, self.n, self.edges, self.halo, self.send, self.recv = axis, n, edges, halo, send, recv
        self.me = lax.axis_index(axis)

    def copy(self, side):
        to = self.me - 1 if side == 0 else self.me + 1
        return pltpu.make_async_remote_copy(
            src_ref=self.edges.at[side],
            dst_ref=self.halo.at[1 - side],
            send_sem=self.send.at[side],
            recv_sem=self.recv.at[1 - side],
            device_id={self.axis: to},
            device_id_type=MESH,
        )

    def start(self):
        @pl.when(self.me > 0)
        def _():
            self.copy(0).start()

        @pl.when(self.me < self.n - 1)
        def _():
            self.copy(1).start()

    def wait(self):
        @pl.when(self.me > 0)
        def _():
            self.copy(1).wait_recv()

        @pl.when(self.me == 0)
        def _():
            self.halo[0] = jnp.zeros((2 * NZ, L), jnp.float32)

        @pl.when(self.me < self.n - 1)
        def _():
            self.copy(0).wait_recv()

        @pl.when(self.me == self.n - 1)
        def _():
            self.halo[1] = jnp.zeros((2 * NZ, L), jnp.float32)

    def finish(self):
        @pl.when(self.me > 0)
        def _():
            self.copy(0).wait_send()

        @pl.when(self.me < self.n - 1)
        def _():
            self.copy(1).wait_send()


def link_between(cond, field, cond_before, field_before):
    weight = (2.0 * inplane_half) * cond * cond_before * inverse(cond + cond_before)
    return weight, weight * (field - field_before)


def inner_links(field_rows, cond_rows, link_ref, sum_ref):
    flux_before = None
    for first in range(0, L, BLOCK):
        t, c = field_rows(first), cond_rows(first)
        if first == 0:
            t_before, c_before = t[:1], c[:1]
        weight, flux = link_between(
            c, t, shifted_down(c, c_before), shifted_down(t, t_before)
        )
        put_nodes(link_ref, first, weight)
        put_nodes(sum_ref, first, shifted_up(flux, jnp.zeros((1, NZ, L), jnp.float32)) - flux)
        if first > 0:
            at = pl.ds((first - 1) * NZ, NZ)
            sum_ref[at, :] = flux[0] - flux_before
        t_before, c_before, flux_before = t[-1:], c[-1:], flux[-1]


def edge_links(edges, halo, link_ref, sum_ref):
    weight, flux = link_between(
        edges[0, NZ:, :], edges[0, :NZ, :], halo[0, NZ:, :], halo[0, :NZ, :]
    )
    link_ref[pl.ds(0, NZ), :] = weight
    sum_ref[pl.ds(0, NZ), :] = sum_ref[pl.ds(0, NZ), :] - flux
    weight, flux = link_between(
        halo[1, NZ:, :], halo[1, :NZ, :], edges[1, NZ:, :], edges[1, :NZ, :]
    )
    at = pl.ds((L - 1) * NZ, NZ)
    sum_ref[at, :] = sum_ref[at, :] + flux


def kernel(
    n_row,
    n_col,
    mag_hbm,
    rate_hbm,
    field_hbm,
    region_hbm,
    source_hbm,
    out,
    mag,
    rate,
    field,
    region,
    source,
    cond,
    wide,
    half_y,
    link_y,
    field_x,
    cond_x,
    side_x,
    extra_x,
    link_x,
    solved,
    gl_x,
    gr_x,
    r_x,
    gl_y,
    gr_y,
    r_y,
    work_a,
    work_b,
    work_c,
    work_d,
    edges_y,
    halo_y,
    edges_x,
    halo_x,
    coef_x,
    rhs_x,
    coef_y,
    rhs_y,
    chain_gx,
    chain_rx,
    chain_vx,
    chain_gy,
    chain_ry,
    chain_vy,
    par_sem,
    in_sem,
    hy_send,
    hy_recv,
    hx_send,
    hx_recv,
    cx_send,
    cx_recv,
    rx_send,
    rx_recv,
    cy_send,
    cy_recv,
    ry_send,
    ry_recv,
):
    my_row, my_col = lax.axis_index("row"), lax.axis_index("col")
    barrier = pltpu.get_barrier_semaphore()
    for step in range(1, n_row):
        pl.semaphore_signal(
            barrier, inc=1, device_id={"row": lax.rem(my_row + step, n_row)}, device_id_type=MESH
        )
    for step in range(1, n_col):
        pl.semaphore_signal(
            barrier, inc=1, device_id={"col": lax.rem(my_col + step, n_col)}, device_id_type=MESH
        )

    parameters = [
        pltpu.make_async_copy(mag_hbm, mag, par_sem.at[0]),
        pltpu.make_async_copy(rate_hbm, rate, par_sem.at[1]),
    ]
    for load in parameters:
        load.start()

    def layer(source_ref, target_ref, kind, z):
        return pltpu.make_async_copy(
            source_ref.at[pl.ds(z * L, L)], target_ref.at[pl.ds(z * PITCH, L)], in_sem.at[kind, z]
        )

    loads = [
        (layer(field_hbm, field, 0, z), layer(region_hbm, region, 1, z)) for z in range(NZ)
    ]
    source_loads = [layer(source_hbm, source, 2, z) for z in range(NZ)]
    for field_load, region_load in loads:
        field_load.start()
        region_load.start()
    for load in source_loads:
        load.start()

    share_y = Halo("row", n_row, edges_y, halo_y, hy_send, hy_recv)
    share_x = Halo("col", n_col, edges_x, halo_x, hx_send, hx_recv)
    gather_cx = PairedGather("col", n_col, coef_x, cx_send, cx_recv)
    gather_rx = PairedGather("col", n_col, rhs_x, rx_send, rx_recv)
    gather_cy = Gather("row", n_row, coef_y, cy_send, cy_recv)
    gather_ry = Gather("row", n_row, rhs_y, ry_send, ry_recv)

    for load in parameters:
        load.wait()
    for field_load, region_load in loads:
        field_load.wait()
        region_load.wait()
    m0, m1, m2 = mag[0], mag[1], mag[2]
    k0, k1, k2 = rate[0], rate[1], rate[2]

    def conductivity(kelvin, kind):
        first, second = kind == 0, kind == 1
        scale = jnp.where(first, m0, jnp.where(second, m1, m2))
        soft = jnp.where(first, k0, jnp.where(second, k1, k2))
        return scale * jnp.exp(-soft * kelvin)

    for z in range(NZ):
        rows = pl.ds(z * PITCH, L)
        kelvin = field[rows, :]
        value = conductivity(kelvin, region[rows, :])
        cond[rows, :] = value
        field_x[pl.ds(z, L, stride=NZ), :] = kelvin.T
        cond_x[pl.ds(z, L, stride=NZ), :] = value.T
    for side, at in ((0, 0), (1, L - 1)):
        edges_y[side, :NZ, :] = field[pl.ds(at, NZ, stride=PITCH), :]
        edges_y[side, NZ:, :] = cond[pl.ds(at, NZ, stride=PITCH), :]
        edges_x[side, :NZ, :] = field_x[pl.ds(at * NZ, NZ), :]
        edges_x[side, NZ:, :] = cond_x[pl.ds(at * NZ, NZ), :]
    pl.semaphore_wait(barrier, n_row + n_col - 2)
    share_x.start()
    share_y.start()

    def y_rows(ref, first):
        return jnp.stack([ref[pl.ds(first + i, NZ, stride=PITCH), :] for i in range(BLOCK)])

    def x_rows(ref, first):
        return nodes(ref, first, BLOCK)

    inner_links(functools.partial(y_rows, field), functools.partial(y_rows, cond), link_y, half_y)
    inner_links(
        functools.partial(x_rows, field_x), functools.partial(x_rows, cond_x), link_x, extra_x
    )
    for load in source_loads:
        load.wait()
    lower = None
    for z in range(NZ):
        rows = pl.ds(z * PITCH, L)
        t, c = field[rows, :], cond[rows, :]
        if z == 0:
            lower = depth_ratio * c * t
        if z < NZ - 1:
            above = pl.ds((z + 1) * PITCH, L)
            ta, ca = field[above, :], cond[above, :]
            upper = (2.0 * depth_ratio) * c * ca * inverse(c + ca) * (ta - t)
            along_z = upper - lower
            lower = upper
        else:
            along_z = -lower
        source[rows, :] = t + along_z + source[rows, :]

    share_x.wait()
    edge_links(edges_x, halo_x, link_x, extra_x)
    w, s, push = eliminate_coefficients(link_x, gl_x, gr_x, r_x, work_a, work_b)
    coef_x[my_col, :NZ, :] = w
    coef_x[my_col, NZ : 2 * NZ, :] = s
    coef_x[my_col, 2 * NZ :, :] = push
    gather_cx.start()

    share_y.wait()
    edge_links(edges_y, halo_y, link_y, half_y)
    for z in range(NZ):
        total = source[pl.ds(z * PITCH, L), :] + 2.0 * half_y[pl.ds(z, L, stride=NZ), :]
        side_x[pl.ds(z, L, stride=NZ), :] = total.T

    def side_of_x(first, count):
        return nodes(side_x, first, count) + nodes(extra_x, first, count)

    d, push = eliminate_right_side(side_of_x, gl_x, gr_x, r_x, work_a, work_b)
    rhs_x[my_col, :NZ, :] = d
    rhs_x[my_col, NZ:, :] = push
    gather_rx.start()

    w, s, push = eliminate_coefficients(link_y, gl_y, gr_y, r_y, work_c, work_d)
    coef_y[my_row, :NZ, :] = w
    coef_y[my_row, NZ : 2 * NZ, :] = s
    coef_y[my_row, 2 * NZ :, :] = push
    gather_cy.start()
    gather_cx.relay()
    gather_cx.wait()
    factor_chain(n_col, coef_x, chain_gx, chain_rx)
    gather_rx.relay()
    gather_rx.wait()
    solve_chain(n_col, rhs_x, chain_gx, chain_rx, chain_vx)

    def store_x(first, values):
        put_nodes(solved, first, values)

    substitute(chain_vx[my_col], chain_vx[my_col + 1], gl_x, gr_x, work_b, work_a, store_x)

    for z in range(NZ):
        at = pl.ds(z, L, stride=NZ)
        side_x[at, :] = solved[at, :].T - half_y[at, :]
    def side_of_y(first, count):
        return nodes(side_x, first, count)

    d, push = eliminate_right_side(side_of_y, gl_y, gr_y, r_y, work_a, work_b)
    rhs_y[my_row, :NZ, :] = d
    rhs_y[my_row, NZ:, :] = push
    gather_ry.start()
    gather_cy.wait()
    factor_chain(n_row, coef_y, chain_gy, chain_ry)
    gather_ry.wait()
    solve_chain(n_row, rhs_y, chain_gy, chain_ry, chain_vy)

    def store_y(first, values):
        for i in range(values.shape[0]):
            wide[pl.ds(first + i, NZ, stride=PITCH), :] = values[i]

    substitute(chain_vy[my_row], chain_vy[my_row + 1], gl_y, gr_y, work_b, work_a, store_y)
    for z in range(NZ):
        out[pl.ds(z * L, L), :] = wide[pl.ds(z * PITCH, L), :]
    for transfer in (share_y, share_x, gather_cx, gather_rx, gather_cy, gather_ry):
        transfer.finish()


def solution(mesh):
    n_row, n_col = mesh.shape["row"], mesh.shape["col"]

    def local(field, region, source, mag, rate):
        def flat(values):
            return values.reshape(NZ * L, L)

        whole = pltpu.VMEM((NZ * L, L), jnp.float32)
        pitched = pltpu.VMEM((NZ * PITCH, L), jnp.float32)
        integer = pltpu.VMEM((NZ * PITCH, L), jnp.int32)

        parameter = pltpu.SMEM((3,), jnp.float32)

        def stack(count, height):
            return pltpu.VMEM((count, height * NZ, L), jnp.float32)

        def dma(count):
            return pltpu.SemaphoreType.DMA((count,))

        result = pl.pallas_call(
            functools.partial(kernel, n_row, n_col),
            out_shape=pltpu.VMEM((NZ * L, L), jnp.float32),
            in_specs=[pl.BlockSpec(memory_space=pltpu.HBM)] * 5,
            out_specs=pl.BlockSpec(memory_space=pltpu.VMEM),
            scratch_shapes=[parameter, parameter, pitched, integer]
            + [pitched] * 3
            + [whole] * 18
            + [stack(2, 2)] * 4
            + [stack(n_col, 3), stack(n_col, 2), stack(n_row, 3), stack(n_row, 2)]
            + [stack(n_col, 1), stack(n_col, 1), stack(n_col + 1, 1)]
            + [stack(n_row, 1), stack(n_row, 1), stack(n_row + 1, 1)]
            + [dma(2), pltpu.SemaphoreType.DMA((3, NZ))]
            + [dma(2)] * 4
            + [dma(n_col - 1)] * 4
            + [dma(n_row - 1)] * 4,
            compiler_params=pltpu.CompilerParams(
                collective_id=0, has_side_effects=True, vmem_limit_bytes=40 * 1024 * 1024
            ),
            cost_estimate=pl.CostEstimate(
                flops=20_000_000, bytes_accessed=2_200_000, transcendentals=400_000
            ),
        )(*[pltpu.with_memory_space_constraint(v, pltpu.HBM) for v in (mag, rate, flat(field), flat(region), flat(source))])
        return result.reshape(NZ, L, L)

    spec = P(None, "row", "col")
    return jax.shard_map(
        local, mesh=mesh, in_specs=(spec, spec, spec, P(), P()), out_specs=spec, check_vma=False
    )
```

```python
import functools

import jax
import jax.numpy as jnp
from jax import lax
from jax.experimental import pallas as pl
from jax.experimental.pallas import tpu as pltpu
from jax.sharding import PartitionSpec as P

MESH = pl.DeviceIdType.MESH
inplane_half = 500.0
depth_ratio = 0.08

NZ = 8
L = 128
PITCH = L + 8
BLOCK = 16


def inverse(value):
    guess = pl.reciprocal(value, approx=True)
    return guess * (2.0 - value * guess)


def pairs(values):
    split = values.reshape((values.shape[0] // 2, 2) + values.shape[1:])
    return split[:, 0], split[:, 1]


def shifted_up(values, last):
    if values.shape[0] == 1:
        return last
    return jnp.concatenate([values[1:], last], axis=0)


def shifted_down(values, first):
    if values.shape[0] == 1:
        return first
    return jnp.concatenate([first, values[:-1]], axis=0)


def nodes(ref, first, count):
    return ref[pl.ds(first * NZ, count * NZ), :].reshape(count, NZ, L)


def put_nodes(ref, first, values):
    count = values.shape[0]
    ref[pl.ds(first * NZ, count * NZ), :] = values.reshape(count * NZ, L)


def levels():
    count = L
    while count > 1:
        half = count // 2
        yield count, half, L - 2 * count, L - 2 * half
        count = half


def eliminate_coefficients(link_ref, gl_ref, gr_ref, r_ref, w_ref, s_ref):
    pushed_out = jnp.zeros((1, NZ, L), jnp.float32)
    for count, half, node_at, pair_at in levels():
        block = min(half, BLOCK)
        carry = jnp.zeros((1, NZ, L), jnp.float32)
        for first in reversed(range(0, half, block)):
            if count == L:
                wl, wr = pairs(nodes(link_ref, 2 * first, 2 * block))
                inv = inverse(1.0 + wl + wr)
                gl, gr = wl * inv, wr * inv
                push = gl
                surplus = 1.0 + gr + shifted_up(push, carry)
            else:
                wl, wr = pairs(nodes(w_ref, node_at + 2 * first, 2 * block))
                se, so = pairs(nodes(s_ref, node_at + 2 * first, 2 * block))
                inv = inverse(se + wl + wr)
                gl, gr = wl * inv, wr * inv
                push = gl * se
                surplus = so + gr * se + shifted_up(push, carry)
            carry = push[:1]
            put_nodes(gl_ref, pair_at + first, gl)
            put_nodes(gr_ref, pair_at + first, gr)
            put_nodes(r_ref, pair_at + first, inv)
            put_nodes(w_ref, L - 2 * half + first, gl * wr)
            put_nodes(s_ref, L - 2 * half + first, surplus)
        pushed_out = pushed_out + carry
    return w_ref[pl.ds((L - 2) * NZ, NZ), :], s_ref[pl.ds((L - 2) * NZ, NZ), :], pushed_out[0]


def eliminate_right_side(load_side, gl_ref, gr_ref, r_ref, d_ref, q_ref):
    pushed_out = jnp.zeros((1, NZ, L), jnp.float32)
    for count, half, node_at, pair_at in levels():
        block = min(half, BLOCK)
        carry = jnp.zeros((1, NZ, L), jnp.float32)
        for first in reversed(range(0, half, block)):
            if count == L:
                de, do = pairs(load_side(2 * first, 2 * block))
            else:
                de, do = pairs(nodes(d_ref, node_at + 2 * first, 2 * block))
            push = nodes(gl_ref, pair_at + first, block) * de
            side = do + nodes(gr_ref, pair_at + first, block) * de + shifted_up(push, carry)
            carry = push[:1]
            put_nodes(q_ref, pair_at + first, nodes(r_ref, pair_at + first, block) * de)
            put_nodes(d_ref, L - 2 * half + first, side)
        pushed_out = pushed_out + carry
    return d_ref[pl.ds((L - 2) * NZ, NZ), :], pushed_out[0]


def substitute(before, last, gl_ref, gr_ref, q_ref, v_ref, store):
    v_ref[pl.ds((L - 2) * NZ, NZ), :] = last
    for count, half, node_at, pair_at in reversed(list(levels())):
        block = min(half, BLOCK)
        carry = before[None]
        for first in range(0, half, block):
            vo = nodes(v_ref, L - 2 * half + first, block)
            ve = (
                nodes(gl_ref, pair_at + first, block) * shifted_down(vo, carry)
                + nodes(gr_ref, pair_at + first, block) * vo
                + nodes(q_ref, pair_at + first, block)
            )
            carry = vo[block - 1 :]
            joined = jnp.stack([ve, vo], axis=1).reshape(2 * block, NZ, L)
            if count == L:
                store(2 * first, joined)
            else:
                put_nodes(v_ref, node_at + 2 * first, joined)


def factor_chain(n, coefficients, chain_g, chain_r):
    flow = None
    for p in range(n):
        surplus = coefficients[p, NZ : 2 * NZ, :]
        if p < n - 1:
            surplus = surplus + coefficients[p + 1, 2 * NZ :, :]
        if flow is not None:
            surplus = surplus + flow
        if p < n - 1:
            weight = coefficients[p + 1, :NZ, :]
            inv = inverse(surplus + weight)
            share = weight * inv
            chain_g[p] = share
            flow = share * surplus
        else:
            inv = inverse(surplus)
        chain_r[p] = inv


def solve_chain(n, sides, chain_g, chain_r, chain_v):
    flow = None
    scaled = []
    for p in range(n):
        side = sides[p, :NZ, :]
        if p < n - 1:
            side = side + sides[p + 1, NZ:, :]
        if flow is not None:
            side = side + flow
        if p < n - 1:
            flow = chain_g[p] * side
        scaled.append(side * chain_r[p])
    value = scaled[n - 1]
    chain_v[0] = jnp.zeros((NZ, L), jnp.float32)
    chain_v[n] = value
    for p in reversed(range(n - 1)):
        value = scaled[p] + chain_g[p] * value
        chain_v[p + 1] = value


class Gather:
    def __init__(self, axis, n, buffer, send, recv):
        self.axis, self.n, self.buffer, self.send, self.recv = axis, n, buffer, send, recv
        self.me = lax.axis_index(axis)

    def copy(self, step, slot):
        return pltpu.make_async_remote_copy(
            src_ref=self.buffer.at[slot],
            dst_ref=self.buffer.at[slot],
            send_sem=self.send.at[step - 1],
            recv_sem=self.recv.at[step - 1],
            device_id={self.axis: lax.rem(self.me + step, self.n)},
            device_id_type=MESH,
        )

    def start(self):
        for step in range(1, self.n):
            self.copy(step, self.me).start()

    def wait(self):
        for step in range(1, self.n):
            self.copy(step, lax.rem(self.me + self.n - step, self.n)).wait_recv()

    def finish(self):
        for step in range(1, self.n):
            self.copy(step, self.me).wait_send()


class PairedGather:
    def __init__(self, axis, n, buffer, send, recv):
        self.axis, self.n, self.buffer, self.send, self.recv = axis, n, buffer, send, recv
        self.me = lax.axis_index(axis)
        self.beside = self.me + 1 - 2 * lax.rem(self.me, 2)

    def copy(self, slot, to, at):
        return pltpu.make_async_remote_copy(
            src_ref=self.buffer.at[slot],
            dst_ref=self.buffer.at[slot],
            send_sem=self.send.at[at],
            recv_sem=self.recv.at[at],
            device_id={self.axis: to},
            device_id_type=MESH,
        )

    def out(self, step):
        return self.copy(self.me, lax.rem(self.me + step, self.n), step - 1)

    def relayed(self, step):
        return self.copy(lax.rem(self.me + self.n - step, self.n), self.beside, step)

    def start(self):
        for step in range(2, self.n, 2):
            self.out(step).start()
        self.copy(self.me, self.beside, 0).start()

    def relay(self):
        for step in range(2, self.n, 2):
            slot = lax.rem(self.me + self.n - step, self.n)
            self.copy(slot, self.beside, step - 1).wait_recv()
            self.relayed(step).start()

    def wait(self):
        self.copy(self.beside, self.beside, 0).wait_recv()
        for step in range(2, self.n, 2):
            slot = lax.rem(self.beside + self.n - step, self.n)
            self.copy(slot, self.beside, step).wait_recv()

    def finish(self):
        self.copy(self.me, self.beside, 0).wait_send()
        for step in range(2, self.n, 2):
            self.out(step).wait_send()
            self.relayed(step).wait_send()


class Halo:
    def __init__(self, axis, n, edges, halo, send, recv):
        self.axis, self.n, self.edges, self.halo, self.send, self.recv = axis, n, edges, halo, send, recv
        self.me = lax.axis_index(axis)

    def copy(self, side):
        to = self.me - 1 if side == 0 else self.me + 1
        return pltpu.make_async_remote_copy(
            src_ref=self.edges.at[side],
            dst_ref=self.halo.at[1 - side],
            send_sem=self.send.at[side],
            recv_sem=self.recv.at[1 - side],
            device_id={self.axis: to},
            device_id_type=MESH,
        )

    def start(self):
        @pl.when(self.me > 0)
        def _():
            self.copy(0).start()

        @pl.when(self.me < self.n - 1)
        def _():
            self.copy(1).start()

    def wait(self):
        @pl.when(self.me > 0)
        def _():
            self.copy(1).wait_recv()

        @pl.when(self.me == 0)
        def _():
            self.halo[0] = jnp.zeros((2 * NZ, L), jnp.float32)

        @pl.when(self.me < self.n - 1)
        def _():
            self.copy(0).wait_recv()

        @pl.when(self.me == self.n - 1)
        def _():
            self.halo[1] = jnp.zeros((2 * NZ, L), jnp.float32)

    def finish(self):
        @pl.when(self.me > 0)
        def _():
            self.copy(0).wait_send()

        @pl.when(self.me < self.n - 1)
        def _():
            self.copy(1).wait_send()


def link_between(cond, field, cond_before, field_before):
    weight = (2.0 * inplane_half) * cond * cond_before * inverse(cond + cond_before)
    return weight, weight * (field - field_before)


def inner_links(field_rows, cond_rows, link_ref, sum_ref):
    flux_before = None
    for first in range(0, L, BLOCK):
        t, c = field_rows(first), cond_rows(first)
        if first == 0:
            t_before, c_before = t[:1], c[:1]
        weight, flux = link_between(
            c, t, shifted_down(c, c_before), shifted_down(t, t_before)
        )
        put_nodes(link_ref, first, weight)
        put_nodes(sum_ref, first, shifted_up(flux, jnp.zeros((1, NZ, L), jnp.float32)) - flux)
        if first > 0:
            at = pl.ds((first - 1) * NZ, NZ)
            sum_ref[at, :] = flux[0] - flux_before
        t_before, c_before, flux_before = t[-1:], c[-1:], flux[-1]


def edge_links(edges, halo, link_ref, sum_ref):
    weight, flux = link_between(
        edges[0, NZ:, :], edges[0, :NZ, :], halo[0, NZ:, :], halo[0, :NZ, :]
    )
    link_ref[pl.ds(0, NZ), :] = weight
    sum_ref[pl.ds(0, NZ), :] = sum_ref[pl.ds(0, NZ), :] - flux
    weight, flux = link_between(
        halo[1, NZ:, :], halo[1, :NZ, :], edges[1, NZ:, :], edges[1, :NZ, :]
    )
    at = pl.ds((L - 1) * NZ, NZ)
    sum_ref[at, :] = sum_ref[at, :] + flux


def kernel(
    n_row,
    n_col,
    mag_hbm,
    rate_hbm,
    field_hbm,
    region_hbm,
    source_hbm,
    out,
    mag,
    rate,
    field,
    region,
    source,
    cond,
    wide,
    half_y,
    link_y,
    field_x,
    cond_x,
    side_x,
    extra_x,
    link_x,
    solved,
    gl_x,
    gr_x,
    r_x,
    gl_y,
    gr_y,
    r_y,
    work_a,
    work_b,
    work_c,
    work_d,
    edges_y,
    halo_y,
    edges_x,
    halo_x,
    coef_x,
    rhs_x,
    coef_y,
    rhs_y,
    chain_gx,
    chain_rx,
    chain_vx,
    chain_gy,
    chain_ry,
    chain_vy,
    par_sem,
    in_sem,
    hy_send,
    hy_recv,
    hx_send,
    hx_recv,
    cx_send,
    cx_recv,
    rx_send,
    rx_recv,
    cy_send,
    cy_recv,
    ry_send,
    ry_recv,
):
    my_row, my_col = lax.axis_index("row"), lax.axis_index("col")
    barrier = pltpu.get_barrier_semaphore()
    for step in range(1, n_row):
        pl.semaphore_signal(
            barrier, inc=1, device_id={"row": lax.rem(my_row + step, n_row)}, device_id_type=MESH
        )
    for step in range(1, n_col):
        pl.semaphore_signal(
            barrier, inc=1, device_id={"col": lax.rem(my_col + step, n_col)}, device_id_type=MESH
        )

    parameters = [
        pltpu.make_async_copy(mag_hbm, mag, par_sem.at[0]),
        pltpu.make_async_copy(rate_hbm, rate, par_sem.at[1]),
    ]
    for load in parameters:
        load.start()

    def layer(source_ref, target_ref, kind, z):
        return pltpu.make_async_copy(
            source_ref.at[pl.ds(z * L, L)], target_ref.at[pl.ds(z * PITCH, L)], in_sem.at[kind, z]
        )

    loads = [
        (layer(field_hbm, field, 0, z), layer(region_hbm, region, 1, z)) for z in range(NZ)
    ]
    source_loads = [layer(source_hbm, source, 2, z) for z in range(NZ)]
    for field_load, region_load in loads:
        field_load.start()
        region_load.start()
    for load in source_loads:
        load.start()

    share_y = Halo("row", n_row, edges_y, halo_y, hy_send, hy_recv)
    share_x = Halo("col", n_col, edges_x, halo_x, hx_send, hx_recv)
    gather_cx = PairedGather("col", n_col, coef_x, cx_send, cx_recv)
    gather_rx = Gather("col", n_col, rhs_x, rx_send, rx_recv)
    gather_cy = Gather("row", n_row, coef_y, cy_send, cy_recv)
    gather_ry = Gather("row", n_row, rhs_y, ry_send, ry_recv)

    for load in parameters:
        load.wait()
    for field_load, region_load in loads:
        field_load.wait()
        region_load.wait()
    m0, m1, m2 = mag[0], mag[1], mag[2]
    k0, k1, k2 = rate[0], rate[1], rate[2]

    def conductivity(kelvin, kind):
        first, second = kind == 0, kind == 1
        scale = jnp.where(first, m0, jnp.where(second, m1, m2))
        soft = jnp.where(first, k0, jnp.where(second, k1, k2))
        return scale * jnp.exp(-soft * kelvin)

    for z in range(NZ):
        rows = pl.ds(z * PITCH, L)
        kelvin = field[rows, :]
        value = conductivity(kelvin, region[rows, :])
        cond[rows, :] = value
        field_x[pl.ds(z, L, stride=NZ), :] = kelvin.T
        cond_x[pl.ds(z, L, stride=NZ), :] = value.T
    for side, at in ((0, 0), (1, L - 1)):
        edges_y[side, :NZ, :] = field[pl.ds(at, NZ, stride=PITCH), :]
        edges_y[side, NZ:, :] = cond[pl.ds(at, NZ, stride=PITCH), :]
        edges_x[side, :NZ, :] = field_x[pl.ds(at * NZ, NZ), :]
        edges_x[side, NZ:, :] = cond_x[pl.ds(at * NZ, NZ), :]
    pl.semaphore_wait(barrier, n_row + n_col - 2)
    share_x.start()
    share_y.start()

    def y_rows(ref, first):
        return jnp.stack([ref[pl.ds(first + i, NZ, stride=PITCH), :] for i in range(BLOCK)])

    def x_rows(ref, first):
        return nodes(ref, first, BLOCK)

    inner_links(functools.partial(y_rows, field), functools.partial(y_rows, cond), link_y, half_y)
    inner_links(
        functools.partial(x_rows, field_x), functools.partial(x_rows, cond_x), link_x, extra_x
    )
    for load in source_loads:
        load.wait()
    lower = None
    for z in range(NZ):
        rows = pl.ds(z * PITCH, L)
        t, c = field[rows, :], cond[rows, :]
        if z == 0:
            lower = depth_ratio * c * t
        if z < NZ - 1:
            above = pl.ds((z + 1) * PITCH, L)
            ta, ca = field[above, :], cond[above, :]
            upper = (2.0 * depth_ratio) * c * ca * inverse(c + ca) * (ta - t)
            along_z = upper - lower
            lower = upper
        else:
            along_z = -lower
        source[rows, :] = t + along_z + source[rows, :]

    share_x.wait()
    edge_links(edges_x, halo_x, link_x, extra_x)
    w, s, push = eliminate_coefficients(link_x, gl_x, gr_x, r_x, work_a, work_b)
    coef_x[my_col, :NZ, :] = w
    coef_x[my_col, NZ : 2 * NZ, :] = s
    coef_x[my_col, 2 * NZ :, :] = push
    gather_cx.start()

    share_y.wait()
    edge_links(edges_y, halo_y, link_y, half_y)
    for z in range(NZ):
        total = source[pl.ds(z * PITCH, L), :] + 2.0 * half_y[pl.ds(z, L, stride=NZ), :]
        side_x[pl.ds(z, L, stride=NZ), :] = total.T

    def side_of_x(first, count):
        return nodes(side_x, first, count) + nodes(extra_x, first, count)

    d, push = eliminate_right_side(side_of_x, gl_x, gr_x, r_x, work_a, work_b)
    rhs_x[my_col, :NZ, :] = d
    rhs_x[my_col, NZ:, :] = push
    gather_rx.start()

    w, s, push = eliminate_coefficients(link_y, gl_y, gr_y, r_y, work_c, work_d)
    coef_y[my_row, :NZ, :] = w
    coef_y[my_row, NZ : 2 * NZ, :] = s
    coef_y[my_row, 2 * NZ :, :] = push
    gather_cy.start()
    gather_cx.relay()
    gather_cx.wait()
    factor_chain(n_col, coef_x, chain_gx, chain_rx)
    gather_rx.wait()
    solve_chain(n_col, rhs_x, chain_gx, chain_rx, chain_vx)

    def store_x(first, values):
        put_nodes(solved, first, values)

    substitute(chain_vx[my_col], chain_vx[my_col + 1], gl_x, gr_x, work_b, work_a, store_x)

    for z in range(NZ):
        at = pl.ds(z, L, stride=NZ)
        side_x[at, :] = solved[at, :].T - half_y[at, :]
    def side_of_y(first, count):
        return nodes(side_x, first, count)

    d, push = eliminate_right_side(side_of_y, gl_y, gr_y, r_y, work_a, work_b)
    rhs_y[my_row, :NZ, :] = d
    rhs_y[my_row, NZ:, :] = push
    gather_ry.start()
    gather_cy.wait()
    factor_chain(n_row, coef_y, chain_gy, chain_ry)
    gather_ry.wait()
    solve_chain(n_row, rhs_y, chain_gy, chain_ry, chain_vy)

    def store_y(first, values):
        for i in range(values.shape[0]):
            wide[pl.ds(first + i, NZ, stride=PITCH), :] = values[i]

    substitute(chain_vy[my_row], chain_vy[my_row + 1], gl_y, gr_y, work_b, work_a, store_y)
    for z in range(NZ):
        out[pl.ds(z * L, L), :] = wide[pl.ds(z * PITCH, L), :]
    for transfer in (share_y, share_x, gather_cx, gather_rx, gather_cy, gather_ry):
        transfer.finish()


def solution(mesh):
    n_row, n_col = mesh.shape["row"], mesh.shape["col"]

    def local(field, region, source, mag, rate):
        def flat(values):
            return values.reshape(NZ * L, L)

        whole = pltpu.VMEM((NZ * L, L), jnp.float32)
        pitched = pltpu.VMEM((NZ * PITCH, L), jnp.float32)
        integer = pltpu.VMEM((NZ * PITCH, L), jnp.int32)

        parameter = pltpu.SMEM((3,), jnp.float32)

        def stack(count, height):
            return pltpu.VMEM((count, height * NZ, L), jnp.float32)

        def dma(count):
            return pltpu.SemaphoreType.DMA((count,))

        result = pl.pallas_call(
            functools.partial(kernel, n_row, n_col),
            out_shape=pltpu.VMEM((NZ * L, L), jnp.float32),
            in_specs=[pl.BlockSpec(memory_space=pltpu.HBM)] * 5,
            out_specs=pl.BlockSpec(memory_space=pltpu.VMEM),
            scratch_shapes=[parameter, parameter, pitched, integer]
            + [pitched] * 3
            + [whole] * 18
            + [stack(2, 2)] * 4
            + [stack(n_col, 3), stack(n_col, 2), stack(n_row, 3), stack(n_row, 2)]
            + [stack(n_col, 1), stack(n_col, 1), stack(n_col + 1, 1)]
            + [stack(n_row, 1), stack(n_row, 1), stack(n_row + 1, 1)]
            + [dma(2), pltpu.SemaphoreType.DMA((3, NZ))]
            + [dma(2)] * 4
            + [dma(n_col - 1)] * 4
            + [dma(n_row - 1)] * 4,
            compiler_params=pltpu.CompilerParams(
                collective_id=0, has_side_effects=True, vmem_limit_bytes=40 * 1024 * 1024
            ),
            cost_estimate=pl.CostEstimate(
                flops=20_000_000, bytes_accessed=2_200_000, transcendentals=400_000
            ),
        )(*[pltpu.with_memory_space_constraint(v, pltpu.HBM) for v in (mag, rate, flat(field), flat(region), flat(source))])
        return result.reshape(NZ, L, L)

    spec = P(None, "row", "col")
    return jax.shard_map(
        local, mesh=mesh, in_specs=(spec, spec, spec, P(), P()), out_specs=spec, check_vma=False
    )
```

```python
import functools

import jax
import jax.numpy as jnp
from jax import lax
from jax.experimental import pallas as pl
from jax.experimental.pallas import tpu as pltpu
from jax.sharding import PartitionSpec as P

MESH = pl.DeviceIdType.MESH
inplane_half = 500.0
depth_ratio = 0.08

NZ = 8
L = 128
PITCH = L + 8
BLOCK = 16


def inverse(value):
    guess = pl.reciprocal(value, approx=True)
    return guess * (2.0 - value * guess)


def pairs(values):
    split = values.reshape((values.shape[0] // 2, 2) + values.shape[1:])
    return split[:, 0], split[:, 1]


def shifted_up(values, last):
    if values.shape[0] == 1:
        return last
    return jnp.concatenate([values[1:], last], axis=0)


def shifted_down(values, first):
    if values.shape[0] == 1:
        return first
    return jnp.concatenate([first, values[:-1]], axis=0)


def nodes(ref, first, count):
    return ref[pl.ds(first * NZ, count * NZ), :].reshape(count, NZ, L)


def put_nodes(ref, first, values):
    count = values.shape[0]
    ref[pl.ds(first * NZ, count * NZ), :] = values.reshape(count * NZ, L)


def levels():
    count = L
    while count > 1:
        half = count // 2
        yield count, half, L - 2 * count, L - 2 * half
        count = half


def eliminate_coefficients(link_ref, gl_ref, gr_ref, r_ref, w_ref, s_ref):
    pushed_out = jnp.zeros((1, NZ, L), jnp.float32)
    for count, half, node_at, pair_at in levels():
        block = min(half, BLOCK)
        carry = jnp.zeros((1, NZ, L), jnp.float32)
        for first in reversed(range(0, half, block)):
            if count == L:
                wl, wr = pairs(nodes(link_ref, 2 * first, 2 * block))
                inv = inverse(1.0 + wl + wr)
                gl, gr = wl * inv, wr * inv
                push = gl
                surplus = 1.0 + gr + shifted_up(push, carry)
            else:
                wl, wr = pairs(nodes(w_ref, node_at + 2 * first, 2 * block))
                se, so = pairs(nodes(s_ref, node_at + 2 * first, 2 * block))
                inv = inverse(se + wl + wr)
                gl, gr = wl * inv, wr * inv
                push = gl * se
                surplus = so + gr * se + shifted_up(push, carry)
            carry = push[:1]
            put_nodes(gl_ref, pair_at + first, gl)
            put_nodes(gr_ref, pair_at + first, gr)
            put_nodes(r_ref, pair_at + first, inv)
            put_nodes(w_ref, L - 2 * half + first, gl * wr)
            put_nodes(s_ref, L - 2 * half + first, surplus)
        pushed_out = pushed_out + carry
    return w_ref[pl.ds((L - 2) * NZ, NZ), :], s_ref[pl.ds((L - 2) * NZ, NZ), :], pushed_out[0]


def close_coefficients(link_ref, gl_ref, gr_ref, r_ref, w_ref, s_ref):
    def one(ref, node):
        return ref[pl.ds(node * NZ, NZ), :]

    weight, surplus, pushed_out = one(link_ref, 0), 1.0, 0.0
    for count, half, node_at, pair_at in levels():
        if count == L:
            wr, so = one(link_ref, 1), 1.0
        else:
            wr, so = one(w_ref, node_at + 1), one(s_ref, node_at + 1)
        inv = inverse(surplus + weight + wr)
        gl, gr = weight * inv, wr * inv
        gl_ref[pl.ds(pair_at * NZ, NZ), :] = gl
        gr_ref[pl.ds(pair_at * NZ, NZ), :] = gr
        r_ref[pl.ds(pair_at * NZ, NZ), :] = inv
        pushed_out = pushed_out + gl * surplus
        surplus = so + gr * surplus
        if half > 1:
            push = one(gl_ref, pair_at + 1)
            if count < L:
                push = push * one(s_ref, node_at + 2)
            surplus = surplus + push
        weight = gl * wr
    return weight, surplus, pushed_out


def eliminate_right_side(load_side, gl_ref, gr_ref, r_ref, d_ref, q_ref):
    pushed_out = jnp.zeros((1, NZ, L), jnp.float32)
    for count, half, node_at, pair_at in levels():
        block = min(half, BLOCK)
        carry = jnp.zeros((1, NZ, L), jnp.float32)
        for first in reversed(range(0, half, block)):
            if count == L:
                de, do = pairs(load_side(2 * first, 2 * block))
            else:
                de, do = pairs(nodes(d_ref, node_at + 2 * first, 2 * block))
            push = nodes(gl_ref, pair_at + first, block) * de
            side = do + nodes(gr_ref, pair_at + first, block) * de + shifted_up(push, carry)
            carry = push[:1]
            put_nodes(q_ref, pair_at + first, nodes(r_ref, pair_at + first, block) * de)
            put_nodes(d_ref, L - 2 * half + first, side)
        pushed_out = pushed_out + carry
    return d_ref[pl.ds((L - 2) * NZ, NZ), :], pushed_out[0]


def substitute(before, last, gl_ref, gr_ref, q_ref, v_ref, store):
    v_ref[pl.ds((L - 2) * NZ, NZ), :] = last
    for count, half, node_at, pair_at in reversed(list(levels())):
        block = min(half, BLOCK)
        carry = before[None]
        for first in range(0, half, block):
            vo = nodes(v_ref, L - 2 * half + first, block)
            ve = (
                nodes(gl_ref, pair_at + first, block) * shifted_down(vo, carry)
                + nodes(gr_ref, pair_at + first, block) * vo
                + nodes(q_ref, pair_at + first, block)
            )
            carry = vo[block - 1 :]
            joined = jnp.stack([ve, vo], axis=1).reshape(2 * block, NZ, L)
            if count == L:
                store(2 * first, joined)
            else:
                put_nodes(v_ref, node_at + 2 * first, joined)


def factor_chain(n, coefficients, chain_g, chain_r):
    flow = None
    for p in range(n):
        surplus = coefficients[p, NZ : 2 * NZ, :]
        if p < n - 1:
            surplus = surplus + coefficients[p + 1, 2 * NZ :, :]
        if flow is not None:
            surplus = surplus + flow
        if p < n - 1:
            weight = coefficients[p + 1, :NZ, :]
            inv = inverse(surplus + weight)
            share = weight * inv
            chain_g[p] = share
            flow = share * surplus
        else:
            inv = inverse(surplus)
        chain_r[p] = inv


def solve_chain(n, sides, chain_g, chain_r, chain_v):
    flow = None
    scaled = []
    for p in range(n):
        side = sides[p, :NZ, :]
        if p < n - 1:
            side = side + sides[p + 1, NZ:, :]
        if flow is not None:
            side = side + flow
        if p < n - 1:
            flow = chain_g[p] * side
        scaled.append(side * chain_r[p])
    value = scaled[n - 1]
    chain_v[0] = jnp.zeros((NZ, L), jnp.float32)
    chain_v[n] = value
    for p in reversed(range(n - 1)):
        value = scaled[p] + chain_g[p] * value
        chain_v[p + 1] = value


class Gather:
    def __init__(self, axis, n, buffer, send, recv):
        self.axis, self.n, self.buffer, self.send, self.recv = axis, n, buffer, send, recv
        self.me = lax.axis_index(axis)

    def copy(self, step, slot):
        return pltpu.make_async_remote_copy(
            src_ref=self.buffer.at[slot],
            dst_ref=self.buffer.at[slot],
            send_sem=self.send.at[step - 1],
            recv_sem=self.recv.at[step - 1],
            device_id={self.axis: lax.rem(self.me + step, self.n)},
            device_id_type=MESH,
        )

    def start(self):
        for step in range(1, self.n):
            self.copy(step, self.me).start()

    def wait(self):
        for step in range(1, self.n):
            self.copy(step, lax.rem(self.me + self.n - step, self.n)).wait_recv()

    def finish(self):
        for step in range(1, self.n):
            self.copy(step, self.me).wait_send()


class PairedGather:
    def __init__(self, axis, n, buffer, send, recv):
        self.axis, self.n, self.buffer, self.send, self.recv = axis, n, buffer, send, recv
        self.me = lax.axis_index(axis)
        self.beside = self.me + 1 - 2 * lax.rem(self.me, 2)

    def copy(self, slot, to, at):
        return pltpu.make_async_remote_copy(
            src_ref=self.buffer.at[slot],
            dst_ref=self.buffer.at[slot],
            send_sem=self.send.at[at],
            recv_sem=self.recv.at[at],
            device_id={self.axis: to},
            device_id_type=MESH,
        )

    def out(self, step):
        return self.copy(self.me, lax.rem(self.me + step, self.n), step - 1)

    def relayed(self, step):
        return self.copy(lax.rem(self.me + self.n - step, self.n), self.beside, step)

    def start(self):
        for step in range(2, self.n, 2):
            self.out(step).start()
        self.copy(self.me, self.beside, 0).start()

    def relay(self):
        for step in range(2, self.n, 2):
            slot = lax.rem(self.me + self.n - step, self.n)
            self.copy(slot, self.beside, step - 1).wait_recv()
            self.relayed(step).start()

    def wait(self):
        self.copy(self.beside, self.beside, 0).wait_recv()
        for step in range(2, self.n, 2):
            slot = lax.rem(self.beside + self.n - step, self.n)
            self.copy(slot, self.beside, step).wait_recv()

    def finish(self):
        self.copy(self.me, self.beside, 0).wait_send()
        for step in range(2, self.n, 2):
            self.out(step).wait_send()
            self.relayed(step).wait_send()


class Halo:
    def __init__(self, axis, n, edges, halo, send, recv):
        self.axis, self.n, self.edges, self.halo, self.send, self.recv = axis, n, edges, halo, send, recv
        self.me = lax.axis_index(axis)

    def copy(self, side):
        to = self.me - 1 if side == 0 else self.me + 1
        return pltpu.make_async_remote_copy(
            src_ref=self.edges.at[side],
            dst_ref=self.halo.at[1 - side],
            send_sem=self.send.at[side],
            recv_sem=self.recv.at[1 - side],
            device_id={self.axis: to},
            device_id_type=MESH,
        )

    def start(self):
        @pl.when(self.me > 0)
        def _():
            self.copy(0).start()

        @pl.when(self.me < self.n - 1)
        def _():
            self.copy(1).start()

    def wait(self):
        @pl.when(self.me > 0)
        def _():
            self.copy(1).wait_recv()

        @pl.when(self.me == 0)
        def _():
            self.halo[0] = jnp.zeros((2 * NZ, L), jnp.float32)

        @pl.when(self.me < self.n - 1)
        def _():
            self.copy(0).wait_recv()

        @pl.when(self.me == self.n - 1)
        def _():
            self.halo[1] = jnp.zeros((2 * NZ, L), jnp.float32)

    def finish(self):
        @pl.when(self.me > 0)
        def _():
            self.copy(0).wait_send()

        @pl.when(self.me < self.n - 1)
        def _():
            self.copy(1).wait_send()


def link_between(cond, field, cond_before, field_before):
    weight = (2.0 * inplane_half) * cond * cond_before * inverse(cond + cond_before)
    return weight, weight * (field - field_before)


def inner_links(field_rows, cond_rows, link_ref, sum_ref):
    flux_before = None
    for first in range(0, L, BLOCK):
        t, c = field_rows(first), cond_rows(first)
        if first == 0:
            t_before, c_before = t[:1], c[:1]
        weight, flux = link_between(
            c, t, shifted_down(c, c_before), shifted_down(t, t_before)
        )
        put_nodes(link_ref, first, weight)
        put_nodes(sum_ref, first, shifted_up(flux, jnp.zeros((1, NZ, L), jnp.float32)) - flux)
        if first > 0:
            at = pl.ds((first - 1) * NZ, NZ)
            sum_ref[at, :] = flux[0] - flux_before
        t_before, c_before, flux_before = t[-1:], c[-1:], flux[-1]


def edge_links(edges, halo, link_ref, sum_ref):
    weight, flux = link_between(
        edges[0, NZ:, :], edges[0, :NZ, :], halo[0, NZ:, :], halo[0, :NZ, :]
    )
    link_ref[pl.ds(0, NZ), :] = weight
    sum_ref[pl.ds(0, NZ), :] = sum_ref[pl.ds(0, NZ), :] - flux
    weight, flux = link_between(
        halo[1, NZ:, :], halo[1, :NZ, :], edges[1, NZ:, :], edges[1, :NZ, :]
    )
    at = pl.ds((L - 1) * NZ, NZ)
    sum_ref[at, :] = sum_ref[at, :] + flux


def kernel(
    n_row,
    n_col,
    mag_hbm,
    rate_hbm,
    field_hbm,
    region_hbm,
    source_hbm,
    out,
    mag,
    rate,
    field,
    region,
    source,
    cond,
    wide,
    half_y,
    link_y,
    field_x,
    cond_x,
    side_x,
    extra_x,
    link_x,
    solved,
    gl_x,
    gr_x,
    r_x,
    gl_y,
    gr_y,
    r_y,
    work_a,
    work_b,
    work_c,
    work_d,
    edges_y,
    halo_y,
    edges_x,
    halo_x,
    coef_x,
    rhs_x,
    coef_y,
    rhs_y,
    chain_gx,
    chain_rx,
    chain_vx,
    chain_gy,
    chain_ry,
    chain_vy,
    par_sem,
    in_sem,
    hy_send,
    hy_recv,
    hx_send,
    hx_recv,
    cx_send,
    cx_recv,
    rx_send,
    rx_recv,
    cy_send,
    cy_recv,
    ry_send,
    ry_recv,
):
    my_row, my_col = lax.axis_index("row"), lax.axis_index("col")
    barrier = pltpu.get_barrier_semaphore()
    for step in range(1, n_row):
        pl.semaphore_signal(
            barrier, inc=1, device_id={"row": lax.rem(my_row + step, n_row)}, device_id_type=MESH
        )
    for step in range(1, n_col):
        pl.semaphore_signal(
            barrier, inc=1, device_id={"col": lax.rem(my_col + step, n_col)}, device_id_type=MESH
        )

    parameters = [
        pltpu.make_async_copy(mag_hbm, mag, par_sem.at[0]),
        pltpu.make_async_copy(rate_hbm, rate, par_sem.at[1]),
    ]
    for load in parameters:
        load.start()

    def layer(source_ref, target_ref, kind, z):
        return pltpu.make_async_copy(
            source_ref.at[pl.ds(z * L, L)], target_ref.at[pl.ds(z * PITCH, L)], in_sem.at[kind, z]
        )

    loads = [
        (layer(field_hbm, field, 0, z), layer(region_hbm, region, 1, z)) for z in range(NZ)
    ]
    source_loads = [layer(source_hbm, source, 2, z) for z in range(NZ)]
    for field_load, region_load in loads:
        field_load.start()
        region_load.start()
    for load in source_loads:
        load.start()

    share_y = Halo("row", n_row, edges_y, halo_y, hy_send, hy_recv)
    share_x = Halo("col", n_col, edges_x, halo_x, hx_send, hx_recv)
    gather_cx = PairedGather("col", n_col, coef_x, cx_send, cx_recv)
    gather_rx = Gather("col", n_col, rhs_x, rx_send, rx_recv)
    gather_cy = Gather("row", n_row, coef_y, cy_send, cy_recv)
    gather_ry = Gather("row", n_row, rhs_y, ry_send, ry_recv)

    for load in parameters:
        load.wait()
    for field_load, region_load in loads:
        field_load.wait()
        region_load.wait()
    m0, m1, m2 = mag[0], mag[1], mag[2]
    k0, k1, k2 = rate[0], rate[1], rate[2]

    def conductivity(kelvin, kind):
        first, second = kind == 0, kind == 1
        scale = jnp.where(first, m0, jnp.where(second, m1, m2))
        soft = jnp.where(first, k0, jnp.where(second, k1, k2))
        return scale * jnp.exp(-soft * kelvin)

    for z in range(NZ):
        rows = pl.ds(z * PITCH, L)
        kelvin = field[rows, :]
        value = conductivity(kelvin, region[rows, :])
        cond[rows, :] = value
        field_x[pl.ds(z, L, stride=NZ), :] = kelvin.T
        cond_x[pl.ds(z, L, stride=NZ), :] = value.T
    for side, at in ((0, 0), (1, L - 1)):
        edges_y[side, :NZ, :] = field[pl.ds(at, NZ, stride=PITCH), :]
        edges_y[side, NZ:, :] = cond[pl.ds(at, NZ, stride=PITCH), :]
        edges_x[side, :NZ, :] = field_x[pl.ds(at * NZ, NZ), :]
        edges_x[side, NZ:, :] = cond_x[pl.ds(at * NZ, NZ), :]
    pl.semaphore_wait(barrier, n_row + n_col - 2)
    share_x.start()
    share_y.start()

    def y_rows(ref, first):
        return jnp.stack([ref[pl.ds(first + i, NZ, stride=PITCH), :] for i in range(BLOCK)])

    def x_rows(ref, first):
        return nodes(ref, first, BLOCK)

    inner_links(functools.partial(y_rows, field), functools.partial(y_rows, cond), link_y, half_y)
    inner_links(
        functools.partial(x_rows, field_x), functools.partial(x_rows, cond_x), link_x, extra_x
    )
    for load in source_loads:
        load.wait()
    lower = None
    for z in range(NZ):
        rows = pl.ds(z * PITCH, L)
        t, c = field[rows, :], cond[rows, :]
        if z == 0:
            lower = depth_ratio * c * t
        if z < NZ - 1:
            above = pl.ds((z + 1) * PITCH, L)
            ta, ca = field[above, :], cond[above, :]
            upper = (2.0 * depth_ratio) * c * ca * inverse(c + ca) * (ta - t)
            along_z = upper - lower
            lower = upper
        else:
            along_z = -lower
        source[rows, :] = t + along_z + source[rows, :]

    eliminate_coefficients(link_x, gl_x, gr_x, r_x, work_a, work_b)
    share_x.wait()
    edge_links(edges_x, halo_x, link_x, extra_x)
    w, s, push = close_coefficients(link_x, gl_x, gr_x, r_x, work_a, work_b)
    coef_x[my_col, :NZ, :] = w
    coef_x[my_col, NZ : 2 * NZ, :] = s
    coef_x[my_col, 2 * NZ :, :] = push
    gather_cx.start()

    share_y.wait()
    edge_links(edges_y, halo_y, link_y, half_y)
    for z in range(NZ):
        total = source[pl.ds(z * PITCH, L), :] + 2.0 * half_y[pl.ds(z, L, stride=NZ), :]
        side_x[pl.ds(z, L, stride=NZ), :] = total.T

    def side_of_x(first, count):
        return nodes(side_x, first, count) + nodes(extra_x, first, count)

    d, push = eliminate_right_side(side_of_x, gl_x, gr_x, r_x, work_a, work_b)
    rhs_x[my_col, :NZ, :] = d
    rhs_x[my_col, NZ:, :] = push
    gather_rx.start()

    w, s, push = eliminate_coefficients(link_y, gl_y, gr_y, r_y, work_c, work_d)
    coef_y[my_row, :NZ, :] = w
    coef_y[my_row, NZ : 2 * NZ, :] = s
    coef_y[my_row, 2 * NZ :, :] = push
    gather_cy.start()
    gather_cx.relay()
    gather_cx.wait()
    factor_chain(n_col, coef_x, chain_gx, chain_rx)
    gather_rx.wait()
    solve_chain(n_col, rhs_x, chain_gx, chain_rx, chain_vx)

    def store_x(first, values):
        put_nodes(solved, first, values)

    substitute(chain_vx[my_col], chain_vx[my_col + 1], gl_x, gr_x, work_b, work_a, store_x)

    for z in range(NZ):
        at = pl.ds(z, L, stride=NZ)
        side_x[at, :] = solved[at, :].T - half_y[at, :]
    def side_of_y(first, count):
        return nodes(side_x, first, count)

    d, push = eliminate_right_side(side_of_y, gl_y, gr_y, r_y, work_a, work_b)
    rhs_y[my_row, :NZ, :] = d
    rhs_y[my_row, NZ:, :] = push
    gather_ry.start()
    gather_cy.wait()
    factor_chain(n_row, coef_y, chain_gy, chain_ry)
    gather_ry.wait()
    solve_chain(n_row, rhs_y, chain_gy, chain_ry, chain_vy)

    def store_y(first, values):
        for i in range(values.shape[0]):
            wide[pl.ds(first + i, NZ, stride=PITCH), :] = values[i]

    substitute(chain_vy[my_row], chain_vy[my_row + 1], gl_y, gr_y, work_b, work_a, store_y)
    for z in range(NZ):
        out[pl.ds(z * L, L), :] = wide[pl.ds(z * PITCH, L), :]
    for transfer in (share_y, share_x, gather_cx, gather_rx, gather_cy, gather_ry):
        transfer.finish()


def solution(mesh):
    n_row, n_col = mesh.shape["row"], mesh.shape["col"]

    def local(field, region, source, mag, rate):
        def flat(values):
            return values.reshape(NZ * L, L)

        whole = pltpu.VMEM((NZ * L, L), jnp.float32)
        pitched = pltpu.VMEM((NZ * PITCH, L), jnp.float32)
        integer = pltpu.VMEM((NZ * PITCH, L), jnp.int32)

        parameter = pltpu.SMEM((3,), jnp.float32)

        def stack(count, height):
            return pltpu.VMEM((count, height * NZ, L), jnp.float32)

        def dma(count):
            return pltpu.SemaphoreType.DMA((count,))

        result = pl.pallas_call(
            functools.partial(kernel, n_row, n_col),
            out_shape=pltpu.VMEM((NZ * L, L), jnp.float32),
            in_specs=[pl.BlockSpec(memory_space=pltpu.HBM)] * 5,
            out_specs=pl.BlockSpec(memory_space=pltpu.VMEM),
            scratch_shapes=[parameter, parameter, pitched, integer]
            + [pitched] * 3
            + [whole] * 18
            + [stack(2, 2)] * 4
            + [stack(n_col, 3), stack(n_col, 2), stack(n_row, 3), stack(n_row, 2)]
            + [stack(n_col, 1), stack(n_col, 1), stack(n_col + 1, 1)]
            + [stack(n_row, 1), stack(n_row, 1), stack(n_row + 1, 1)]
            + [dma(2), pltpu.SemaphoreType.DMA((3, NZ))]
            + [dma(2)] * 4
            + [dma(n_col - 1)] * 4
            + [dma(n_row - 1)] * 4,
            compiler_params=pltpu.CompilerParams(
                collective_id=0, has_side_effects=True, vmem_limit_bytes=40 * 1024 * 1024
            ),
            cost_estimate=pl.CostEstimate(
                flops=20_000_000, bytes_accessed=2_200_000, transcendentals=400_000
            ),
        )(*[pltpu.with_memory_space_constraint(v, pltpu.HBM) for v in (mag, rate, flat(field), flat(region), flat(source))])
        return result.reshape(NZ, L, L)

    spec = P(None, "row", "col")
    return jax.shard_map(
        local, mesh=mesh, in_specs=(spec, spec, spec, P(), P()), out_specs=spec, check_vma=False
    )
```

```python
import functools

import jax
import jax.numpy as jnp
from jax import lax
from jax.experimental import pallas as pl
from jax.experimental.pallas import tpu as pltpu
from jax.sharding import PartitionSpec as P

MESH = pl.DeviceIdType.MESH
inplane_half = 500.0
depth_ratio = 0.08

NZ = 8
L = 128
PITCH = L + 8
BLOCK = 16


def inverse(value):
    guess = pl.reciprocal(value, approx=True)
    return guess * (2.0 - value * guess)


def pairs(values):
    split = values.reshape((values.shape[0] // 2, 2) + values.shape[1:])
    return split[:, 0], split[:, 1]


def shifted_up(values, last):
    if values.shape[0] == 1:
        return last
    return jnp.concatenate([values[1:], last], axis=0)


def shifted_down(values, first):
    if values.shape[0] == 1:
        return first
    return jnp.concatenate([first, values[:-1]], axis=0)


def nodes(ref, first, count):
    return ref[pl.ds(first * NZ, count * NZ), :].reshape(count, NZ, L)


def put_nodes(ref, first, values):
    count = values.shape[0]
    ref[pl.ds(first * NZ, count * NZ), :] = values.reshape(count * NZ, L)


def levels():
    count = L
    while count > 1:
        half = count // 2
        yield count, half, L - 2 * count, L - 2 * half
        count = half


def eliminate_coefficients(link_ref, gl_ref, gr_ref, r_ref, w_ref, s_ref):
    pushed_out = jnp.zeros((1, NZ, L), jnp.float32)
    for count, half, node_at, pair_at in levels():
        block = min(half, BLOCK)
        carry = jnp.zeros((1, NZ, L), jnp.float32)
        for first in reversed(range(0, half, block)):
            if count == L:
                wl, wr = pairs(nodes(link_ref, 2 * first, 2 * block))
                inv = inverse(1.0 + wl + wr)
                gl, gr = wl * inv, wr * inv
                push = gl
                surplus = 1.0 + gr + shifted_up(push, carry)
            else:
                wl, wr = pairs(nodes(w_ref, node_at + 2 * first, 2 * block))
                se, so = pairs(nodes(s_ref, node_at + 2 * first, 2 * block))
                inv = inverse(se + wl + wr)
                gl, gr = wl * inv, wr * inv
                push = gl * se
                surplus = so + gr * se + shifted_up(push, carry)
            carry = push[:1]
            put_nodes(gl_ref, pair_at + first, gl)
            put_nodes(gr_ref, pair_at + first, gr)
            put_nodes(r_ref, pair_at + first, inv)
            put_nodes(w_ref, L - 2 * half + first, gl * wr)
            put_nodes(s_ref, L - 2 * half + first, surplus)
        pushed_out = pushed_out + carry
    return w_ref[pl.ds((L - 2) * NZ, NZ), :], s_ref[pl.ds((L - 2) * NZ, NZ), :], pushed_out[0]


def close_coefficients(link_ref, gl_ref, gr_ref, r_ref, w_ref, s_ref):
    def one(ref, node):
        return ref[pl.ds(node * NZ, NZ), :]

    weight, surplus, pushed_out = one(link_ref, 0), 1.0, 0.0
    for count, half, node_at, pair_at in levels():
        if count == L:
            wr, so = one(link_ref, 1), 1.0
        else:
            wr, so = one(w_ref, node_at + 1), one(s_ref, node_at + 1)
        inv = inverse(surplus + weight + wr)
        gl, gr = weight * inv, wr * inv
        gl_ref[pl.ds(pair_at * NZ, NZ), :] = gl
        gr_ref[pl.ds(pair_at * NZ, NZ), :] = gr
        r_ref[pl.ds(pair_at * NZ, NZ), :] = inv
        pushed_out = pushed_out + gl * surplus
        surplus = so + gr * surplus
        if half > 1:
            push = one(gl_ref, pair_at + 1)
            if count < L:
                push = push * one(s_ref, node_at + 2)
            surplus = surplus + push
        weight = gl * wr
    return weight, surplus, pushed_out


def eliminate_right_side(load_side, gl_ref, gr_ref, r_ref, d_ref, q_ref):
    pushed_out = jnp.zeros((1, NZ, L), jnp.float32)
    for count, half, node_at, pair_at in levels():
        block = min(half, BLOCK)
        carry = jnp.zeros((1, NZ, L), jnp.float32)
        for first in reversed(range(0, half, block)):
            if count == L:
                de, do = pairs(load_side(2 * first, 2 * block))
            else:
                de, do = pairs(nodes(d_ref, node_at + 2 * first, 2 * block))
            push = nodes(gl_ref, pair_at + first, block) * de
            side = do + nodes(gr_ref, pair_at + first, block) * de + shifted_up(push, carry)
            carry = push[:1]
            put_nodes(q_ref, pair_at + first, nodes(r_ref, pair_at + first, block) * de)
            put_nodes(d_ref, L - 2 * half + first, side)
        pushed_out = pushed_out + carry
    return d_ref[pl.ds((L - 2) * NZ, NZ), :], pushed_out[0]


def substitute(before, last, gl_ref, gr_ref, q_ref, v_ref, store):
    v_ref[pl.ds((L - 2) * NZ, NZ), :] = last
    for count, half, node_at, pair_at in reversed(list(levels())):
        block = min(half, BLOCK)
        carry = before[None]
        for first in range(0, half, block):
            vo = nodes(v_ref, L - 2 * half + first, block)
            ve = (
                nodes(gl_ref, pair_at + first, block) * shifted_down(vo, carry)
                + nodes(gr_ref, pair_at + first, block) * vo
                + nodes(q_ref, pair_at + first, block)
            )
            carry = vo[block - 1 :]
            joined = jnp.stack([ve, vo], axis=1).reshape(2 * block, NZ, L)
            if count == L:
                store(2 * first, joined)
            else:
                put_nodes(v_ref, node_at + 2 * first, joined)


def factor_chain(n, coefficients, chain_g, chain_r):
    flow = None
    for p in range(n):
        surplus = coefficients[p, NZ : 2 * NZ, :]
        if p < n - 1:
            surplus = surplus + coefficients[p + 1, 2 * NZ :, :]
        if flow is not None:
            surplus = surplus + flow
        if p < n - 1:
            weight = coefficients[p + 1, :NZ, :]
            inv = inverse(surplus + weight)
            share = weight * inv
            chain_g[p] = share
            flow = share * surplus
        else:
            inv = inverse(surplus)
        chain_r[p] = inv


def solve_chain(n, sides, chain_g, chain_r, chain_v):
    flow = None
    scaled = []
    for p in range(n):
        side = sides[p, :NZ, :]
        if p < n - 1:
            side = side + sides[p + 1, NZ:, :]
        if flow is not None:
            side = side + flow
        if p < n - 1:
            flow = chain_g[p] * side
        scaled.append(side * chain_r[p])
    value = scaled[n - 1]
    chain_v[0] = jnp.zeros((NZ, L), jnp.float32)
    chain_v[n] = value
    for p in reversed(range(n - 1)):
        value = scaled[p] + chain_g[p] * value
        chain_v[p + 1] = value


def far_first(n, stride):
    return sorted(range(stride, n, stride), key=lambda step: (abs(2 * step - n), step))


class Gather:
    def __init__(self, axis, n, buffer, send, recv):
        self.axis, self.n, self.buffer, self.send, self.recv = axis, n, buffer, send, recv
        self.me = lax.axis_index(axis)

    def copy(self, step, slot):
        return pltpu.make_async_remote_copy(
            src_ref=self.buffer.at[slot],
            dst_ref=self.buffer.at[slot],
            send_sem=self.send.at[step - 1],
            recv_sem=self.recv.at[step - 1],
            device_id={self.axis: lax.rem(self.me + step, self.n)},
            device_id_type=MESH,
        )

    def start(self):
        for step in far_first(self.n, 1):
            self.copy(step, self.me).start()

    def wait(self):
        for step in range(1, self.n):
            self.copy(step, lax.rem(self.me + self.n - step, self.n)).wait_recv()

    def finish(self):
        for step in range(1, self.n):
            self.copy(step, self.me).wait_send()


class PairedGather:
    def __init__(self, axis, n, buffer, send, recv):
        self.axis, self.n, self.buffer, self.send, self.recv = axis, n, buffer, send, recv
        self.me = lax.axis_index(axis)
        self.beside = self.me + 1 - 2 * lax.rem(self.me, 2)

    def copy(self, slot, to, at):
        return pltpu.make_async_remote_copy(
            src_ref=self.buffer.at[slot],
            dst_ref=self.buffer.at[slot],
            send_sem=self.send.at[at],
            recv_sem=self.recv.at[at],
            device_id={self.axis: to},
            device_id_type=MESH,
        )

    def out(self, step):
        return self.copy(self.me, lax.rem(self.me + step, self.n), step - 1)

    def relayed(self, step):
        return self.copy(lax.rem(self.me + self.n - step, self.n), self.beside, step)

    def start(self):
        for step in far_first(self.n, 2):
            self.out(step).start()
        self.copy(self.me, self.beside, 0).start()

    def relay(self):
        for step in range(2, self.n, 2):
            slot = lax.rem(self.me + self.n - step, self.n)
            self.copy(slot, self.beside, step - 1).wait_recv()
            self.relayed(step).start()

    def wait(self):
        self.copy(self.beside, self.beside, 0).wait_recv()
        for step in range(2, self.n, 2):
            slot = lax.rem(self.beside + self.n - step, self.n)
            self.copy(slot, self.beside, step).wait_recv()

    def finish(self):
        self.copy(self.me, self.beside, 0).wait_send()
        for step in range(2, self.n, 2):
            self.out(step).wait_send()
            self.relayed(step).wait_send()


class Halo:
    def __init__(self, axis, n, edges, halo, send, recv):
        self.axis, self.n, self.edges, self.halo, self.send, self.recv = axis, n, edges, halo, send, recv
        self.me = lax.axis_index(axis)

    def copy(self, side):
        to = self.me - 1 if side == 0 else self.me + 1
        return pltpu.make_async_remote_copy(
            src_ref=self.edges.at[side],
            dst_ref=self.halo.at[1 - side],
            send_sem=self.send.at[side],
            recv_sem=self.recv.at[1 - side],
            device_id={self.axis: to},
            device_id_type=MESH,
        )

    def start(self):
        @pl.when(self.me > 0)
        def _():
            self.copy(0).start()

        @pl.when(self.me < self.n - 1)
        def _():
            self.copy(1).start()

    def wait(self):
        @pl.when(self.me > 0)
        def _():
            self.copy(1).wait_recv()

        @pl.when(self.me == 0)
        def _():
            self.halo[0] = jnp.zeros((2 * NZ, L), jnp.float32)

        @pl.when(self.me < self.n - 1)
        def _():
            self.copy(0).wait_recv()

        @pl.when(self.me == self.n - 1)
        def _():
            self.halo[1] = jnp.zeros((2 * NZ, L), jnp.float32)

    def finish(self):
        @pl.when(self.me > 0)
        def _():
            self.copy(0).wait_send()

        @pl.when(self.me < self.n - 1)
        def _():
            self.copy(1).wait_send()


def link_between(cond, field, cond_before, field_before):
    weight = (2.0 * inplane_half) * cond * cond_before * inverse(cond + cond_before)
    return weight, weight * (field - field_before)


def inner_links(field_rows, cond_rows, link_ref, sum_ref):
    flux_before = None
    for first in range(0, L, BLOCK):
        t, c = field_rows(first), cond_rows(first)
        if first == 0:
            t_before, c_before = t[:1], c[:1]
        weight, flux = link_between(
            c, t, shifted_down(c, c_before), shifted_down(t, t_before)
        )
        put_nodes(link_ref, first, weight)
        put_nodes(sum_ref, first, shifted_up(flux, jnp.zeros((1, NZ, L), jnp.float32)) - flux)
        if first > 0:
            at = pl.ds((first - 1) * NZ, NZ)
            sum_ref[at, :] = flux[0] - flux_before
        t_before, c_before, flux_before = t[-1:], c[-1:], flux[-1]


def edge_links(edges, halo, link_ref, sum_ref):
    weight, flux = link_between(
        edges[0, NZ:, :], edges[0, :NZ, :], halo[0, NZ:, :], halo[0, :NZ, :]
    )
    link_ref[pl.ds(0, NZ), :] = weight
    sum_ref[pl.ds(0, NZ), :] = sum_ref[pl.ds(0, NZ), :] - flux
    weight, flux = link_between(
        halo[1, NZ:, :], halo[1, :NZ, :], edges[1, NZ:, :], edges[1, :NZ, :]
    )
    at = pl.ds((L - 1) * NZ, NZ)
    sum_ref[at, :] = sum_ref[at, :] + flux


def kernel(
    n_row,
    n_col,
    mag_hbm,
    rate_hbm,
    field_hbm,
    region_hbm,
    source_hbm,
    out,
    mag,
    rate,
    field,
    region,
    source,
    cond,
    wide,
    half_y,
    link_y,
    field_x,
    cond_x,
    side_x,
    extra_x,
    link_x,
    solved,
    gl_x,
    gr_x,
    r_x,
    gl_y,
    gr_y,
    r_y,
    work_a,
    work_b,
    work_c,
    work_d,
    edges_y,
    halo_y,
    edges_x,
    halo_x,
    coef_x,
    rhs_x,
    coef_y,
    rhs_y,
    chain_gx,
    chain_rx,
    chain_vx,
    chain_gy,
    chain_ry,
    chain_vy,
    par_sem,
    in_sem,
    hy_send,
    hy_recv,
    hx_send,
    hx_recv,
    cx_send,
    cx_recv,
    rx_send,
    rx_recv,
    cy_send,
    cy_recv,
    ry_send,
    ry_recv,
):
    my_row, my_col = lax.axis_index("row"), lax.axis_index("col")
    barrier = pltpu.get_barrier_semaphore()
    for step in range(1, n_row):
        pl.semaphore_signal(
            barrier, inc=1, device_id={"row": lax.rem(my_row + step, n_row)}, device_id_type=MESH
        )
    for step in range(1, n_col):
        pl.semaphore_signal(
            barrier, inc=1, device_id={"col": lax.rem(my_col + step, n_col)}, device_id_type=MESH
        )

    parameters = [
        pltpu.make_async_copy(mag_hbm, mag, par_sem.at[0]),
        pltpu.make_async_copy(rate_hbm, rate, par_sem.at[1]),
    ]
    for load in parameters:
        load.start()

    def layer(source_ref, target_ref, kind, z):
        return pltpu.make_async_copy(
            source_ref.at[pl.ds(z * L, L)], target_ref.at[pl.ds(z * PITCH, L)], in_sem.at[kind, z]
        )

    loads = [
        (layer(field_hbm, field, 0, z), layer(region_hbm, region, 1, z)) for z in range(NZ)
    ]
    source_loads = [layer(source_hbm, source, 2, z) for z in range(NZ)]
    for field_load, region_load in loads:
        field_load.start()
        region_load.start()
    for load in source_loads:
        load.start()

    share_y = Halo("row", n_row, edges_y, halo_y, hy_send, hy_recv)
    share_x = Halo("col", n_col, edges_x, halo_x, hx_send, hx_recv)
    gather_cx = PairedGather("col", n_col, coef_x, cx_send, cx_recv)
    gather_rx = Gather("col", n_col, rhs_x, rx_send, rx_recv)
    gather_cy = Gather("row", n_row, coef_y, cy_send, cy_recv)
    gather_ry = Gather("row", n_row, rhs_y, ry_send, ry_recv)

    for load in parameters:
        load.wait()
    for field_load, region_load in loads:
        field_load.wait()
        region_load.wait()
    m0, m1, m2 = mag[0], mag[1], mag[2]
    k0, k1, k2 = rate[0], rate[1], rate[2]

    def conductivity(kelvin, kind):
        first, second = kind == 0, kind == 1
        scale = jnp.where(first, m0, jnp.where(second, m1, m2))
        soft = jnp.where(first, k0, jnp.where(second, k1, k2))
        return scale * jnp.exp(-soft * kelvin)

    for z in range(NZ):
        rows = pl.ds(z * PITCH, L)
        kelvin = field[rows, :]
        value = conductivity(kelvin, region[rows, :])
        cond[rows, :] = value
        field_x[pl.ds(z, L, stride=NZ), :] = kelvin.T
        cond_x[pl.ds(z, L, stride=NZ), :] = value.T
    for side, at in ((0, 0), (1, L - 1)):
        edges_y[side, :NZ, :] = field[pl.ds(at, NZ, stride=PITCH), :]
        edges_y[side, NZ:, :] = cond[pl.ds(at, NZ, stride=PITCH), :]
        edges_x[side, :NZ, :] = field_x[pl.ds(at * NZ, NZ), :]
        edges_x[side, NZ:, :] = cond_x[pl.ds(at * NZ, NZ), :]
    pl.semaphore_wait(barrier, n_row + n_col - 2)
    share_x.start()
    share_y.start()

    def y_rows(ref, first):
        return jnp.stack([ref[pl.ds(first + i, NZ, stride=PITCH), :] for i in range(BLOCK)])

    def x_rows(ref, first):
        return nodes(ref, first, BLOCK)

    inner_links(functools.partial(y_rows, field), functools.partial(y_rows, cond), link_y, half_y)
    inner_links(
        functools.partial(x_rows, field_x), functools.partial(x_rows, cond_x), link_x, extra_x
    )
    for load in source_loads:
        load.wait()
    lower = None
    for z in range(NZ):
        rows = pl.ds(z * PITCH, L)
        t, c = field[rows, :], cond[rows, :]
        if z == 0:
            lower = depth_ratio * c * t
        if z < NZ - 1:
            above = pl.ds((z + 1) * PITCH, L)
            ta, ca = field[above, :], cond[above, :]
            upper = (2.0 * depth_ratio) * c * ca * inverse(c + ca) * (ta - t)
            along_z = upper - lower
            lower = upper
        else:
            along_z = -lower
        source[rows, :] = t + along_z + source[rows, :]

    eliminate_coefficients(link_x, gl_x, gr_x, r_x, work_a, work_b)
    share_x.wait()
    edge_links(edges_x, halo_x, link_x, extra_x)
    w, s, push = close_coefficients(link_x, gl_x, gr_x, r_x, work_a, work_b)
    coef_x[my_col, :NZ, :] = w
    coef_x[my_col, NZ : 2 * NZ, :] = s
    coef_x[my_col, 2 * NZ :, :] = push
    gather_cx.start()

    share_y.wait()
    edge_links(edges_y, halo_y, link_y, half_y)
    for z in range(NZ):
        total = source[pl.ds(z * PITCH, L), :] + 2.0 * half_y[pl.ds(z, L, stride=NZ), :]
        side_x[pl.ds(z, L, stride=NZ), :] = total.T

    def side_of_x(first, count):
        return nodes(side_x, first, count) + nodes(extra_x, first, count)

    d, push = eliminate_right_side(side_of_x, gl_x, gr_x, r_x, work_a, work_b)
    rhs_x[my_col, :NZ, :] = d
    rhs_x[my_col, NZ:, :] = push
    gather_rx.start()

    w, s, push = eliminate_coefficients(link_y, gl_y, gr_y, r_y, work_c, work_d)
    coef_y[my_row, :NZ, :] = w
    coef_y[my_row, NZ : 2 * NZ, :] = s
    coef_y[my_row, 2 * NZ :, :] = push
    gather_cy.start()
    gather_cx.relay()
    gather_cx.wait()
    factor_chain(n_col, coef_x, chain_gx, chain_rx)
    gather_rx.wait()
    solve_chain(n_col, rhs_x, chain_gx, chain_rx, chain_vx)

    def store_x(first, values):
        put_nodes(solved, first, values)

    substitute(chain_vx[my_col], chain_vx[my_col + 1], gl_x, gr_x, work_b, work_a, store_x)

    for z in range(NZ):
        at = pl.ds(z, L, stride=NZ)
        side_x[at, :] = solved[at, :].T - half_y[at, :]
    def side_of_y(first, count):
        return nodes(side_x, first, count)

    d, push = eliminate_right_side(side_of_y, gl_y, gr_y, r_y, work_a, work_b)
    rhs_y[my_row, :NZ, :] = d
    rhs_y[my_row, NZ:, :] = push
    gather_ry.start()
    gather_cy.wait()
    factor_chain(n_row, coef_y, chain_gy, chain_ry)
    gather_ry.wait()
    solve_chain(n_row, rhs_y, chain_gy, chain_ry, chain_vy)

    def store_y(first, values):
        for i in range(values.shape[0]):
            wide[pl.ds(first + i, NZ, stride=PITCH), :] = values[i]

    substitute(chain_vy[my_row], chain_vy[my_row + 1], gl_y, gr_y, work_b, work_a, store_y)
    for z in range(NZ):
        out[pl.ds(z * L, L), :] = wide[pl.ds(z * PITCH, L), :]
    for transfer in (share_y, share_x, gather_cx, gather_rx, gather_cy, gather_ry):
        transfer.finish()


def solution(mesh):
    n_row, n_col = mesh.shape["row"], mesh.shape["col"]

    def local(field, region, source, mag, rate):
        def flat(values):
            return values.reshape(NZ * L, L)

        whole = pltpu.VMEM((NZ * L, L), jnp.float32)
        pitched = pltpu.VMEM((NZ * PITCH, L), jnp.float32)
        integer = pltpu.VMEM((NZ * PITCH, L), jnp.int32)

        parameter = pltpu.SMEM((3,), jnp.float32)

        def stack(count, height):
            return pltpu.VMEM((count, height * NZ, L), jnp.float32)

        def dma(count):
            return pltpu.SemaphoreType.DMA((count,))

        result = pl.pallas_call(
            functools.partial(kernel, n_row, n_col),
            out_shape=pltpu.VMEM((NZ * L, L), jnp.float32),
            in_specs=[pl.BlockSpec(memory_space=pltpu.HBM)] * 5,
            out_specs=pl.BlockSpec(memory_space=pltpu.VMEM),
            scratch_shapes=[parameter, parameter, pitched, integer]
            + [pitched] * 3
            + [whole] * 18
            + [stack(2, 2)] * 4
            + [stack(n_col, 3), stack(n_col, 2), stack(n_row, 3), stack(n_row, 2)]
            + [stack(n_col, 1), stack(n_col, 1), stack(n_col + 1, 1)]
            + [stack(n_row, 1), stack(n_row, 1), stack(n_row + 1, 1)]
            + [dma(2), pltpu.SemaphoreType.DMA((3, NZ))]
            + [dma(2)] * 4
            + [dma(n_col - 1)] * 4
            + [dma(n_row - 1)] * 4,
            compiler_params=pltpu.CompilerParams(
                collective_id=0, has_side_effects=True, vmem_limit_bytes=40 * 1024 * 1024
            ),
            cost_estimate=pl.CostEstimate(
                flops=20_000_000, bytes_accessed=2_200_000, transcendentals=400_000
            ),
        )(*[pltpu.with_memory_space_constraint(v, pltpu.HBM) for v in (mag, rate, flat(field), flat(region), flat(source))])
        return result.reshape(NZ, L, L)

    spec = P(None, "row", "col")
    return jax.shard_map(
        local, mesh=mesh, in_specs=(spec, spec, spec, P(), P()), out_specs=spec, check_vma=False
    )
```

```python
import functools

import jax
import jax.numpy as jnp
from jax import lax
from jax.experimental import pallas as pl
from jax.experimental.pallas import tpu as pltpu
from jax.sharding import PartitionSpec as P

MESH = pl.DeviceIdType.MESH
inplane_half = 500.0
depth_ratio = 0.08

NZ = 8
L = 128
PITCH = L + 8
BLOCK = 8


def inverse(value):
    guess = pl.reciprocal(value, approx=True)
    return guess * (2.0 - value * guess)


def pairs(values):
    split = values.reshape((values.shape[0] // 2, 2) + values.shape[1:])
    return split[:, 0], split[:, 1]


def shifted_up(values, last):
    if values.shape[0] == 1:
        return last
    return jnp.concatenate([values[1:], last], axis=0)


def shifted_down(values, first):
    if values.shape[0] == 1:
        return first
    return jnp.concatenate([first, values[:-1]], axis=0)


def nodes(ref, first, count):
    return ref[pl.ds(first * NZ, count * NZ), :].reshape(count, NZ, L)


def put_nodes(ref, first, values):
    count = values.shape[0]
    ref[pl.ds(first * NZ, count * NZ), :] = values.reshape(count * NZ, L)


def levels():
    count = L
    while count > 1:
        half = count // 2
        yield count, half, L - 2 * count, L - 2 * half
        count = half


def eliminate_coefficients(link_ref, gl_ref, gr_ref, r_ref, w_ref, s_ref):
    pushed_out = jnp.zeros((1, NZ, L), jnp.float32)
    for count, half, node_at, pair_at in levels():
        block = min(half, BLOCK)
        carry = jnp.zeros((1, NZ, L), jnp.float32)
        for first in reversed(range(0, half, block)):
            if count == L:
                wl, wr = pairs(nodes(link_ref, 2 * first, 2 * block))
                inv = inverse(1.0 + wl + wr)
                gl, gr = wl * inv, wr * inv
                push = gl
                surplus = 1.0 + gr + shifted_up(push, carry)
            else:
                wl, wr = pairs(nodes(w_ref, node_at + 2 * first, 2 * block))
                se, so = pairs(nodes(s_ref, node_at + 2 * first, 2 * block))
                inv = inverse(se + wl + wr)
                gl, gr = wl * inv, wr * inv
                push = gl * se
                surplus = so + gr * se + shifted_up(push, carry)
            carry = push[:1]
            put_nodes(gl_ref, pair_at + first, gl)
            put_nodes(gr_ref, pair_at + first, gr)
            put_nodes(r_ref, pair_at + first, inv)
            put_nodes(w_ref, L - 2 * half + first, gl * wr)
            put_nodes(s_ref, L - 2 * half + first, surplus)
        pushed_out = pushed_out + carry
    return w_ref[pl.ds((L - 2) * NZ, NZ), :], s_ref[pl.ds((L - 2) * NZ, NZ), :], pushed_out[0]


def close_coefficients(link_ref, gl_ref, gr_ref, r_ref, w_ref, s_ref):
    def one(ref, node):
        return ref[pl.ds(node * NZ, NZ), :]

    weight, surplus, pushed_out = one(link_ref, 0), 1.0, 0.0
    for count, half, node_at, pair_at in levels():
        if count == L:
            wr, so = one(link_ref, 1), 1.0
        else:
            wr, so = one(w_ref, node_at + 1), one(s_ref, node_at + 1)
        inv = inverse(surplus + weight + wr)
        gl, gr = weight * inv, wr * inv
        gl_ref[pl.ds(pair_at * NZ, NZ), :] = gl
        gr_ref[pl.ds(pair_at * NZ, NZ), :] = gr
        r_ref[pl.ds(pair_at * NZ, NZ), :] = inv
        pushed_out = pushed_out + gl * surplus
        surplus = so + gr * surplus
        if half > 1:
            push = one(gl_ref, pair_at + 1)
            if count < L:
                push = push * one(s_ref, node_at + 2)
            surplus = surplus + push
        weight = gl * wr
    return weight, surplus, pushed_out


def eliminate_right_side(load_side, gl_ref, gr_ref, r_ref, d_ref, q_ref):
    pushed_out = jnp.zeros((1, NZ, L), jnp.float32)
    for count, half, node_at, pair_at in levels():
        block = min(half, BLOCK)
        carry = jnp.zeros((1, NZ, L), jnp.float32)
        for first in reversed(range(0, half, block)):
            if count == L:
                de, do = pairs(load_side(2 * first, 2 * block))
            else:
                de, do = pairs(nodes(d_ref, node_at + 2 * first, 2 * block))
            push = nodes(gl_ref, pair_at + first, block) * de
            side = do + nodes(gr_ref, pair_at + first, block) * de + shifted_up(push, carry)
            carry = push[:1]
            put_nodes(q_ref, pair_at + first, nodes(r_ref, pair_at + first, block) * de)
            put_nodes(d_ref, L - 2 * half + first, side)
        pushed_out = pushed_out + carry
    return d_ref[pl.ds((L - 2) * NZ, NZ), :], pushed_out[0]


def substitute(before, last, gl_ref, gr_ref, q_ref, v_ref, store):
    v_ref[pl.ds((L - 2) * NZ, NZ), :] = last
    for count, half, node_at, pair_at in reversed(list(levels())):
        block = min(half, BLOCK)
        carry = before[None]
        for first in range(0, half, block):
            vo = nodes(v_ref, L - 2 * half + first, block)
            ve = (
                nodes(gl_ref, pair_at + first, block) * shifted_down(vo, carry)
                + nodes(gr_ref, pair_at + first, block) * vo
                + nodes(q_ref, pair_at + first, block)
            )
            carry = vo[block - 1 :]
            joined = jnp.stack([ve, vo], axis=1).reshape(2 * block, NZ, L)
            if count == L:
                store(2 * first, joined)
            else:
                put_nodes(v_ref, node_at + 2 * first, joined)


def factor_chain(n, coefficients, chain_g, chain_r):
    flow = None
    for p in range(n):
        surplus = coefficients[p, NZ : 2 * NZ, :]
        if p < n - 1:
            surplus = surplus + coefficients[p + 1, 2 * NZ :, :]
        if flow is not None:
            surplus = surplus + flow
        if p < n - 1:
            weight = coefficients[p + 1, :NZ, :]
            inv = inverse(surplus + weight)
            share = weight * inv
            chain_g[p] = share
            flow = share * surplus
        else:
            inv = inverse(surplus)
        chain_r[p] = inv


def solve_chain(n, sides, chain_g, chain_r, chain_v):
    flow = None
    scaled = []
    for p in range(n):
        side = sides[p, :NZ, :]
        if p < n - 1:
            side = side + sides[p + 1, NZ:, :]
        if flow is not None:
            side = side + flow
        if p < n - 1:
            flow = chain_g[p] * side
        scaled.append(side * chain_r[p])
    value = scaled[n - 1]
    chain_v[0] = jnp.zeros((NZ, L), jnp.float32)
    chain_v[n] = value
    for p in reversed(range(n - 1)):
        value = scaled[p] + chain_g[p] * value
        chain_v[p + 1] = value


class Gather:
    def __init__(self, axis, n, buffer, send, recv):
        self.axis, self.n, self.buffer, self.send, self.recv = axis, n, buffer, send, recv
        self.me = lax.axis_index(axis)

    def copy(self, step, slot):
        return pltpu.make_async_remote_copy(
            src_ref=self.buffer.at[slot],
            dst_ref=self.buffer.at[slot],
            send_sem=self.send.at[step - 1],
            recv_sem=self.recv.at[step - 1],
            device_id={self.axis: lax.rem(self.me + step, self.n)},
            device_id_type=MESH,
        )

    def start(self):
        for step in range(1, self.n):
            self.copy(step, self.me).start()

    def wait(self):
        for step in range(1, self.n):
            self.copy(step, lax.rem(self.me + self.n - step, self.n)).wait_recv()

    def finish(self):
        for step in range(1, self.n):
            self.copy(step, self.me).wait_send()


class PairedGather:
    def __init__(self, axis, n, buffer, send, recv):
        self.axis, self.n, self.buffer, self.send, self.recv = axis, n, buffer, send, recv
        self.me = lax.axis_index(axis)
        self.beside = self.me + 1 - 2 * lax.rem(self.me, 2)

    def copy(self, slot, to, at):
        return pltpu.make_async_remote_copy(
            src_ref=self.buffer.at[slot],
            dst_ref=self.buffer.at[slot],
            send_sem=self.send.at[at],
            recv_sem=self.recv.at[at],
            device_id={self.axis: to},
            device_id_type=MESH,
        )

    def out(self, step):
        return self.copy(self.me, lax.rem(self.me + step, self.n), step - 1)

    def relayed(self, step):
        return self.copy(lax.rem(self.me + self.n - step, self.n), self.beside, step)

    def start(self):
        for step in range(2, self.n, 2):
            self.out(step).start()
        self.copy(self.me, self.beside, 0).start()

    def relay(self):
        for step in range(2, self.n, 2):
            slot = lax.rem(self.me + self.n - step, self.n)
            self.copy(slot, self.beside, step - 1).wait_recv()
            self.relayed(step).start()

    def wait(self):
        self.copy(self.beside, self.beside, 0).wait_recv()
        for step in range(2, self.n, 2):
            slot = lax.rem(self.beside + self.n - step, self.n)
            self.copy(slot, self.beside, step).wait_recv()

    def finish(self):
        self.copy(self.me, self.beside, 0).wait_send()
        for step in range(2, self.n, 2):
            self.out(step).wait_send()
            self.relayed(step).wait_send()


class Halo:
    def __init__(self, axis, n, edges, halo, send, recv):
        self.axis, self.n, self.edges, self.halo, self.send, self.recv = axis, n, edges, halo, send, recv
        self.me = lax.axis_index(axis)

    def copy(self, side):
        to = self.me - 1 if side == 0 else self.me + 1
        return pltpu.make_async_remote_copy(
            src_ref=self.edges.at[side],
            dst_ref=self.halo.at[1 - side],
            send_sem=self.send.at[side],
            recv_sem=self.recv.at[1 - side],
            device_id={self.axis: to},
            device_id_type=MESH,
        )

    def start(self):
        @pl.when(self.me > 0)
        def _():
            self.copy(0).start()

        @pl.when(self.me < self.n - 1)
        def _():
            self.copy(1).start()

    def wait(self):
        @pl.when(self.me > 0)
        def _():
            self.copy(1).wait_recv()

        @pl.when(self.me == 0)
        def _():
            self.halo[0] = jnp.zeros((2 * NZ, L), jnp.float32)

        @pl.when(self.me < self.n - 1)
        def _():
            self.copy(0).wait_recv()

        @pl.when(self.me == self.n - 1)
        def _():
            self.halo[1] = jnp.zeros((2 * NZ, L), jnp.float32)

    def finish(self):
        @pl.when(self.me > 0)
        def _():
            self.copy(0).wait_send()

        @pl.when(self.me < self.n - 1)
        def _():
            self.copy(1).wait_send()


def link_between(cond, field, cond_before, field_before):
    weight = (2.0 * inplane_half) * cond * cond_before * inverse(cond + cond_before)
    return weight, weight * (field - field_before)


def inner_links(field_rows, cond_rows, link_ref, sum_ref):
    flux_before = None
    for first in range(0, L, BLOCK):
        t, c = field_rows(first), cond_rows(first)
        if first == 0:
            t_before, c_before = t[:1], c[:1]
        weight, flux = link_between(
            c, t, shifted_down(c, c_before), shifted_down(t, t_before)
        )
        put_nodes(link_ref, first, weight)
        put_nodes(sum_ref, first, shifted_up(flux, jnp.zeros((1, NZ, L), jnp.float32)) - flux)
        if first > 0:
            at = pl.ds((first - 1) * NZ, NZ)
            sum_ref[at, :] = flux[0] - flux_before
        t_before, c_before, flux_before = t[-1:], c[-1:], flux[-1]


def edge_links(edges, halo, link_ref, sum_ref):
    weight, flux = link_between(
        edges[0, NZ:, :], edges[0, :NZ, :], halo[0, NZ:, :], halo[0, :NZ, :]
    )
    link_ref[pl.ds(0, NZ), :] = weight
    sum_ref[pl.ds(0, NZ), :] = sum_ref[pl.ds(0, NZ), :] - flux
    weight, flux = link_between(
        halo[1, NZ:, :], halo[1, :NZ, :], edges[1, NZ:, :], edges[1, :NZ, :]
    )
    at = pl.ds((L - 1) * NZ, NZ)
    sum_ref[at, :] = sum_ref[at, :] + flux


def kernel(
    n_row,
    n_col,
    mag_hbm,
    rate_hbm,
    field_hbm,
    region_hbm,
    source_hbm,
    out,
    mag,
    rate,
    field,
    region,
    source,
    cond,
    wide,
    half_y,
    link_y,
    field_x,
    cond_x,
    side_x,
    extra_x,
    link_x,
    solved,
    gl_x,
    gr_x,
    r_x,
    gl_y,
    gr_y,
    r_y,
    work_a,
    work_b,
    work_c,
    work_d,
    edges_y,
    halo_y,
    edges_x,
    halo_x,
    coef_x,
    rhs_x,
    coef_y,
    rhs_y,
    chain_gx,
    chain_rx,
    chain_vx,
    chain_gy,
    chain_ry,
    chain_vy,
    par_sem,
    in_sem,
    hy_send,
    hy_recv,
    hx_send,
    hx_recv,
    cx_send,
    cx_recv,
    rx_send,
    rx_recv,
    cy_send,
    cy_recv,
    ry_send,
    ry_recv,
):
    my_row, my_col = lax.axis_index("row"), lax.axis_index("col")
    barrier = pltpu.get_barrier_semaphore()
    for step in range(1, n_row):
        pl.semaphore_signal(
            barrier, inc=1, device_id={"row": lax.rem(my_row + step, n_row)}, device_id_type=MESH
        )
    for step in range(1, n_col):
        pl.semaphore_signal(
            barrier, inc=1, device_id={"col": lax.rem(my_col + step, n_col)}, device_id_type=MESH
        )

    parameters = [
        pltpu.make_async_copy(mag_hbm, mag, par_sem.at[0]),
        pltpu.make_async_copy(rate_hbm, rate, par_sem.at[1]),
    ]
    for load in parameters:
        load.start()

    def layer(source_ref, target_ref, kind, z):
        return pltpu.make_async_copy(
            source_ref.at[pl.ds(z * L, L)], target_ref.at[pl.ds(z * PITCH, L)], in_sem.at[kind, z]
        )

    loads = [
        (layer(field_hbm, field, 0, z), layer(region_hbm, region, 1, z)) for z in range(NZ)
    ]
    source_loads = [layer(source_hbm, source, 2, z) for z in range(NZ)]
    for field_load, region_load in loads:
        field_load.start()
        region_load.start()
    for load in source_loads:
        load.start()

    share_y = Halo("row", n_row, edges_y, halo_y, hy_send, hy_recv)
    share_x = Halo("col", n_col, edges_x, halo_x, hx_send, hx_recv)
    gather_cx = PairedGather("col", n_col, coef_x, cx_send, cx_recv)
    gather_rx = Gather("col", n_col, rhs_x, rx_send, rx_recv)
    gather_cy = Gather("row", n_row, coef_y, cy_send, cy_recv)
    gather_ry = Gather("row", n_row, rhs_y, ry_send, ry_recv)

    for load in parameters:
        load.wait()
    for field_load, region_load in loads:
        field_load.wait()
        region_load.wait()
    m0, m1, m2 = mag[0], mag[1], mag[2]
    k0, k1, k2 = rate[0], rate[1], rate[2]

    def conductivity(kelvin, kind):
        first, second = kind == 0, kind == 1
        scale = jnp.where(first, m0, jnp.where(second, m1, m2))
        soft = jnp.where(first, k0, jnp.where(second, k1, k2))
        return scale * jnp.exp(-soft * kelvin)

    for z in range(NZ):
        rows = pl.ds(z * PITCH, L)
        kelvin = field[rows, :]
        value = conductivity(kelvin, region[rows, :])
        cond[rows, :] = value
        field_x[pl.ds(z, L, stride=NZ), :] = kelvin.T
        cond_x[pl.ds(z, L, stride=NZ), :] = value.T
    for side, at in ((0, 0), (1, L - 1)):
        edges_y[side, :NZ, :] = field[pl.ds(at, NZ, stride=PITCH), :]
        edges_y[side, NZ:, :] = cond[pl.ds(at, NZ, stride=PITCH), :]
        edges_x[side, :NZ, :] = field_x[pl.ds(at * NZ, NZ), :]
        edges_x[side, NZ:, :] = cond_x[pl.ds(at * NZ, NZ), :]
    pl.semaphore_wait(barrier, n_row + n_col - 2)
    share_x.start()
    share_y.start()

    def y_rows(ref, first):
        return jnp.stack([ref[pl.ds(first + i, NZ, stride=PITCH), :] for i in range(BLOCK)])

    def x_rows(ref, first):
        return nodes(ref, first, BLOCK)

    inner_links(functools.partial(y_rows, field), functools.partial(y_rows, cond), link_y, half_y)
    inner_links(
        functools.partial(x_rows, field_x), functools.partial(x_rows, cond_x), link_x, extra_x
    )
    for load in source_loads:
        load.wait()
    lower = None
    for z in range(NZ):
        rows = pl.ds(z * PITCH, L)
        t, c = field[rows, :], cond[rows, :]
        if z == 0:
            lower = depth_ratio * c * t
        if z < NZ - 1:
            above = pl.ds((z + 1) * PITCH, L)
            ta, ca = field[above, :], cond[above, :]
            upper = (2.0 * depth_ratio) * c * ca * inverse(c + ca) * (ta - t)
            along_z = upper - lower
            lower = upper
        else:
            along_z = -lower
        source[rows, :] = t + along_z + source[rows, :]

    eliminate_coefficients(link_x, gl_x, gr_x, r_x, work_a, work_b)
    share_x.wait()
    edge_links(edges_x, halo_x, link_x, extra_x)
    w, s, push = close_coefficients(link_x, gl_x, gr_x, r_x, work_a, work_b)
    coef_x[my_col, :NZ, :] = w
    coef_x[my_col, NZ : 2 * NZ, :] = s
    coef_x[my_col, 2 * NZ :, :] = push
    gather_cx.start()

    share_y.wait()
    edge_links(edges_y, halo_y, link_y, half_y)
    for z in range(NZ):
        total = source[pl.ds(z * PITCH, L), :] + 2.0 * half_y[pl.ds(z, L, stride=NZ), :]
        side_x[pl.ds(z, L, stride=NZ), :] = total.T

    def side_of_x(first, count):
        return nodes(side_x, first, count) + nodes(extra_x, first, count)

    d, push = eliminate_right_side(side_of_x, gl_x, gr_x, r_x, work_a, work_b)
    rhs_x[my_col, :NZ, :] = d
    rhs_x[my_col, NZ:, :] = push
    gather_rx.start()

    w, s, push = eliminate_coefficients(link_y, gl_y, gr_y, r_y, work_c, work_d)
    coef_y[my_row, :NZ, :] = w
    coef_y[my_row, NZ : 2 * NZ, :] = s
    coef_y[my_row, 2 * NZ :, :] = push
    gather_cy.start()
    gather_cx.relay()
    gather_cx.wait()
    factor_chain(n_col, coef_x, chain_gx, chain_rx)
    gather_rx.wait()
    solve_chain(n_col, rhs_x, chain_gx, chain_rx, chain_vx)

    def store_x(first, values):
        put_nodes(solved, first, values)

    substitute(chain_vx[my_col], chain_vx[my_col + 1], gl_x, gr_x, work_b, work_a, store_x)

    for z in range(NZ):
        at = pl.ds(z, L, stride=NZ)
        side_x[at, :] = solved[at, :].T - half_y[at, :]
    def side_of_y(first, count):
        return nodes(side_x, first, count)

    d, push = eliminate_right_side(side_of_y, gl_y, gr_y, r_y, work_a, work_b)
    rhs_y[my_row, :NZ, :] = d
    rhs_y[my_row, NZ:, :] = push
    gather_ry.start()
    gather_cy.wait()
    factor_chain(n_row, coef_y, chain_gy, chain_ry)
    gather_ry.wait()
    solve_chain(n_row, rhs_y, chain_gy, chain_ry, chain_vy)

    def store_y(first, values):
        for i in range(values.shape[0]):
            wide[pl.ds(first + i, NZ, stride=PITCH), :] = values[i]

    substitute(chain_vy[my_row], chain_vy[my_row + 1], gl_y, gr_y, work_b, work_a, store_y)
    for z in range(NZ):
        out[pl.ds(z * L, L), :] = wide[pl.ds(z * PITCH, L), :]
    for transfer in (share_y, share_x, gather_cx, gather_rx, gather_cy, gather_ry):
        transfer.finish()


def solution(mesh):
    n_row, n_col = mesh.shape["row"], mesh.shape["col"]

    def local(field, region, source, mag, rate):
        def flat(values):
            return values.reshape(NZ * L, L)

        whole = pltpu.VMEM((NZ * L, L), jnp.float32)
        pitched = pltpu.VMEM((NZ * PITCH, L), jnp.float32)
        integer = pltpu.VMEM((NZ * PITCH, L), jnp.int32)

        parameter = pltpu.SMEM((3,), jnp.float32)

        def stack(count, height):
            return pltpu.VMEM((count, height * NZ, L), jnp.float32)

        def dma(count):
            return pltpu.SemaphoreType.DMA((count,))

        result = pl.pallas_call(
            functools.partial(kernel, n_row, n_col),
            out_shape=pltpu.VMEM((NZ * L, L), jnp.float32),
            in_specs=[pl.BlockSpec(memory_space=pltpu.HBM)] * 5,
            out_specs=pl.BlockSpec(memory_space=pltpu.VMEM),
            scratch_shapes=[parameter, parameter, pitched, integer]
            + [pitched] * 3
            + [whole] * 18
            + [stack(2, 2)] * 4
            + [stack(n_col, 3), stack(n_col, 2), stack(n_row, 3), stack(n_row, 2)]
            + [stack(n_col, 1), stack(n_col, 1), stack(n_col + 1, 1)]
            + [stack(n_row, 1), stack(n_row, 1), stack(n_row + 1, 1)]
            + [dma(2), pltpu.SemaphoreType.DMA((3, NZ))]
            + [dma(2)] * 4
            + [dma(n_col - 1)] * 4
            + [dma(n_row - 1)] * 4,
            compiler_params=pltpu.CompilerParams(
                collective_id=0, has_side_effects=True, vmem_limit_bytes=40 * 1024 * 1024
            ),
            cost_estimate=pl.CostEstimate(
                flops=20_000_000, bytes_accessed=2_200_000, transcendentals=400_000
            ),
        )(*[pltpu.with_memory_space_constraint(v, pltpu.HBM) for v in (mag, rate, flat(field), flat(region), flat(source))])
        return result.reshape(NZ, L, L)

    spec = P(None, "row", "col")
    return jax.shard_map(
        local, mesh=mesh, in_specs=(spec, spec, spec, P(), P()), out_specs=spec, check_vma=False
    )
```
